256 devices in a mesh: row: 16 (over y, x), col: 16 (over z, core).
Axes of the slice: x: 4, y: 4, z: 8, core: 2. Of those that a mesh axis runs over, the one named last changes fastest.
Arguments:
- slab: float32 [32768, 16384], P('row', 'col'), may hold values from -30 to 30, as said below
- test_matrix: float32 [16384, 128], P('col'), may hold values from -0.046875 to 0.046875
Outputs:
- basis: float32 [32768, 128], P(('row', 'col'))
- r_factor: float32 [128, 128], replicated
The draws below stay inside these ranges and needn't reach their ends.
Inputs may be any that keep to these rules, and one draw needn't show every extreme that they name: `slab`: the sketch's condition number (largest over smallest singular value) is at most 2000.
All inputs are finite; a program needn't handle non-finite values.
Results may differ from the reference program's by a relative error of at most 0.0003.
Values sent between devices are 32-bit elements; how exact they have to be, the bound alone decides.
No kernel may reach another device: no remote copies, remote signals or barrier semaphores. Data moves between devices by JAX's collectives and lax.ppermute only.
A program may use at most 64 MiB of HBM per device.

```python
import math
import jax
import jax.numpy as jnp
from jax import lax

N = 16384
K = 128
ROWS = 32768


def draw_slab(key, part):
    base = jax.random.fold_in(key, 17)
    keys = jax.random.split(base, 6)
    row_index = jnp.arange(ROWS, dtype=jnp.float32)[:, None]
    ramp = 1.0 + 2.0 * row_index / max(ROWS - 1, 1)
    row_scale = jnp.exp(jax.random.uniform(keys[1], (ROWS, 1), jnp.float32, -0.7, 0.7))
    ranked = jax.random.permutation(keys[2], N).astype(jnp.float32)[None, :]
    graded = jnp.exp(-0.75 * math.log(10.0) * ranked / K)
    spread = jnp.exp(jax.random.uniform(keys[5], (1, N), jnp.float32, math.log(0.015), math.log(0.06)))
    col_scale = jnp.where(ranked < 2 * K, graded, spread)
    left = jnp.clip(jax.random.normal(keys[3], (ROWS, 1), jnp.float32), -5.0, 5.0)
    right = jnp.clip(jax.random.normal(keys[4], (1, N), jnp.float32), -5.0, 5.0)
    noise = jax.random.normal(keys[0], (ROWS, N), jnp.float32)
    common = 1.0
    values = ramp * row_scale * col_scale * noise + common / math.sqrt(N) * left * right
    return jnp.clip(values, -30.0, 30.0).astype(jnp.float32)


def levels(own_key, shape, cuts, least, largest):
    factor_of, own = 1.0, jax.random.fold_in(own_key, 6)
    for dim, blocks in cuts:
        draws = jnp.exp(jax.random.uniform(jax.random.fold_in(own, dim), (blocks,), jnp.float32, least / len(cuts), largest / len(cuts)))
        factor_of = factor_of * jnp.repeat(draws, shape[dim] // blocks).reshape([-1 if axis == dim else 1 for axis in range(len(shape))])
    return factor_of


def bell_draw(stream_key, dims, deviation, most, pieces=(), kind=jnp.bfloat16):
    result = deviation * jax.random.normal(stream_key, dims, jnp.float32)
    if pieces:
        result = result * levels(stream_key, dims, pieces, -0.22, 0.18)
    return jnp.clip(result, -most, most).astype(kind)


def setup_inputs(seed: int = 0) -> dict:
    streams_of = jax.random.split(jax.random.key(seed), 3)
    return {
        "slab": draw_slab(jax.random.fold_in(streams_of[2], 71), 0),
        "test_matrix": bell_draw(streams_of[1], (N, K), N ** -0.5, 0.046875, ((0, 16),), jnp.float32),
    }


def reference(slab, test_matrix):
    highest = lax.Precision.HIGHEST
    sketch_one = jnp.dot(slab.astype(jnp.float32), test_matrix.astype(jnp.float32), precision=highest, preferred_element_type=jnp.float32)
    pulled = lax.dot_general(slab.astype(jnp.float32), sketch_one.astype(jnp.float32), (((0,), (0,)), ((), ())), precision=highest, preferred_element_type=jnp.float32) / ROWS
    sketch = jnp.dot(slab.astype(jnp.float32), pulled.astype(jnp.float32), precision=highest, preferred_element_type=jnp.float32)
    factor_q, factor_r = jnp.linalg.qr(sketch)
    sign_fix = jnp.where(jnp.diagonal(factor_r) < 0, -1.0, 1.0).astype(factor_r.dtype)
    root_rows = math.sqrt(ROWS)
    basis = factor_q * sign_fix[None, :] * root_rows
    r_factor = factor_r * sign_fix[:, None] / root_rows
    return (basis, r_factor)
```

```python
import math

import jax
import jax.numpy as jnp
from jax import lax
from jax.sharding import Mesh
from jax.sharding import PartitionSpec as P

HIGH = lax.Precision.HIGH
HIGHEST = lax.Precision.HIGHEST
CONTRACT = (((0,), (0,)), ((), ()))
ROW = ("y", "x")
SWAP = [(0, 1), (1, 0)]


def swap(value):
    return lax.ppermute(value, "core", SWAP)


def exchange(value, axes):
    return lax.all_to_all(value, axes, 0, 0, tiled=False)


def gathered(value, axes):
    count = lax.axis_size(axes)
    return exchange(jnp.broadcast_to(value, (count,) + value.shape), axes)


def halves(value):
    first, second = jnp.split(value, 2, axis=0)
    zero = lax.axis_index("core") == 0
    return jnp.where(zero, first, second), jnp.where(zero, second, first)


def whole(own, other):
    zero = lax.axis_index("core") == 0
    return jnp.concatenate([jnp.where(zero, own, other), jnp.where(zero, other, own)], axis=0)


def gram_of(matrix):
    return lax.dot_general(
        matrix, matrix, CONTRACT, precision=HIGHEST, preferred_element_type=jnp.float32
    )


def pack(gram):
    half = gram.shape[0] // 2
    last = gram[half:, half:]
    return jnp.concatenate(
        [gram[:half], jnp.concatenate([last[: half // 2], last[half // 2 :]], axis=1)], axis=0
    )


def unpack(packed):
    half = packed.shape[1] // 2
    top = packed[:half]
    tail = packed[half:]
    last = jnp.concatenate([tail[:, :half], tail[:, half:]], axis=0)
    return jnp.concatenate([top, jnp.concatenate([top[:, half:].T, last], axis=1)], axis=0)


def sum_gram(gram, stages):
    own, other = halves(pack(gram))
    value = own + swap(other)
    for axes in stages:
        value = jnp.sum(gathered(value, axes), axis=0)
    return unpack(whole(value, swap(value)))


def factor(gram):
    lower = jnp.linalg.cholesky(gram)
    eye = jnp.eye(gram.shape[0], dtype=gram.dtype)
    inverse = lax.linalg.triangular_solve(lower, eye, left_side=True, lower=True)
    return lower.T, inverse.T


def matmul(a, b, precision=HIGHEST):
    return jnp.dot(a, b, precision=precision, preferred_element_type=jnp.float32)


def local(slab, test_matrix):
    rows, columns = slab.shape
    wide = test_matrix.shape[1]
    zs = lax.axis_size("z")
    row_count = lax.axis_size(ROW)
    row_total = rows * row_count
    root_rows = math.sqrt(row_total)

    own, other = halves(matmul(slab, test_matrix, HIGH))
    part = (own + swap(other)).reshape(zs, -1, wide)
    piece = jnp.sum(exchange(part, "z"), axis=0)
    own = gathered(piece, "z").reshape(-1, wide)
    sketch_one = whole(own, swap(own))

    pulled_part = lax.dot_general(
        slab, sketch_one, CONTRACT, precision=HIGH, preferred_element_type=jnp.float32
    )
    piece = jnp.sum(exchange(pulled_part.reshape(row_count, -1, wide), ROW), axis=0) / row_total
    pulled = gathered(piece, ROW).reshape(-1, wide)

    before, before_inverse = factor(sum_gram(gram_of(pulled), ("z",)))

    product = matmul(slab, pulled).reshape(zs, 2, -1, wide)
    own, other = halves(jnp.swapaxes(product, 0, 1).reshape(rows, wide))
    part = (own + swap(other)).reshape(zs, -1, wide)
    sketch = jnp.sum(exchange(part, "z"), axis=0)

    inner = matmul(sketch, before_inverse)
    after, after_inverse = factor(sum_gram(gram_of(inner), (ROW, "z")))
    basis = matmul(inner, after_inverse) * root_rows
    return basis, matmul(after, before) / root_rows


def solution(mesh):
    sizes = dict(mesh.shape)
    chips = mesh.devices.reshape(4, sizes["row"] // 4, sizes["col"] // 2, 2)
    fine = Mesh(chips, ("y", "x", "z", "core"))
    col = ("z", "core")
    in_specs = (P(ROW, col), P(col, None))
    out_specs = (P(ROW + col, None), P())
    return jax.shard_map(local, mesh=fine, in_specs=in_specs, out_specs=out_specs, check_vma=False)
```

```python
import functools
import math

import jax
import jax.numpy as jnp
from jax import lax
from jax.experimental import pallas as pl
from jax.experimental.pallas import tpu as pltpu
from jax.sharding import Mesh
from jax.sharding import PartitionSpec as P

HIGHEST = lax.Precision.HIGHEST
CONTRACT = (((0,), (0,)), ((), ()))
TRANSPOSED = (((1,), (1,)), ((), ()))
ROW = ("y", "x")
SWAP = [(0, 1), (1, 0)]
TILE = 8
PANEL = 16
STEP = 2
VMEM = 48 * 1024 * 1024


def swap(value):
    return lax.ppermute(value, "core", SWAP)


def exchange(value, axes):
    return lax.all_to_all(value, axes, 0, 0, tiled=False)


def gathered(value, axes):
    count = lax.axis_size(axes)
    return exchange(jnp.broadcast_to(value, (count,) + value.shape), axes)


def dot(a, b, dims=(((1,), (0,)), ((), ())), precision=None):
    return lax.dot_general(a, b, dims, precision=precision, preferred_element_type=jnp.float32)


def split(value, count):
    parts = []
    for _ in range(count):
        parts.append(value.astype(jnp.bfloat16))
        value = value - parts[-1].astype(jnp.float32)
    return parts


def params():
    return pltpu.CompilerParams(vmem_limit_bytes=VMEM)


def project_kernel(count, half_ref, slab_ref, right_ref, out_ref, parts_ref):
    wide = right_ref.shape[1]

    @pl.when(pl.program_id(0) == 0)
    def _():
        for place, part in enumerate(split(right_ref[...], count)):
            parts_ref[:, place * wide : (place + 1) * wide] = part

    block = slab_ref[...].reshape(-1, slab_ref.shape[-1])
    parts = split(block, count)
    pair = parts_ref[:, : 2 * wide]
    first = dot(parts[0], pair)
    if count == 2:
        small = first[:, wide:] + dot(parts[1], parts_ref[:, :wide])
    else:
        second = dot(parts[1], pair)
        third = dot(parts[0], parts_ref[:, 2 * wide :]) + dot(parts[2], parts_ref[:, :wide])
        small = (first[:, wide:] + second[:, :wide]) + (second[:, wide:] + third)
    out_ref[...] = (first[:, :wide] + small).reshape(out_ref.shape)


def project(slab, right, half, count):
    zs, _, height, depth = slab.shape
    wide = right.shape[1]
    return pl.pallas_call(
        functools.partial(project_kernel, count),
        grid_spec=pltpu.PrefetchScalarGridSpec(
            num_scalar_prefetch=1,
            grid=(zs // STEP,),
            in_specs=[
                pl.BlockSpec((STEP, 1, height, depth), lambda i, half: (i, half[0], 0, 0)),
                pl.BlockSpec((depth, wide), lambda i, half: (0, 0)),
            ],
            out_specs=pl.BlockSpec((STEP, height, wide), lambda i, half: (i, 0, 0)),
            scratch_shapes=[pltpu.VMEM((depth, count * wide), jnp.bfloat16)],
        ),
        out_shape=jax.ShapeDtypeStruct((zs, height, wide), jnp.float32),
        compiler_params=params(),
        cost_estimate=pl.CostEstimate(
            flops=2 * zs * height * depth * wide * (4 if count == 2 else 8),
            bytes_accessed=4 * zs * height * depth,
            transcendentals=0,
        ),
        name="project%d" % count,
    )(half, slab, right)


def pull_kernel(more, half_ref, slab_ref, left_ref, *refs):
    out_ref, total_ref = refs[-2:]
    step = pl.program_id(0)
    wide = left_ref.shape[-1]
    block = slab_ref[...].reshape(-1, slab_ref.shape[-1])
    high, low = split(block, 2)
    left = jnp.concatenate(split(left_ref[...].reshape(-1, wide), 2), axis=1)
    left = jnp.transpose(left.astype(jnp.float32)).astype(jnp.bfloat16)
    both = dot(left, high)
    value = both[:wide] + (both[wide:] + dot(left[:wide], low))

    @pl.when(step == 0)
    def _():
        total_ref[...] = value

    @pl.when(step > 0)
    def _():
        total_ref[...] += value

    @pl.when(step == pl.num_programs(0) - 1)
    def _():
        result = jnp.transpose(total_ref[...])
        out_ref[...] = result + refs[0][...] if more else result


def pull(slab, left, half, before=None):
    zs, _, height, depth = slab.shape
    wide = left.shape[-1]
    flat = pl.BlockSpec((depth, wide), lambda i, half: (0, 0))
    more = before is not None
    return pl.pallas_call(
        functools.partial(pull_kernel, more),
        grid_spec=pltpu.PrefetchScalarGridSpec(
            num_scalar_prefetch=1,
            grid=(zs // STEP,),
            in_specs=[
                pl.BlockSpec((STEP, 1, height, depth), lambda i, half: (i, half[0], 0, 0)),
                pl.BlockSpec((STEP, height, wide), lambda i, half: (i, 0, 0)),
            ]
            + [flat] * more,
            out_specs=flat,
            scratch_shapes=[pltpu.VMEM((wide, depth), jnp.float32)],
        ),
        out_shape=jax.ShapeDtypeStruct((depth, wide), jnp.float32),
        compiler_params=params(),
        cost_estimate=pl.CostEstimate(
            flops=2 * zs * height * depth * wide * 4,
            bytes_accessed=4 * zs * height * depth,
            transcendentals=0,
        ),
        name="pull",
    )(half, slab, left, *([before] if more else []))


def spread(row):
    return jnp.broadcast_to(row, (TILE, row.shape[1]))


def eliminate(gram, floor):
    n = gram.shape[0]
    count, per = n // TILE, PANEL // TILE
    sub = lax.broadcasted_iota(jnp.int32, (TILE, n), 0)
    lane = lax.broadcasted_iota(jnp.int32, (TILE, n), 1)
    left = [gram[TILE * i : TILE * (i + 1)] for i in range(count)]
    right = [(lane == sub + TILE * i).astype(jnp.float32) for i in range(count)]
    scale = [None] * count
    for start in range(0, count, per):
        tiles = range(start, min(start + 2 * per, count))
        base = start * TILE
        column = {
            (t, q): jnp.broadcast_to(left[q][:, base + t : base + t + 1], (TILE, n))
            for t in range(PANEL)
            for q in tiles
            if start + t // TILE <= q
        }
        pivots = []
        for s in range(PANEL):
            here, at = start + s // TILE, s % TILE
            pivot = jnp.maximum(spread(column[s, here][at : at + 1]), floor)
            over = 1.0 / pivot
            pivots.append(pivot)
            entry = {
                t: spread(column[s, start + t // TILE][t % TILE : t % TILE + 1])
                if start + t // TILE > here
                else spread(column[t, here][at : at + 1])
                for t in range(s + 1, PANEL)
            }
            left_row, right_row = spread(left[here][at : at + 1]), spread(right[here][at : at + 1])
            for q in tiles:
                if q < here:
                    continue
                ratio = column[s, q] * over
                if q == here:
                    ratio = jnp.where(sub > at, ratio, 0.0)
                for t in range(s + 1, PANEL):
                    if (t, q) in column:
                        column[t, q] = column[t, q] - ratio * entry[t]
                left[q] = left[q] - ratio * left_row
                right[q] = right[q] - ratio * right_row
        for i in range(per):
            own = [pivots[i * TILE + s][s : s + 1] for s in range(TILE)]
            scale[start + i] = lax.rsqrt(jnp.concatenate(own, axis=0))
        rest = start + 2 * per
        if rest < count:
            panel = range(start, start + per)
            u = jnp.concatenate([left[i] * scale[i] for i in panel], axis=0)
            v = jnp.concatenate([right[i] * scale[i] for i in panel], axis=0)
            change = dot(u, jnp.concatenate([u, v], axis=1), CONTRACT, HIGHEST)
            for q in range(rest, count):
                rows = change[TILE * q : TILE * (q + 1)]
                left[q] = left[q] - rows[:, :n]
                right[q] = right[q] - rows[:, n:]
    upper = [jnp.where(lane >= sub + TILE * i, left[i] * scale[i], 0.0) for i in range(count)]
    lower = [right[i] * scale[i] for i in range(count)]
    return jnp.concatenate(upper, axis=0), jnp.concatenate(lower, axis=0)


def store_packed(core, gram, own_ref, other_ref):
    half = gram.shape[0] // 2
    last = gram[half:, half:]
    tail = jnp.concatenate([last[: half // 2], last[half // 2 :]], axis=1)
    packed = jnp.concatenate([gram[:half], tail], axis=0)
    middle = packed.shape[0] // 2
    first, second = packed[:middle], packed[middle:]
    own_ref[...] = jnp.where(core == 0, first, second)
    other_ref[...] = jnp.where(core == 0, second, first)


def load_packed(core, own, other):
    packed = jnp.concatenate(
        [jnp.where(core == 0, own, other), jnp.where(core == 0, other, own)], axis=0
    )
    half = packed.shape[1] // 2
    top, tail = packed[:half], packed[half:]
    last = jnp.concatenate([tail[:, :half], tail[:, half:]], axis=0)
    bottom = jnp.concatenate([jnp.transpose(top[:, half:]), last], axis=1)
    return jnp.concatenate([top, bottom], axis=0)


def floor_of(gram):
    return 1e-9 * jnp.max(gram)


def small_call(kernel, shapes, name, flops, core, *operands):
    memory = pl.BlockSpec(memory_space=pltpu.VMEM)
    return pl.pallas_call(
        kernel,
        in_specs=[pl.BlockSpec(memory_space=pltpu.SMEM)] + [memory] * len(operands),
        out_specs=[memory] * len(shapes),
        out_shape=[jax.ShapeDtypeStruct(shape, jnp.float32) for shape in shapes],
        compiler_params=params(),
        cost_estimate=pl.CostEstimate(
            flops=flops,
            bytes_accessed=4 * sum(operand.size for operand in operands),
            transcendentals=0,
        ),
        name=name,
    )(core, *operands)


def gram_kernel(core_ref, value_ref, own_ref, other_ref):
    value = value_ref[...]
    store_packed(core_ref[0], dot(value, value, CONTRACT, HIGHEST), own_ref, other_ref)


def factor_kernel(core_ref, own_ref, other_ref, upper_ref, lower_ref):
    gram = load_packed(core_ref[0], own_ref[...], other_ref[...])
    upper_ref[...], lower_ref[...] = eliminate(gram, floor_of(gram))


def middle_kernel(core_ref, parts_ref, lower_ref, inner_ref, own_ref, other_ref):
    sketch = parts_ref[0]
    for place in range(1, parts_ref.shape[0]):
        sketch += parts_ref[place]
    inner = dot(sketch, lower_ref[...], TRANSPOSED, HIGHEST)
    inner_ref[...] = inner
    store_packed(core_ref[0], dot(inner, inner, CONTRACT, HIGHEST), own_ref, other_ref)


def last_kernel(
    root_rows, core_ref, own_ref, other_ref, inner_ref, before_ref, basis_ref, factor_ref
):
    gram = load_packed(core_ref[0], own_ref[...], other_ref[...])
    upper, lower = eliminate(gram, floor_of(gram))
    basis_ref[...] = dot(inner_ref[...], lower, TRANSPOSED, HIGHEST) * root_rows
    factor_ref[...] = dot(upper, before_ref[...], precision=HIGHEST) / root_rows


def summed(own, other, stages):
    value = own + swap(other)
    for axes in stages:
        value = jnp.sum(gathered(value, axes), axis=0)
    return value, swap(value)


def local(slab, test_matrix):
    rows, columns = slab.shape
    wide = test_matrix.shape[1]
    zs = lax.axis_size("z")
    row_count = lax.axis_size(ROW)
    row_total = rows * row_count
    root_rows = math.sqrt(row_total)
    core = lax.axis_index("core").astype(jnp.int32).reshape(1)
    far = 1 - core
    slab = slab.reshape(zs, 2, -1, columns)
    square = (wide, wide)
    packed = [(3 * wide // 8, wide)] * 2

    sent = swap(project(slab, test_matrix, far, 2))
    part = project(slab, test_matrix, core, 2) + sent
    own = gathered(jnp.sum(exchange(part, "z"), axis=0), "z")

    other = swap(own)
    part = pull(slab, other, far, pull(slab, own, core))
    piece = jnp.sum(exchange(part.reshape(row_count, -1, wide), ROW), axis=0) / row_total
    pulled = gathered(piece, ROW).reshape(-1, wide)

    halves = small_call(gram_kernel, packed, "gram", 12 * columns * wide**2, core, pulled)
    halves = summed(*halves, ("z",))
    before, lower = small_call(factor_kernel, [square] * 2, "factor", 6 * 10**9, core, *halves)

    sent = swap(project(slab, pulled, far, 3))
    part = project(slab, pulled, core, 3) + sent
    parts = exchange(part, "z")

    inner, *halves = small_call(
        middle_kernel, [(rows // (2 * zs), wide)] + packed, "middle", 10**8, core, parts, lower
    )
    halves = summed(*halves, (ROW, "z"))
    basis, factor = small_call(
        functools.partial(last_kernel, root_rows),
        [inner.shape, square],
        "last",
        6 * 10**9,
        core,
        *halves,
        inner,
        before,
    )
    return basis, factor


def solution(mesh):
    sizes = dict(mesh.shape)
    chips = mesh.devices.reshape(4, sizes["row"] // 4, sizes["col"] // 2, 2)
    fine = Mesh(chips, ("y", "x", "z", "core"))
    col = ("z", "core")
    in_specs = (P(ROW, col), P(col, None))
    out_specs = (P(ROW + col, None), P())
    return jax.shard_map(local, mesh=fine, in_specs=in_specs, out_specs=out_specs, check_vma=False)
```

```python
import functools
import math

import jax
import jax.numpy as jnp
from jax import lax
from jax.experimental import pallas as pl
from jax.experimental.pallas import tpu as pltpu
from jax.sharding import Mesh
from jax.sharding import PartitionSpec as P

HIGHEST = lax.Precision.HIGHEST
CONTRACT = (((0,), (0,)), ((), ()))
TRANSPOSED = (((1,), (1,)), ((), ()))
ROW = ("y", "x")
SWAP = [(0, 1), (1, 0)]
TILE = 8
PANEL = 16
STEP = 2
PULL = 8
COUNT = 3
VMEM = 12 * 1024 * 1024
LOAD_VMEM = 46 * 1024 * 1024


def swap(value):
    return lax.ppermute(value, "core", SWAP)


def exchange(value, axes):
    return lax.all_to_all(value, axes, 0, 0, tiled=False)


def gathered(value, axes):
    count = lax.axis_size(axes)
    return exchange(jnp.broadcast_to(value, (count,) + value.shape), axes)


def dot(a, b, dims=(((1,), (0,)), ((), ())), precision=None):
    return lax.dot_general(a, b, dims, precision=precision, preferred_element_type=jnp.float32)


def split(value, count):
    parts = []
    for _ in range(count):
        parts.append(value.astype(jnp.bfloat16))
        value = value - parts[-1].astype(jnp.float32)
    return parts


def params(limit=VMEM):
    return pltpu.CompilerParams(vmem_limit_bytes=limit)


def rows_of(ref, place, height):
    return ref[place : place + height].reshape(-1, ref.shape[-1])


def load_kernel(half_ref, slab_ref, right_ref, out_ref, *refs):
    part_refs, (pair_ref, block_ref, right_buffer, sems) = refs[:COUNT], refs[COUNT:]
    half, zs, wide = half_ref[0], block_ref.shape[0], out_ref.shape[-1]
    right_copy = pltpu.make_async_copy(right_ref, right_buffer, sems.at[zs])
    right_copy.start()
    copies = [
        pltpu.make_async_copy(slab_ref.at[place, half], block_ref.at[place], sems.at[place])
        for place in range(zs)
    ]
    for copy in copies:
        copy.start()
    right_copy.wait()
    high, low = split(right_buffer[...], 2)
    pair_ref[:, :wide] = high
    pair_ref[:, wide:] = low
    for place in range(0, zs, STEP):
        for copy in copies[place : place + STEP]:
            copy.wait()
        parts = split(rows_of(block_ref, place, STEP), COUNT)
        for part, ref in zip(parts, part_refs):
            ref[place : place + STEP] = part.reshape(STEP, -1, ref.shape[-1])
        first = dot(parts[0], pair_ref[...])
        value = first[:, :wide] + (first[:, wide:] + dot(parts[1], pair_ref[:, :wide]))
        out_ref[place : place + STEP] = value.reshape(STEP, -1, wide)


def load(slab, right, half):
    zs, _, height, depth = slab.shape
    wide = right.shape[1]
    memory = pl.BlockSpec(memory_space=pltpu.VMEM)
    anywhere = pl.BlockSpec(memory_space=pl.ANY)
    part = jax.ShapeDtypeStruct((zs, height, depth), jnp.bfloat16)
    product, *parts = pl.pallas_call(
        load_kernel,
        in_specs=[pl.BlockSpec(memory_space=pltpu.SMEM), anywhere, anywhere],
        out_specs=[memory] * (1 + COUNT),
        scratch_shapes=[
            pltpu.VMEM((depth, 2 * wide), jnp.bfloat16),
            pltpu.VMEM((zs, height, depth), jnp.float32),
            pltpu.VMEM((depth, wide), jnp.float32),
            pltpu.SemaphoreType.DMA((zs + 1,)),
        ],
        out_shape=[jax.ShapeDtypeStruct((zs, height, wide), jnp.float32)] + [part] * COUNT,
        compiler_params=params(LOAD_VMEM),
        cost_estimate=cost(zs * height, depth, wide, 4),
        name="load",
    )(half, slab, right)
    return product, parts


def cost(height, depth, wide, times):
    return pl.CostEstimate(
        flops=2 * height * depth * wide * times,
        bytes_accessed=4 * height * depth,
        transcendentals=0,
    )


def project_kernel(right_ref, high_ref, middle_ref, low_ref, out_ref):
    wide = right_ref.shape[1]
    parts = split(right_ref[...], COUNT)
    pair = jnp.concatenate(parts[:2], axis=1)
    for place in range(0, out_ref.shape[0], STEP):
        high, middle = rows_of(high_ref, place, STEP), rows_of(middle_ref, place, STEP)
        first, second = dot(high, pair), dot(middle, pair)
        third = dot(high, parts[2]) + dot(rows_of(low_ref, place, STEP), parts[0])
        small = (first[:, wide:] + second[:, :wide]) + (second[:, wide:] + third)
        out_ref[place : place + STEP] = (first[:, :wide] + small).reshape(STEP, -1, wide)


def project(right, parts):
    zs, height, depth = parts[0].shape
    wide = right.shape[1]
    memory = pl.BlockSpec(memory_space=pltpu.VMEM)
    return pl.pallas_call(
        project_kernel,
        in_specs=[memory] * (1 + COUNT),
        out_specs=memory,
        out_shape=jax.ShapeDtypeStruct((zs, height, wide), jnp.float32),
        compiler_params=params(),
        cost_estimate=cost(zs * height, depth, wide, 8),
        name="project",
    )(right, *parts)


def pull_kernel(more, left_ref, high_ref, low_ref, *refs):
    out_ref = refs[-1]
    zs, wide = left_ref.shape[0], left_ref.shape[-1]
    total = None
    for place in range(0, zs, PULL):
        left = jnp.transpose(rows_of(left_ref, place, PULL))
        high, low = split(left, 2)
        block = rows_of(high_ref, place, PULL)
        both = dot(jnp.concatenate([high, low], axis=0), block)
        value = both[:wide] + (both[wide:] + dot(high, rows_of(low_ref, place, PULL)))
        total = value if total is None else total + value
    result = jnp.transpose(total)
    out_ref[...] = result + refs[0][...] if more else result


def pull(left, parts, before=None):
    zs, height, depth = parts[0].shape
    wide = left.shape[-1]
    memory = pl.BlockSpec(memory_space=pltpu.VMEM)
    more = before is not None
    return pl.pallas_call(
        functools.partial(pull_kernel, more),
        in_specs=[memory] * (3 + more),
        out_specs=memory,
        out_shape=jax.ShapeDtypeStruct((depth, wide), jnp.float32),
        compiler_params=params(),
        cost_estimate=cost(zs * height, depth, wide, 4),
        name="pull",
    )(left, *parts[:2], *([before] if more else []))


def spread(row):
    return jnp.broadcast_to(row, (TILE, row.shape[1]))


def eliminate(gram, floor):
    n = gram.shape[0]
    count, per = n // TILE, PANEL // TILE
    sub = lax.broadcasted_iota(jnp.int32, (TILE, n), 0)
    lane = lax.broadcasted_iota(jnp.int32, (TILE, n), 1)
    left = [gram[TILE * i : TILE * (i + 1)] for i in range(count)]
    right = [(lane == sub + TILE * i).astype(jnp.float32) for i in range(count)]
    scale = [None] * count
    for start in range(0, count, per):
        tiles = range(start, min(start + 2 * per, count))
        base = start * TILE
        column = {
            (t, q): jnp.broadcast_to(left[q][:, base + t : base + t + 1], (TILE, n))
            for t in range(PANEL)
            for q in tiles
            if start + t // TILE <= q
        }
        pivots = []
        for s in range(PANEL):
            here, at = start + s // TILE, s % TILE
            pivot = jnp.maximum(spread(column[s, here][at : at + 1]), floor)
            over = 1.0 / pivot
            pivots.append(pivot)
            entry = {
                t: spread(column[s, start + t // TILE][t % TILE : t % TILE + 1])
                if start + t // TILE > here
                else spread(column[t, here][at : at + 1])
                for t in range(s + 1, PANEL)
            }
            left_row, right_row = spread(left[here][at : at + 1]), spread(right[here][at : at + 1])
            for q in tiles:
                if q < here:
                    continue
                ratio = column[s, q] * over
                if q == here:
                    ratio = jnp.where(sub > at, ratio, 0.0)
                for t in range(s + 1, PANEL):
                    if (t, q) in column:
                        column[t, q] = column[t, q] - ratio * entry[t]
                left[q] = left[q] - ratio * left_row
                right[q] = right[q] - ratio * right_row
        for i in range(per):
            own = [pivots[i * TILE + s][s : s + 1] for s in range(TILE)]
            scale[start + i] = lax.rsqrt(jnp.concatenate(own, axis=0))
        rest = start + 2 * per
        if rest < count:
            panel = range(start, start + per)
            u = jnp.concatenate([left[i] * scale[i] for i in panel], axis=0)
            v = jnp.concatenate([right[i] * scale[i] for i in panel], axis=0)
            change = dot(u, jnp.concatenate([u, v], axis=1), CONTRACT, HIGHEST)
            for q in range(rest, count):
                rows = change[TILE * q : TILE * (q + 1)]
                left[q] = left[q] - rows[:, :n]
                right[q] = right[q] - rows[:, n:]
    upper = [jnp.where(lane >= sub + TILE * i, left[i] * scale[i], 0.0) for i in range(count)]
    lower = [right[i] * scale[i] for i in range(count)]
    return jnp.concatenate(upper, axis=0), jnp.concatenate(lower, axis=0)


def store_packed(core, gram, own_ref, other_ref):
    half = gram.shape[0] // 2
    last = gram[half:, half:]
    tail = jnp.concatenate([last[: half // 2], last[half // 2 :]], axis=1)
    packed = jnp.concatenate([gram[:half], tail], axis=0)
    middle = packed.shape[0] // 2
    first, second = packed[:middle], packed[middle:]
    own_ref[...] = jnp.where(core == 0, first, second)
    other_ref[...] = jnp.where(core == 0, second, first)


def load_packed(core, own, other):
    packed = jnp.concatenate(
        [jnp.where(core == 0, own, other), jnp.where(core == 0, other, own)], axis=0
    )
    half = packed.shape[1] // 2
    top, tail = packed[:half], packed[half:]
    last = jnp.concatenate([tail[:, :half], tail[:, half:]], axis=0)
    bottom = jnp.concatenate([jnp.transpose(top[:, half:]), last], axis=1)
    return jnp.concatenate([top, bottom], axis=0)


def floor_of(gram):
    return 1e-9 * jnp.max(gram)


def small_call(kernel, shapes, name, flops, core, *operands):
    memory = pl.BlockSpec(memory_space=pltpu.VMEM)
    return pl.pallas_call(
        kernel,
        in_specs=[pl.BlockSpec(memory_space=pltpu.SMEM)] + [memory] * len(operands),
        out_specs=[memory] * len(shapes),
        out_shape=[jax.ShapeDtypeStruct(shape, jnp.float32) for shape in shapes],
        compiler_params=params(),
        cost_estimate=pl.CostEstimate(
            flops=flops,
            bytes_accessed=4 * sum(operand.size for operand in operands),
            transcendentals=0,
        ),
        name=name,
    )(core, *operands)


def gram_kernel(core_ref, value_ref, own_ref, other_ref):
    value = value_ref[...]
    store_packed(core_ref[0], dot(value, value, CONTRACT, HIGHEST), own_ref, other_ref)


def factor_kernel(core_ref, own_ref, other_ref, upper_ref, lower_ref):
    gram = load_packed(core_ref[0], own_ref[...], other_ref[...])
    upper_ref[...], lower_ref[...] = eliminate(gram, floor_of(gram))


def middle_kernel(core_ref, parts_ref, lower_ref, inner_ref, own_ref, other_ref):
    sketch = parts_ref[0]
    for place in range(1, parts_ref.shape[0]):
        sketch += parts_ref[place]
    inner = dot(sketch, lower_ref[...], TRANSPOSED, HIGHEST)
    inner_ref[...] = inner
    store_packed(core_ref[0], dot(inner, inner, CONTRACT, HIGHEST), own_ref, other_ref)


def last_kernel(
    root_rows, core_ref, own_ref, other_ref, inner_ref, before_ref, basis_ref, factor_ref
):
    gram = load_packed(core_ref[0], own_ref[...], other_ref[...])
    upper, lower = eliminate(gram, floor_of(gram))
    basis_ref[...] = dot(inner_ref[...], lower, TRANSPOSED, HIGHEST) * root_rows
    factor_ref[...] = dot(upper, before_ref[...], precision=HIGHEST) / root_rows


def summed(own, other, stages):
    value = own + swap(other)
    for axes in stages:
        value = jnp.sum(gathered(value, axes), axis=0)
    return value, swap(value)


def local(slab, test_matrix):
    rows, columns = slab.shape
    wide = test_matrix.shape[1]
    zs = lax.axis_size("z")
    row_count = lax.axis_size(ROW)
    row_total = rows * row_count
    root_rows = math.sqrt(row_total)
    core = lax.axis_index("core").astype(jnp.int32).reshape(1)
    far = 1 - core
    slab = slab.reshape(zs, 2, -1, columns)
    square = (wide, wide)
    packed = [(3 * wide // 8, wide)] * 2

    product, far_parts = load(slab, test_matrix, far)
    sent = swap(product)
    product, parts = load(slab, test_matrix, core)
    part = product + sent
    own = gathered(jnp.sum(exchange(part, "z"), axis=0), "z")

    other = swap(own)
    part = pull(other, far_parts, pull(own, parts))
    piece = jnp.sum(exchange(part.reshape(row_count, -1, wide), ROW), axis=0) / row_total
    pulled = gathered(piece, ROW).reshape(-1, wide)

    halves = small_call(gram_kernel, packed, "gram", 12 * columns * wide**2, core, pulled)
    halves = summed(*halves, ("z",))
    before, lower = small_call(factor_kernel, [square] * 2, "factor", 6 * 10**9, core, *halves)

    sent = swap(project(pulled, far_parts))
    part = project(pulled, parts) + sent
    pieces = exchange(part, "z")

    inner, *halves = small_call(
        middle_kernel, [(rows // (2 * zs), wide)] + packed, "middle", 10**8, core, pieces, lower
    )
    halves = summed(*halves, (ROW, "z"))
    basis, factor = small_call(
        functools.partial(last_kernel, root_rows),
        [inner.shape, square],
        "last",
        6 * 10**9,
        core,
        *halves,
        inner,
        before,
    )
    return basis, factor


def solution(mesh):
    sizes = dict(mesh.shape)
    chips = mesh.devices.reshape(4, sizes["row"] // 4, sizes["col"] // 2, 2)
    fine = Mesh(chips, ("y", "x", "z", "core"))
    col = ("z", "core")
    in_specs = (P(ROW, col), P(col, None))
    out_specs = (P(ROW + col, None), P())
    return jax.shard_map(local, mesh=fine, in_specs=in_specs, out_specs=out_specs, check_vma=False)
```

```python
import functools
import math

import jax
import jax.numpy as jnp
from jax import lax
from jax.experimental import pallas as pl
from jax.experimental.pallas import tpu as pltpu
from jax.sharding import Mesh
from jax.sharding import PartitionSpec as P

HIGHEST = lax.Precision.HIGHEST
CONTRACT = (((0,), (0,)), ((), ()))
TRANSPOSED = (((1,), (1,)), ((), ()))
ROW = ("y", "x")
SWAP = [(0, 1), (1, 0)]
TILE = 8
PANEL = 16
STEP = 2
PULL = 8
COUNT = 3
VMEM = 12 * 1024 * 1024


def swap(value):
    return lax.ppermute(value, "core", SWAP)


def exchange(value, axes):
    return lax.all_to_all(value, axes, 0, 0, tiled=False)


def dot(a, b, dims=(((1,), (0,)), ((), ())), precision=None):
    return lax.dot_general(a, b, dims, precision=precision, preferred_element_type=jnp.float32)


def split(value, count):
    parts = []
    for _ in range(count):
        parts.append(value.astype(jnp.bfloat16))
        value = value - parts[-1].astype(jnp.float32)
    return parts


keep = pltpu.with_memory_space_constraint


def params():
    return pltpu.CompilerParams(vmem_limit_bytes=VMEM)


def rows_of(ref, place, height):
    return ref[place : place + height].reshape(-1, ref.shape[-1])


def load_kernel(half_ref, slab_ref, right_ref, out_ref, *refs):
    part_refs, (pair_ref, block_ref, right_buffer, sems) = refs[:COUNT], refs[COUNT:]
    half, zs, wide = half_ref[0], block_ref.shape[0], out_ref.shape[-1]
    right_copy = pltpu.make_async_copy(right_ref, right_buffer, sems.at[zs])
    right_copy.start()
    copies = [
        pltpu.make_async_copy(slab_ref.at[place, half], block_ref.at[place], sems.at[place])
        for place in range(zs)
    ]
    for copy in copies:
        copy.start()
    right_copy.wait()
    high, low = split(right_buffer[...], 2)
    pair_ref[:, :wide] = high
    pair_ref[:, wide:] = low
    for place in range(0, zs, STEP):
        for copy in copies[place : place + STEP]:
            copy.wait()
        parts = split(rows_of(block_ref, place, STEP), COUNT)
        for part, ref in zip(parts, part_refs):
            ref[place : place + STEP] = part.reshape(STEP, -1, ref.shape[-1])
        first = dot(parts[0], pair_ref[...])
        value = first[:, :wide] + (first[:, wide:] + dot(parts[1], pair_ref[:, :wide]))
        out_ref[place : place + STEP] = value.reshape(STEP, -1, wide)


def load(slab, right, half):
    zs, _, height, depth = slab.shape
    wide = right.shape[1]
    memory = pl.BlockSpec(memory_space=pltpu.VMEM)
    anywhere = pl.BlockSpec(memory_space=pltpu.HBM)
    part = pltpu.VMEM((zs, height, depth), jnp.bfloat16)
    product, *parts = pl.pallas_call(
        load_kernel,
        in_specs=[pl.BlockSpec(memory_space=pltpu.SMEM), anywhere, anywhere],
        out_specs=[memory] * (1 + COUNT),
        scratch_shapes=[
            pltpu.VMEM((depth, 2 * wide), jnp.bfloat16),
            pltpu.VMEM((zs, height, depth), jnp.float32),
            pltpu.VMEM((depth, wide), jnp.float32),
            pltpu.SemaphoreType.DMA((zs + 1,)),
        ],
        out_shape=[jax.ShapeDtypeStruct((zs, height, wide), jnp.float32)] + [part] * COUNT,
        compiler_params=params(),
        cost_estimate=cost(zs * height, depth, wide, 4),
        name="load",
    )(half, keep(slab, pltpu.HBM), keep(right, pltpu.HBM))
    return product, parts


def cost(height, depth, wide, times):
    return pl.CostEstimate(
        flops=2 * height * depth * wide * times,
        bytes_accessed=4 * height * depth,
        transcendentals=0,
    )


def project_kernel(right_ref, high_ref, middle_ref, low_ref, out_ref):
    wide = right_ref.shape[1]
    parts = split(right_ref[...], COUNT)
    pair = jnp.concatenate(parts[:2], axis=1)
    for place in range(0, out_ref.shape[0], STEP):
        high, middle = rows_of(high_ref, place, STEP), rows_of(middle_ref, place, STEP)
        first, second = dot(high, pair), dot(middle, pair)
        third = dot(high, parts[2]) + dot(rows_of(low_ref, place, STEP), parts[0])
        small = (first[:, wide:] + second[:, :wide]) + (second[:, wide:] + third)
        out_ref[place : place + STEP] = (first[:, :wide] + small).reshape(STEP, -1, wide)


def project(right, parts):
    zs, height, depth = parts[0].shape
    wide = right.shape[1]
    memory = pl.BlockSpec(memory_space=pltpu.VMEM)
    return pl.pallas_call(
        project_kernel,
        in_specs=[memory] * (1 + COUNT),
        out_specs=memory,
        out_shape=jax.ShapeDtypeStruct((zs, height, wide), jnp.float32),
        compiler_params=params(),
        cost_estimate=cost(zs * height, depth, wide, 8),
        name="project",
    )(right, *[keep(part, pltpu.VMEM) for part in parts])


def pull_kernel(more, left_ref, high_ref, low_ref, *refs):
    out_ref = refs[-1]
    zs, wide = left_ref.shape[0], left_ref.shape[-1]
    total = None
    for place in range(0, zs, PULL):
        left = jnp.transpose(rows_of(left_ref, place, PULL))
        high, low = split(left, 2)
        block = rows_of(high_ref, place, PULL)
        both = dot(jnp.concatenate([high, low], axis=0), block)
        value = both[:wide] + (both[wide:] + dot(high, rows_of(low_ref, place, PULL)))
        total = value if total is None else total + value
    result = jnp.transpose(total)
    out_ref[...] = result + refs[0][...] if more else result


def pull(left, parts, before=None):
    zs, height, depth = parts[0].shape
    wide = left.shape[-1]
    memory = pl.BlockSpec(memory_space=pltpu.VMEM)
    more = before is not None
    return pl.pallas_call(
        functools.partial(pull_kernel, more),
        in_specs=[memory] * (3 + more),
        out_specs=memory,
        out_shape=jax.ShapeDtypeStruct((depth, wide), jnp.float32),
        compiler_params=params(),
        cost_estimate=cost(zs * height, depth, wide, 4),
        name="pull",
    )(left, *[keep(part, pltpu.VMEM) for part in parts[:2]], *([before] if more else []))


def spread(row):
    return jnp.broadcast_to(row, (TILE, row.shape[1]))


def eliminate(gram, floor):
    n = gram.shape[0]
    count, per = n // TILE, PANEL // TILE
    sub = lax.broadcasted_iota(jnp.int32, (TILE, n), 0)
    lane = lax.broadcasted_iota(jnp.int32, (TILE, n), 1)
    left = [gram[TILE * i : TILE * (i + 1)] for i in range(count)]
    right = [(lane == sub + TILE * i).astype(jnp.float32) for i in range(count)]
    scale = [None] * count
    for start in range(0, count, per):
        tiles = range(start, min(start + 2 * per, count))
        base = start * TILE
        column = {
            (t, q): jnp.broadcast_to(left[q][:, base + t : base + t + 1], (TILE, n))
            for t in range(PANEL)
            for q in tiles
            if start + t // TILE <= q
        }
        pivots = []
        for s in range(PANEL):
            here, at = start + s // TILE, s % TILE
            pivot = jnp.maximum(spread(column[s, here][at : at + 1]), floor)
            over = 1.0 / pivot
            pivots.append(pivot)
            entry = {
                t: spread(column[s, start + t // TILE][t % TILE : t % TILE + 1])
                if start + t // TILE > here
                else spread(column[t, here][at : at + 1])
                for t in range(s + 1, PANEL)
            }
            left_row, right_row = spread(left[here][at : at + 1]), spread(right[here][at : at + 1])
            for q in tiles:
                if q < here:
                    continue
                ratio = column[s, q] * over
                if q == here:
                    ratio = jnp.where(sub > at, ratio, 0.0)
                for t in range(s + 1, PANEL):
                    if (t, q) in column:
                        column[t, q] = column[t, q] - ratio * entry[t]
                left[q] = left[q] - ratio * left_row
                right[q] = right[q] - ratio * right_row
        for i in range(per):
            own = [pivots[i * TILE + s][s : s + 1] for s in range(TILE)]
            scale[start + i] = lax.rsqrt(jnp.concatenate(own, axis=0))
        rest = start + 2 * per
        if rest < count:
            panel = range(start, start + per)
            u = jnp.concatenate([left[i] * scale[i] for i in panel], axis=0)
            v = jnp.concatenate([right[i] * scale[i] for i in panel], axis=0)
            change = dot(u, jnp.concatenate([u, v], axis=1), CONTRACT, HIGHEST)
            for q in range(rest, count):
                rows = change[TILE * q : TILE * (q + 1)]
                left[q] = left[q] - rows[:, :n]
                right[q] = right[q] - rows[:, n:]
    upper = [jnp.where(lane >= sub + TILE * i, left[i] * scale[i], 0.0) for i in range(count)]
    lower = [right[i] * scale[i] for i in range(count)]
    return jnp.concatenate(upper, axis=0), jnp.concatenate(lower, axis=0)


def store_packed(core, gram, own_ref, other_ref):
    half = gram.shape[0] // 2
    last = gram[half:, half:]
    tail = jnp.concatenate([last[: half // 2], last[half // 2 :]], axis=1)
    packed = jnp.concatenate([gram[:half], tail], axis=0)
    middle = packed.shape[0] // 2
    first, second = packed[:middle], packed[middle:]
    own_ref[...] = jnp.where(core == 0, first, second)
    other_ref[...] = jnp.where(core == 0, second, first)


def load_packed(core, own, other):
    packed = jnp.concatenate(
        [jnp.where(core == 0, own, other), jnp.where(core == 0, other, own)], axis=0
    )
    half = packed.shape[1] // 2
    top, tail = packed[:half], packed[half:]
    last = jnp.concatenate([tail[:, :half], tail[:, half:]], axis=0)
    bottom = jnp.concatenate([jnp.transpose(top[:, half:]), last], axis=1)
    return jnp.concatenate([top, bottom], axis=0)


def floor_of(gram):
    return 1e-9 * jnp.max(gram)


def small_call(kernel, shapes, name, flops, core, *operands):
    memory = pl.BlockSpec(memory_space=pltpu.VMEM)
    return pl.pallas_call(
        kernel,
        in_specs=[pl.BlockSpec(memory_space=pltpu.SMEM)] + [memory] * len(operands),
        out_specs=[memory] * len(shapes),
        out_shape=[jax.ShapeDtypeStruct(shape, jnp.float32) for shape in shapes],
        compiler_params=params(),
        cost_estimate=pl.CostEstimate(
            flops=flops,
            bytes_accessed=4 * sum(operand.size for operand in operands),
            transcendentals=0,
        ),
        name=name,
    )(core, *operands)


def gram_kernel(core_ref, value_ref, own_ref, other_ref):
    value = value_ref[...]
    store_packed(core_ref[0], dot(value, value, CONTRACT, HIGHEST), own_ref, other_ref)


def add_kernel(first_ref, second_ref, out_ref):
    out_ref[...] = first_ref[...] + second_ref[...]


def total_kernel(scale, pieces_ref, out_ref):
    value = pieces_ref[0]
    for place in range(1, pieces_ref.shape[0]):
        value += pieces_ref[place]
    out_ref[...] = jnp.broadcast_to((value * scale)[None], out_ref.shape)


def plain_call(kernel, shape, name, *operands):
    memory = pl.BlockSpec(memory_space=pltpu.VMEM)
    return pl.pallas_call(
        kernel,
        in_specs=[memory] * len(operands),
        out_specs=memory,
        out_shape=jax.ShapeDtypeStruct(shape, jnp.float32),
        compiler_params=params(),
        name=name,
    )(*operands)


def tail_kernel(start, pieces_ref, out_ref):
    value = pieces_ref[0, start:]
    for place in range(1, pieces_ref.shape[0]):
        value += pieces_ref[place, start:]
    out_ref[...] = value


def pair_kernel(own_ref, other_ref, out_ref):
    out_ref[...] = jnp.broadcast_to((own_ref[...] + other_ref[...])[None], out_ref.shape)


def total(pieces, count, scale=1.0):
    shape = (count,) + pieces.shape[1:]
    return plain_call(functools.partial(total_kernel, scale), shape, "total", pieces)


def join_kernel(product_ref, sent_ref, own_ref, other_ref, out_ref):
    height = product_ref.shape[1]
    out_ref[:, :height] = product_ref[...] + sent_ref[...]
    gram = own_ref[...] + other_ref[...]
    out_ref[:, height:] = jnp.broadcast_to(gram[None], (out_ref.shape[0],) + gram.shape)


def middle_kernel(
    core_ref, pieces_ref, pulled_own_ref, pulled_other_ref, inner_ref, before_ref, own_ref, other_ref
):
    gram = load_packed(core_ref[0], pulled_own_ref[...], pulled_other_ref[...])
    before_ref[...], lower = eliminate(gram, floor_of(gram))
    height = inner_ref.shape[0]
    sketch = pieces_ref[0, :height]
    for place in range(1, pieces_ref.shape[0]):
        sketch += pieces_ref[place, :height]
    inner = dot(sketch, lower, TRANSPOSED, HIGHEST)
    inner_ref[...] = inner
    store_packed(core_ref[0], dot(inner, inner, CONTRACT, HIGHEST), own_ref, other_ref)


def last_kernel(
    root_rows, core_ref, own_ref, other_ref, inner_ref, before_ref, basis_ref, factor_ref
):
    gram = load_packed(core_ref[0], own_ref[...], other_ref[...])
    upper, lower = eliminate(gram, floor_of(gram))
    basis_ref[...] = dot(inner_ref[...], lower, TRANSPOSED, HIGHEST) * root_rows
    factor_ref[...] = dot(upper, before_ref[...], precision=HIGHEST) / root_rows


def local(slab, test_matrix):
    rows, columns = slab.shape
    wide = test_matrix.shape[1]
    zs = lax.axis_size("z")
    row_count = lax.axis_size(ROW)
    row_total = rows * row_count
    root_rows = math.sqrt(row_total)
    core = lax.axis_index("core").astype(jnp.int32).reshape(1)
    far = 1 - core
    slab = slab.reshape(zs, 2, -1, columns)
    square = (wide, wide)
    packed = [(3 * wide // 8, wide)] * 2

    product, far_parts = load(slab, test_matrix, far)
    sent = swap(product)
    product, parts = load(slab, test_matrix, core)
    part = plain_call(add_kernel, product.shape, "add", product, sent)
    own = exchange(total(exchange(part, "z"), zs), "z")

    other = swap(own)
    part = pull(other, far_parts, pull(own, parts))
    pieces = total(exchange(part.reshape(row_count, -1, wide), ROW), row_count, 1.0 / row_total)
    pulled = exchange(pieces, ROW).reshape(-1, wide)

    own, other = small_call(gram_kernel, packed, "gram", 12 * columns * wide**2, core, pulled)
    other = swap(other)
    sent = swap(project(pulled, far_parts))
    product = project(pulled, parts)
    height = product.shape[1]
    shape = (zs, height + own.shape[0], wide)
    joined = plain_call(join_kernel, shape, "join", product, sent, own, other)
    pieces = exchange(joined, "z")
    own = plain_call(functools.partial(tail_kernel, height), own.shape, "tail", pieces)

    inner, before, *halves = small_call(
        middle_kernel,
        [(height, wide), square] + packed,
        "middle",
        6 * 10**9,
        core,
        pieces,
        own,
        swap(own),
    )
    own, other = halves
    copies = plain_call(pair_kernel, (row_count,) + own.shape, "pair", own, swap(other))
    copies = total(exchange(copies, ROW), zs)
    own = total(exchange(copies, "z"), 1)[0]
    basis, factor = small_call(
        functools.partial(last_kernel, root_rows),
        [inner.shape, square],
        "last",
        6 * 10**9,
        core,
        own,
        swap(own),
        inner,
        before,
    )
    return basis, factor


def solution(mesh):
    sizes = dict(mesh.shape)
    chips = mesh.devices.reshape(4, sizes["row"] // 4, sizes["col"] // 2, 2)
    fine = Mesh(chips, ("y", "x", "z", "core"))
    col = ("z", "core")
    in_specs = (P(ROW, col), P(col, None))
    out_specs = (P(ROW + col, None), P())
    return jax.shard_map(local, mesh=fine, in_specs=in_specs, out_specs=out_specs, check_vma=False)
```

```python
import functools
import math

import jax
import jax.numpy as jnp
from jax import lax
from jax.experimental import pallas as pl
from jax.experimental.pallas import tpu as pltpu
from jax.sharding import Mesh
from jax.sharding import PartitionSpec as P

HIGHEST = lax.Precision.HIGHEST
CONTRACT = (((0,), (0,)), ((), ()))
TRANSPOSED = (((1,), (1,)), ((), ()))
ROW = ("y", "x")
SWAP = [(0, 1), (1, 0)]
TILE = 8
PANEL = 16
STEP = 2
PULL = 8
COUNT = 3
VMEM = 12 * 1024 * 1024


def swap(value):
    return lax.ppermute(value, "core", SWAP)


def exchange(value, axes):
    return lax.all_to_all(value, axes, 0, 0, tiled=False)


def dot(a, b, dims=(((1,), (0,)), ((), ())), precision=None):
    return lax.dot_general(a, b, dims, precision=precision, preferred_element_type=jnp.float32)


def split(value, count):
    parts = []
    for _ in range(count):
        parts.append(value.astype(jnp.bfloat16))
        value = value - parts[-1].astype(jnp.float32)
    return parts


keep = pltpu.with_memory_space_constraint


def params():
    return pltpu.CompilerParams(vmem_limit_bytes=VMEM)


def rows_of(ref, place, height):
    return ref[place : place + height].reshape(-1, ref.shape[-1])


def load_kernel(half_ref, slab_ref, right_ref, out_ref, *refs):
    part_refs, (pair_ref, block_ref, right_buffer, sems) = refs[:COUNT], refs[COUNT:]
    half, zs, wide = half_ref[0], block_ref.shape[0], out_ref.shape[-1]
    right_copy = pltpu.make_async_copy(right_ref, right_buffer, sems.at[zs])
    right_copy.start()
    copies = [
        pltpu.make_async_copy(slab_ref.at[place, half], block_ref.at[place], sems.at[place])
        for place in range(zs)
    ]
    for copy in copies:
        copy.start()
    right_copy.wait()
    high, low = split(right_buffer[...], 2)
    pair_ref[:, :wide] = high
    pair_ref[:, wide:] = low
    for place in range(0, zs, STEP):
        for copy in copies[place : place + STEP]:
            copy.wait()
        parts = split(rows_of(block_ref, place, STEP), COUNT)
        for part, ref in zip(parts, part_refs):
            ref[place : place + STEP] = part.reshape(STEP, -1, ref.shape[-1])
        first = dot(parts[0], pair_ref[...])
        value = first[:, :wide] + (first[:, wide:] + dot(parts[1], pair_ref[:, :wide]))
        out_ref[place : place + STEP] = value.reshape(STEP, -1, wide)


def load(slab, right, half):
    zs, _, height, depth = slab.shape
    wide = right.shape[1]
    memory = pl.BlockSpec(memory_space=pltpu.VMEM)
    anywhere = pl.BlockSpec(memory_space=pltpu.HBM)
    part = pltpu.VMEM((zs, height, depth), jnp.bfloat16)
    product, *parts = pl.pallas_call(
        load_kernel,
        in_specs=[pl.BlockSpec(memory_space=pltpu.SMEM), anywhere, anywhere],
        out_specs=[memory] * (1 + COUNT),
        scratch_shapes=[
            pltpu.VMEM((depth, 2 * wide), jnp.bfloat16),
            pltpu.VMEM((zs, height, depth), jnp.float32),
            pltpu.VMEM((depth, wide), jnp.float32),
            pltpu.SemaphoreType.DMA((zs + 1,)),
        ],
        out_shape=[jax.ShapeDtypeStruct((zs, height, wide), jnp.float32)] + [part] * COUNT,
        compiler_params=params(),
        cost_estimate=cost(zs * height, depth, wide, 4),
        name="load",
    )(half, keep(slab, pltpu.HBM), keep(right, pltpu.HBM))
    return product, parts


def cost(height, depth, wide, times):
    return pl.CostEstimate(
        flops=2 * height * depth * wide * times,
        bytes_accessed=4 * height * depth,
        transcendentals=0,
    )


def project_kernel(right_ref, high_ref, middle_ref, low_ref, out_ref):
    wide = right_ref.shape[1]
    parts = split(right_ref[...], COUNT)
    pair = jnp.concatenate(parts[:2], axis=1)
    for place in range(0, out_ref.shape[0], STEP):
        high, middle = rows_of(high_ref, place, STEP), rows_of(middle_ref, place, STEP)
        first, second = dot(high, pair), dot(middle, pair)
        third = dot(high, parts[2]) + dot(rows_of(low_ref, place, STEP), parts[0])
        small = (first[:, wide:] + second[:, :wide]) + (second[:, wide:] + third)
        out_ref[place : place + STEP] = (first[:, :wide] + small).reshape(STEP, -1, wide)


def project(right, parts, after=()):
    zs, height, depth = parts[0].shape
    wide = right.shape[1]
    memory = pl.BlockSpec(memory_space=pltpu.VMEM)
    return pl.pallas_call(
        without(project_kernel, 1 + COUNT, len(after)),
        in_specs=[memory] * (1 + COUNT) + [pl.BlockSpec(memory_space=pl.ANY)] * len(after),
        out_specs=memory,
        out_shape=jax.ShapeDtypeStruct((zs, height, wide), jnp.float32),
        compiler_params=params(),
        cost_estimate=cost(zs * height, depth, wide, 8),
        name="project",
    )(right, *[keep(part, pltpu.VMEM) for part in parts], *after)


def pull_kernel(more, left_ref, high_ref, low_ref, *refs):
    out_ref = refs[-1]
    zs, wide = left_ref.shape[0], left_ref.shape[-1]
    total = None
    for place in range(0, zs, PULL):
        left = jnp.transpose(rows_of(left_ref, place, PULL))
        high, low = split(left, 2)
        block = rows_of(high_ref, place, PULL)
        both = dot(jnp.concatenate([high, low], axis=0), block)
        value = both[:wide] + (both[wide:] + dot(high, rows_of(low_ref, place, PULL)))
        total = value if total is None else total + value
    result = jnp.transpose(total)
    out_ref[...] = result + refs[0][...] if more else result


def pull(left, parts, before=None):
    zs, height, depth = parts[0].shape
    wide = left.shape[-1]
    memory = pl.BlockSpec(memory_space=pltpu.VMEM)
    more = before is not None
    return pl.pallas_call(
        functools.partial(pull_kernel, more),
        in_specs=[memory] * (3 + more),
        out_specs=memory,
        out_shape=jax.ShapeDtypeStruct((depth, wide), jnp.float32),
        compiler_params=params(),
        cost_estimate=cost(zs * height, depth, wide, 4),
        name="pull",
    )(left, *[keep(part, pltpu.VMEM) for part in parts[:2]], *([before] if more else []))


def spread(row):
    return jnp.broadcast_to(row, (TILE, row.shape[1]))


def eliminate(gram, floor):
    n = gram.shape[0]
    count, per = n // TILE, PANEL // TILE
    sub = lax.broadcasted_iota(jnp.int32, (TILE, n), 0)
    lane = lax.broadcasted_iota(jnp.int32, (TILE, n), 1)
    left = [gram[TILE * i : TILE * (i + 1)] for i in range(count)]
    right = [(lane == sub + TILE * i).astype(jnp.float32) for i in range(count)]
    scale = [None] * count
    for start in range(0, count, per):
        tiles = range(start, min(start + 2 * per, count))
        base = start * TILE
        column = {
            (t, q): jnp.broadcast_to(left[q][:, base + t : base + t + 1], (TILE, n))
            for t in range(PANEL)
            for q in tiles
            if start + t // TILE <= q
        }
        pivots = []
        for s in range(PANEL):
            here, at = start + s // TILE, s % TILE
            pivot = jnp.maximum(spread(column[s, here][at : at + 1]), floor)
            over = 1.0 / pivot
            pivots.append(pivot)
            entry = {
                t: spread(column[s, start + t // TILE][t % TILE : t % TILE + 1])
                if start + t // TILE > here
                else spread(column[t, here][at : at + 1])
                for t in range(s + 1, PANEL)
            }
            left_row, right_row = spread(left[here][at : at + 1]), spread(right[here][at : at + 1])
            for q in tiles:
                if q < here:
                    continue
                ratio = column[s, q] * over
                if q == here:
                    ratio = jnp.where(sub > at, ratio, 0.0)
                for t in range(s + 1, PANEL):
                    if (t, q) in column:
                        column[t, q] = column[t, q] - ratio * entry[t]
                left[q] = left[q] - ratio * left_row
                right[q] = right[q] - ratio * right_row
        for i in range(per):
            own = [pivots[i * TILE + s][s : s + 1] for s in range(TILE)]
            scale[start + i] = lax.rsqrt(jnp.concatenate(own, axis=0))
        rest = start + 2 * per
        if rest < count:
            panel = range(start, start + per)
            u = jnp.concatenate([left[i] * scale[i] for i in panel], axis=0)
            v = jnp.concatenate([right[i] * scale[i] for i in panel], axis=0)
            change = dot(u, jnp.concatenate([u, v], axis=1), CONTRACT, HIGHEST)
            for q in range(rest, count):
                rows = change[TILE * q : TILE * (q + 1)]
                left[q] = left[q] - rows[:, :n]
                right[q] = right[q] - rows[:, n:]
    upper = [jnp.where(lane >= sub + TILE * i, left[i] * scale[i], 0.0) for i in range(count)]
    lower = [right[i] * scale[i] for i in range(count)]
    return jnp.concatenate(upper, axis=0), jnp.concatenate(lower, axis=0)


def pack(gram):
    n = gram.shape[0]
    q = n // 4
    middle = jnp.concatenate([gram[q : 2 * q, q:], gram[3 * q :, 3 * q :]], axis=1)
    low = gram[2 * q : 3 * q, 2 * q :]
    tail = jnp.concatenate([low[: q // 2], low[q // 2 :]], axis=1)
    return jnp.concatenate([gram[:q], middle, tail], axis=0)


def unpack(packed):
    n = packed.shape[1]
    q = n // 4
    middle, tail = packed[q : 2 * q], packed[2 * q :]
    low = jnp.concatenate([tail[:, : 2 * q], tail[:, 2 * q :]], axis=0)
    second = jnp.concatenate([jnp.zeros((q, q), jnp.float32), middle[:, : 3 * q]], axis=1)
    third = jnp.concatenate([jnp.zeros((q, 2 * q), jnp.float32), low], axis=1)
    fourth = jnp.concatenate([jnp.zeros((q, 3 * q), jnp.float32), middle[:, 3 * q :]], axis=1)
    upper = jnp.concatenate([packed[:q], second, third, fourth], axis=0)
    row = lax.broadcasted_iota(jnp.int32, (n, n), 0)
    column = lax.broadcasted_iota(jnp.int32, (n, n), 1)
    return jnp.where(row <= column, upper, jnp.transpose(upper))


def store_halves(core, gram, own_ref, other_ref):
    packed = pack(gram)
    middle = packed.shape[0] // 2
    first, second = packed[:middle], packed[middle:]
    own_ref[...] = jnp.where(core == 0, first, second)
    other_ref[...] = jnp.where(core == 0, second, first)


def load_halves(core, own, other):
    first = jnp.where(core == 0, own, other)
    second = jnp.where(core == 0, other, own)
    return unpack(jnp.concatenate([first, second], axis=0))


def floor_of(gram):
    return 1e-9 * jnp.max(gram)


def without(kernel, place, count):
    def call(*refs):
        kernel(*refs[:place], *refs[place + count :])

    return call


def small_call(kernel, shapes, name, cycles, operands, scalars=(), after=()):
    memory = pl.BlockSpec(memory_space=pltpu.VMEM)
    return pl.pallas_call(
        without(kernel, len(scalars) + len(operands), len(after)),
        in_specs=[pl.BlockSpec(memory_space=pltpu.SMEM)] * len(scalars)
        + [memory] * len(operands)
        + [pl.BlockSpec(memory_space=pl.ANY)] * len(after),
        out_specs=[memory] * len(shapes),
        out_shape=[jax.ShapeDtypeStruct(shape, jnp.float32) for shape in shapes],
        compiler_params=params(),
        cost_estimate=pl.CostEstimate(
            flops=cycles * 10**6, bytes_accessed=4 * shapes[0][-1], transcendentals=0
        ),
        name=name,
    )(*scalars, *operands, *after)


def plain_call(kernel, shape, name, *operands, after=()):
    return small_call(kernel, [shape], name, 100, operands, after=after)[0]


def gram_kernel(value_ref, out_ref):
    value = value_ref[...]
    out_ref[...] = pack(dot(value, value, CONTRACT, HIGHEST))


def factor_kernel(first_ref, second_ref, upper_ref, lower_ref):
    gram = unpack(first_ref[...] + second_ref[...])
    upper_ref[...], lower_ref[...] = eliminate(gram, floor_of(gram))


def add_kernel(first_ref, second_ref, out_ref):
    out_ref[...] = first_ref[...] + second_ref[...]


def total_kernel(scale, pieces_ref, out_ref):
    value = pieces_ref[0]
    for place in range(1, pieces_ref.shape[0]):
        value += pieces_ref[place]
    out_ref[...] = jnp.broadcast_to((value * scale)[None], out_ref.shape)


def add(first, second, after=()):
    return plain_call(add_kernel, first.shape, "add", first, second, after=after)


def pair_kernel(own_ref, other_ref, out_ref):
    out_ref[...] = jnp.broadcast_to((own_ref[...] + other_ref[...])[None], out_ref.shape)


def total(pieces, count, scale=1.0):
    shape = (count,) + pieces.shape[1:]
    return plain_call(functools.partial(total_kernel, scale), shape, "total", pieces)


def middle_kernel(core_ref, pieces_ref, lower_ref, inner_ref, own_ref, other_ref):
    sketch = pieces_ref[0]
    for place in range(1, pieces_ref.shape[0]):
        sketch += pieces_ref[place]
    inner = dot(sketch, lower_ref[...], TRANSPOSED, HIGHEST)
    inner_ref[...] = inner
    store_halves(core_ref[0], dot(inner, inner, CONTRACT, HIGHEST), own_ref, other_ref)


def last_kernel(
    root_rows, core_ref, own_ref, other_ref, inner_ref, before_ref, basis_ref, factor_ref
):
    gram = load_halves(core_ref[0], own_ref[...], other_ref[...])
    upper, lower = eliminate(gram, floor_of(gram))
    basis_ref[...] = dot(inner_ref[...], lower, TRANSPOSED, HIGHEST) * root_rows
    factor_ref[...] = dot(upper, before_ref[...], precision=HIGHEST) / root_rows


def local(slab, test_matrix):
    rows, columns = slab.shape
    wide = test_matrix.shape[1]
    zs = lax.axis_size("z")
    row_count = lax.axis_size(ROW)
    row_total = rows * row_count
    root_rows = math.sqrt(row_total)
    core = lax.axis_index("core").astype(jnp.int32).reshape(1)
    far = 1 - core
    slab = slab.reshape(zs, 2, -1, columns)
    square = (wide, wide)
    packed = (5 * wide // 8, wide)
    halves = [(5 * wide // 16, wide)] * 2

    product, far_parts = load(slab, test_matrix, far)
    sent = swap(product)
    product, parts = load(slab, test_matrix, core)
    part = add(product, sent)
    own = exchange(total(exchange(part, "z"), zs), "z")

    other = swap(own)
    part = pull(other, far_parts, pull(own, parts))
    pieces = total(exchange(part.reshape(row_count, -1, wide), ROW), row_count, 1.0 / row_total)
    pulled = exchange(pieces, ROW).reshape(-1, wide)

    gram = small_call(gram_kernel, [packed], "gram", 700, [pulled])[0]
    grams, distance = [gram], 1
    while distance < zs:
        partners = [(place, place ^ distance) for place in range(zs)]
        grams.append(add(grams[-1], lax.ppermute(grams[-1], "z", partners)))
        distance *= 2
    pair = [grams[-1], swap(grams[-1])]
    before, lower = small_call(factor_kernel, [square] * 2, "factor", 3600, pair)

    sent = swap(project(pulled, far_parts, grams[:1]))
    part = add(project(pulled, parts, grams[:1]), sent, grams[1:2])
    pieces = exchange(part, "z")

    inner, own, other = small_call(
        middle_kernel, [part.shape[1:]] + halves, "middle", 650, [pieces, lower], [core]
    )
    copies = plain_call(pair_kernel, (row_count,) + own.shape, "pair", own, swap(other))
    copies = total(exchange(copies, ROW), zs)
    own = total(exchange(copies, "z"), 1)[0]
    basis, factor = small_call(
        functools.partial(last_kernel, root_rows),
        [inner.shape, square],
        "last",
        4600,
        [own, swap(own), inner, before],
        [core],
    )
    return basis, factor


def solution(mesh):
    sizes = dict(mesh.shape)
    chips = mesh.devices.reshape(4, sizes["row"] // 4, sizes["col"] // 2, 2)
    fine = Mesh(chips, ("y", "x", "z", "core"))
    col = ("z", "core")
    in_specs = (P(ROW, col), P(col, None))
    out_specs = (P(ROW + col, None), P())
    return jax.shard_map(local, mesh=fine, in_specs=in_specs, out_specs=out_specs, check_vma=False)
```

```python
import functools
import math

import jax
import jax.numpy as jnp
from jax import lax
from jax.experimental import pallas as pl
from jax.experimental.pallas import tpu as pltpu
from jax.sharding import Mesh
from jax.sharding import PartitionSpec as P

HIGHEST = lax.Precision.HIGHEST
CONTRACT = (((0,), (0,)), ((), ()))
TRANSPOSED = (((1,), (1,)), ((), ()))
ROW = ("y", "x")
SWAP = [(0, 1), (1, 0)]
TILE = 8
PANEL = 16
STEP = 2
PULL = 8
COUNT = 3
VMEM = 12 * 1024 * 1024


def swap(value):
    return lax.ppermute(value, "core", SWAP)


def exchange(value, axes):
    return lax.all_to_all(value, axes, 0, 0, tiled=False)


def dot(a, b, dims=(((1,), (0,)), ((), ())), precision=None):
    return lax.dot_general(a, b, dims, precision=precision, preferred_element_type=jnp.float32)


def split(value, count):
    parts = []
    for _ in range(count):
        parts.append(value.astype(jnp.bfloat16))
        value = value - parts[-1].astype(jnp.float32)
    return parts


keep = pltpu.with_memory_space_constraint


def params():
    return pltpu.CompilerParams(vmem_limit_bytes=VMEM)


def rows_of(ref, place, height):
    return ref[place : place + height].reshape(-1, ref.shape[-1])


def multiply_kernel(half_ref, slab_ref, right_ref, out_ref, pair_ref, block_ref, right_buffer, sems):
    half, zs, wide = half_ref[0], block_ref.shape[0], out_ref.shape[-1]
    right_copy = pltpu.make_async_copy(right_ref, right_buffer, sems.at[zs])
    right_copy.start()
    copies = [
        pltpu.make_async_copy(slab_ref.at[place, half], block_ref.at[place], sems.at[place])
        for place in range(zs)
    ]
    for copy in copies:
        copy.start()
    right_copy.wait()
    high, low = split(right_buffer[...], 2)
    pair_ref[:, :wide] = high
    pair_ref[:, wide:] = low
    for place in range(0, zs, STEP):
        for copy in copies[place : place + STEP]:
            copy.wait()
        high, low = split(rows_of(block_ref, place, STEP), 2)
        first = dot(high, pair_ref[...])
        value = first[:, :wide] + (first[:, wide:] + dot(low, pair_ref[:, :wide]))
        out_ref[place : place + STEP] = value.reshape(STEP, -1, wide)


def multiply(slab, right, half):
    zs, _, height, depth = slab.shape
    wide = right.shape[1]
    high_memory = pl.BlockSpec(memory_space=pltpu.HBM)
    return pl.pallas_call(
        multiply_kernel,
        in_specs=[pl.BlockSpec(memory_space=pltpu.SMEM), high_memory, high_memory],
        out_specs=pl.BlockSpec(memory_space=pltpu.VMEM),
        scratch_shapes=[
            pltpu.VMEM((depth, 2 * wide), jnp.bfloat16),
            pltpu.VMEM((zs, height, depth), jnp.float32),
            pltpu.VMEM((depth, wide), jnp.float32),
            pltpu.SemaphoreType.DMA((zs + 1,)),
        ],
        out_shape=jax.ShapeDtypeStruct((zs, height, wide), jnp.float32),
        compiler_params=params(),
        cost_estimate=cost(zs * height, depth, wide, 4),
        name="multiply",
    )(half, keep(slab, pltpu.HBM), keep(right, pltpu.HBM))


def parts_kernel(turn, core_ref, slab_ref, *refs):
    block_ref, sems = refs[-2:]
    part_refs = refs[-2 - 2 * COUNT : -2]
    zs, core = block_ref.shape[0], core_ref[0]

    @pl.when(core == turn)
    def _():
        copies = [
            [
                pltpu.make_async_copy(
                    slab_ref.at[place, half], block_ref.at[place, half], sems.at[place, half]
                )
                for half in range(2)
            ]
            for place in range(zs)
        ]
        for pair in copies:
            for copy in pair:
                copy.start()
        for place in range(zs):
            for half, refs in ((turn, part_refs[:COUNT]), (1 - turn, part_refs[COUNT:])):
                copies[place][half].wait()
                for part, ref in zip(split(block_ref[place, half], COUNT), refs):
                    ref[place] = part


def parts_of(slab, core, turn, before=(), passed=None):
    zs, _, height, depth = slab.shape
    high_memory = pl.BlockSpec(memory_space=pltpu.HBM)
    memory = pl.BlockSpec(memory_space=pltpu.VMEM)
    count = 2 * COUNT
    through = [] if passed is None else [passed]
    shapes = [pltpu.VMEM((zs, height, depth), jnp.bfloat16)] * count
    shapes += [jax.ShapeDtypeStruct(value.shape, value.dtype) for value in through]
    place = 2 + len(through)
    aliases = {2: count} if through else {}
    aliases |= {place + i: i for i in range(len(before))}

    def kernel(*refs):
        outs = refs[place + len(before) :]
        parts_kernel(turn, *refs[:2], *outs[:count], *outs[-2:])

    return pl.pallas_call(
        kernel,
        in_specs=[pl.BlockSpec(memory_space=pltpu.SMEM), high_memory]
        + [memory] * (len(through) + len(before)),
        out_specs=[memory] * (count + len(through)),
        scratch_shapes=[
            pltpu.VMEM((zs, 2, height, depth), jnp.float32),
            pltpu.SemaphoreType.DMA((zs, 2)),
        ],
        out_shape=shapes,
        input_output_aliases=aliases,
        compiler_params=params(),
        cost_estimate=cost(2 * zs * height, depth, 128, 4),
        name="parts",
    )(core, keep(slab, pltpu.HBM), *through, *[keep(part, pltpu.VMEM) for part in before])


def cost(height, depth, wide, times):
    return pl.CostEstimate(
        flops=2 * height * depth * wide * times,
        bytes_accessed=4 * height * depth,
        transcendentals=0,
    )


def project_kernel(right_ref, high_ref, middle_ref, low_ref, out_ref):
    wide = right_ref.shape[1]
    parts = split(right_ref[...], COUNT)
    pair = jnp.concatenate(parts[:2], axis=1)
    for place in range(0, out_ref.shape[0], STEP):
        high, middle = rows_of(high_ref, place, STEP), rows_of(middle_ref, place, STEP)
        first, second = dot(high, pair), dot(middle, pair)
        third = dot(high, parts[2]) + dot(rows_of(low_ref, place, STEP), parts[0])
        small = (first[:, wide:] + second[:, :wide]) + (second[:, wide:] + third)
        out_ref[place : place + STEP] = (first[:, :wide] + small).reshape(STEP, -1, wide)


def project(right, parts, after=()):
    zs, height, depth = parts[0].shape
    wide = right.shape[1]
    memory = pl.BlockSpec(memory_space=pltpu.VMEM)
    return pl.pallas_call(
        without(project_kernel, 1 + COUNT, len(after)),
        in_specs=[memory] * (1 + COUNT) + [pl.BlockSpec(memory_space=pl.ANY)] * len(after),
        out_specs=memory,
        out_shape=jax.ShapeDtypeStruct((zs, height, wide), jnp.float32),
        compiler_params=params(),
        cost_estimate=cost(zs * height, depth, wide, 8),
        name="project",
    )(right, *[keep(part, pltpu.VMEM) for part in parts], *after)


def pull_kernel(more, left_ref, high_ref, low_ref, *refs):
    out_ref = refs[-1]
    zs, wide = left_ref.shape[0], left_ref.shape[-1]
    total = None
    for place in range(0, zs, PULL):
        left = jnp.transpose(rows_of(left_ref, place, PULL))
        high, low = split(left, 2)
        block = rows_of(high_ref, place, PULL)
        both = dot(jnp.concatenate([high, low], axis=0), block)
        value = both[:wide] + (both[wide:] + dot(high, rows_of(low_ref, place, PULL)))
        total = value if total is None else total + value
    result = jnp.transpose(total)
    out_ref[...] = result + refs[0][...] if more else result


def pull(left, parts, before=None):
    zs, height, depth = parts[0].shape
    wide = left.shape[-1]
    memory = pl.BlockSpec(memory_space=pltpu.VMEM)
    more = before is not None
    return pl.pallas_call(
        functools.partial(pull_kernel, more),
        in_specs=[memory] * (3 + more),
        out_specs=memory,
        out_shape=jax.ShapeDtypeStruct((depth, wide), jnp.float32),
        compiler_params=params(),
        cost_estimate=cost(zs * height, depth, wide, 4),
        name="pull",
    )(left, *[keep(part, pltpu.VMEM) for part in parts[:2]], *([before] if more else []))


def spread(row):
    return jnp.broadcast_to(row, (TILE, row.shape[1]))


def eliminate(gram, floor):
    n = gram.shape[0]
    count, per = n // TILE, PANEL // TILE
    sub = lax.broadcasted_iota(jnp.int32, (TILE, n), 0)
    lane = lax.broadcasted_iota(jnp.int32, (TILE, n), 1)
    left = [gram[TILE * i : TILE * (i + 1)] for i in range(count)]
    right = [(lane == sub + TILE * i).astype(jnp.float32) for i in range(count)]
    scale = [None] * count
    for start in range(0, count, per):
        tiles = range(start, min(start + 2 * per, count))
        base = start * TILE
        column = {
            (t, q): jnp.broadcast_to(left[q][:, base + t : base + t + 1], (TILE, n))
            for t in range(PANEL)
            for q in tiles
            if start + t // TILE <= q
        }
        pivots = []
        for s in range(PANEL):
            here, at = start + s // TILE, s % TILE
            pivot = jnp.maximum(spread(column[s, here][at : at + 1]), floor)
            over = 1.0 / pivot
            pivots.append(pivot)
            entry = {
                t: spread(column[s, start + t // TILE][t % TILE : t % TILE + 1])
                if start + t // TILE > here
                else spread(column[t, here][at : at + 1])
                for t in range(s + 1, PANEL)
            }
            left_row, right_row = spread(left[here][at : at + 1]), spread(right[here][at : at + 1])
            for q in tiles:
                if q < here:
                    continue
                ratio = column[s, q] * over
                if q == here:
                    ratio = jnp.where(sub > at, ratio, 0.0)
                for t in range(s + 1, PANEL):
                    if (t, q) in column:
                        column[t, q] = column[t, q] - ratio * entry[t]
                left[q] = left[q] - ratio * left_row
                right[q] = right[q] - ratio * right_row
        for i in range(per):
            own = [pivots[i * TILE + s][s : s + 1] for s in range(TILE)]
            scale[start + i] = lax.rsqrt(jnp.concatenate(own, axis=0))
        rest = start + 2 * per
        if rest < count:
            panel = range(start, start + per)
            u = jnp.concatenate([left[i] * scale[i] for i in panel], axis=0)
            v = jnp.concatenate([right[i] * scale[i] for i in panel], axis=0)
            change = dot(u, jnp.concatenate([u, v], axis=1), CONTRACT, HIGHEST)
            for q in range(rest, count):
                rows = change[TILE * q : TILE * (q + 1)]
                left[q] = left[q] - rows[:, :n]
                right[q] = right[q] - rows[:, n:]
    upper = [jnp.where(lane >= sub + TILE * i, left[i] * scale[i], 0.0) for i in range(count)]
    lower = [right[i] * scale[i] for i in range(count)]
    return jnp.concatenate(upper, axis=0), jnp.concatenate(lower, axis=0)


def pack(gram):
    n = gram.shape[0]
    q = n // 4
    middle = jnp.concatenate([gram[q : 2 * q, q:], gram[3 * q :, 3 * q :]], axis=1)
    low = gram[2 * q : 3 * q, 2 * q :]
    tail = jnp.concatenate([low[: q // 2], low[q // 2 :]], axis=1)
    return jnp.concatenate([gram[:q], middle, tail], axis=0)


def unpack(packed):
    n = packed.shape[1]
    q = n // 4
    middle, tail = packed[q : 2 * q], packed[2 * q :]
    low = jnp.concatenate([tail[:, : 2 * q], tail[:, 2 * q :]], axis=0)
    second = jnp.concatenate([jnp.zeros((q, q), jnp.float32), middle[:, : 3 * q]], axis=1)
    third = jnp.concatenate([jnp.zeros((q, 2 * q), jnp.float32), low], axis=1)
    fourth = jnp.concatenate([jnp.zeros((q, 3 * q), jnp.float32), middle[:, 3 * q :]], axis=1)
    upper = jnp.concatenate([packed[:q], second, third, fourth], axis=0)
    row = lax.broadcasted_iota(jnp.int32, (n, n), 0)
    column = lax.broadcasted_iota(jnp.int32, (n, n), 1)
    return jnp.where(row <= column, upper, jnp.transpose(upper))


def store_halves(core, gram, own_ref, other_ref):
    packed = pack(gram)
    middle = packed.shape[0] // 2
    first, second = packed[:middle], packed[middle:]
    own_ref[...] = jnp.where(core == 0, first, second)
    other_ref[...] = jnp.where(core == 0, second, first)


def load_halves(core, own, other):
    first = jnp.where(core == 0, own, other)
    second = jnp.where(core == 0, other, own)
    return unpack(jnp.concatenate([first, second], axis=0))


def floor_of(gram):
    return 1e-9 * jnp.max(gram)


def without(kernel, place, count):
    def call(*refs):
        kernel(*refs[:place], *refs[place + count :])

    return call


def small_call(kernel, shapes, name, cycles, operands, scalars=(), after=()):
    memory = pl.BlockSpec(memory_space=pltpu.VMEM)
    return pl.pallas_call(
        without(kernel, len(scalars) + len(operands), len(after)),
        in_specs=[pl.BlockSpec(memory_space=pltpu.SMEM)] * len(scalars)
        + [memory] * len(operands)
        + [pl.BlockSpec(memory_space=pl.ANY)] * len(after),
        out_specs=[memory] * len(shapes),
        out_shape=[jax.ShapeDtypeStruct(shape, jnp.float32) for shape in shapes],
        compiler_params=params(),
        cost_estimate=pl.CostEstimate(
            flops=cycles * 10**6, bytes_accessed=4 * shapes[0][-1], transcendentals=0
        ),
        name=name,
    )(*scalars, *operands, *after)


def plain_call(kernel, shape, name, *operands, after=()):
    return small_call(kernel, [shape], name, 100, operands, after=after)[0]


def gram_kernel(core_ref, value_ref, own_ref, other_ref):
    value = value_ref[...]
    store_halves(core_ref[0], dot(value, value, CONTRACT, HIGHEST), own_ref, other_ref)


def add_kernel(first_ref, second_ref, out_ref):
    out_ref[...] = first_ref[...] + second_ref[...]


def total_kernel(scale, pieces_ref, out_ref):
    value = pieces_ref[0]
    for place in range(1, pieces_ref.shape[0]):
        value += pieces_ref[place]
    out_ref[...] = jnp.broadcast_to((value * scale)[None], out_ref.shape)


def add(first, second, after=()):
    return plain_call(add_kernel, first.shape, "add", first, second, after=after)


def pair_kernel(own_ref, other_ref, out_ref):
    out_ref[...] = jnp.broadcast_to((own_ref[...] + other_ref[...])[None], out_ref.shape)


def total(pieces, count, scale=1.0):
    shape = (count,) + pieces.shape[1:]
    return plain_call(functools.partial(total_kernel, scale), shape, "total", pieces)


def join_kernel(product_ref, sent_ref, own_ref, other_ref, out_ref):
    height = product_ref.shape[1]
    out_ref[:, :height] = product_ref[...] + sent_ref[...]
    gram = own_ref[...] + other_ref[...]
    out_ref[:, height:] = jnp.broadcast_to(gram[None], (out_ref.shape[0],) + gram.shape)


def tail_kernel(start, pieces_ref, out_ref):
    value = pieces_ref[0, start:]
    for place in range(1, pieces_ref.shape[0]):
        value += pieces_ref[place, start:]
    out_ref[...] = value


def middle_kernel(
    core_ref, pieces_ref, pulled_own_ref, pulled_other_ref, inner_ref, before_ref, own_ref, other_ref
):
    gram = load_halves(core_ref[0], pulled_own_ref[...], pulled_other_ref[...])
    before_ref[...], lower = eliminate(gram, floor_of(gram))
    height = inner_ref.shape[0]
    sketch = pieces_ref[0, :height]
    for place in range(1, pieces_ref.shape[0]):
        sketch += pieces_ref[place, :height]
    inner = dot(sketch, lower, TRANSPOSED, HIGHEST)
    inner_ref[...] = inner
    store_halves(core_ref[0], dot(inner, inner, CONTRACT, HIGHEST), own_ref, other_ref)


def last_kernel(
    root_rows, core_ref, own_ref, other_ref, inner_ref, before_ref, basis_ref, factor_ref
):
    gram = load_halves(core_ref[0], own_ref[...], other_ref[...])
    upper, lower = eliminate(gram, floor_of(gram))
    basis_ref[...] = dot(inner_ref[...], lower, TRANSPOSED, HIGHEST) * root_rows
    factor_ref[...] = dot(upper, before_ref[...], precision=HIGHEST) / root_rows


def local(slab, test_matrix):
    rows, columns = slab.shape
    wide = test_matrix.shape[1]
    zs = lax.axis_size("z")
    row_count = lax.axis_size(ROW)
    row_total = rows * row_count
    root_rows = math.sqrt(row_total)
    core = lax.axis_index("core").astype(jnp.int32).reshape(1)
    far = 1 - core
    slab = slab.reshape(zs, 2, -1, columns)
    square = (wide, wide)
    halves = [(5 * wide // 16, wide)] * 2

    sent = swap(multiply(slab, test_matrix, far))
    product = multiply(slab, test_matrix, core)
    made = parts_of(slab, core, 1)
    part = add(product, sent, made[:1])
    own = exchange(total(exchange(part, "z"), zs), "z")

    *made, own = parts_of(slab, core, 0, made, own)
    parts, far_parts = made[:COUNT], made[COUNT:]
    other = swap(own)
    part = pull(other, far_parts, pull(own, parts))
    pieces = total(exchange(part.reshape(row_count, -1, wide), ROW), row_count, 1.0 / row_total)
    pulled = exchange(pieces, ROW).reshape(-1, wide)

    own, other = small_call(gram_kernel, halves, "gram", 700, [pulled], [core])
    other = swap(other)
    sent = swap(project(pulled, far_parts))
    product = project(pulled, parts)
    height = product.shape[1]
    shape = (zs, height + own.shape[0], wide)
    joined = plain_call(join_kernel, shape, "join", product, sent, own, other)
    pieces = exchange(joined, "z")
    own = plain_call(functools.partial(tail_kernel, height), own.shape, "tail", pieces)

    inner, before, own, other = small_call(
        middle_kernel,
        [(height, wide), square] + halves,
        "middle",
        4300,
        [pieces, own, swap(own)],
        [core],
    )
    copies = plain_call(pair_kernel, (row_count,) + own.shape, "pair", own, swap(other))
    copies = total(exchange(copies, ROW), zs)
    own = total(exchange(copies, "z"), 1)[0]
    basis, factor = small_call(
        functools.partial(last_kernel, root_rows),
        [inner.shape, square],
        "last",
        4600,
        [own, swap(own), inner, before],
        [core],
    )
    return basis, factor


def solution(mesh):
    sizes = dict(mesh.shape)
    chips = mesh.devices.reshape(4, sizes["row"] // 4, sizes["col"] // 2, 2)
    fine = Mesh(chips, ("y", "x", "z", "core"))
    col = ("z", "core")
    in_specs = (P(ROW, col), P(col, None))
    out_specs = (P(ROW + col, None), P())
    return jax.shard_map(local, mesh=fine, in_specs=in_specs, out_specs=out_specs, check_vma=False)
```

```python
import functools
import math

import jax
import jax.numpy as jnp
from jax import lax
from jax.experimental import pallas as pl
from jax.experimental.pallas import tpu as pltpu
from jax.sharding import Mesh
from jax.sharding import PartitionSpec as P

HIGHEST = lax.Precision.HIGHEST
CONTRACT = (((0,), (0,)), ((), ()))
TRANSPOSED = (((1,), (1,)), ((), ()))
ROW = ("y", "x")
SWAP = [(0, 1), (1, 0)]
TILE = 8
PANEL = 16
STEP = 2
PULL = 8
COUNT = 3
VMEM = 12 * 1024 * 1024


def swap(value):
    return lax.ppermute(value, "core", SWAP)


def exchange(value, axes):
    return lax.all_to_all(value, axes, 0, 0, tiled=False)


def dot(a, b, dims=(((1,), (0,)), ((), ())), precision=None):
    return lax.dot_general(a, b, dims, precision=precision, preferred_element_type=jnp.float32)


def split(value, count):
    parts = []
    for _ in range(count):
        parts.append(value.astype(jnp.bfloat16))
        value = value - parts[-1].astype(jnp.float32)
    return parts


keep = pltpu.with_memory_space_constraint


def params():
    return pltpu.CompilerParams(vmem_limit_bytes=VMEM)


def rows_of(ref, place, height):
    return ref[place : place + height].reshape(-1, ref.shape[-1])


def multiply_kernel(half_ref, slab_ref, right_ref, out_ref, pair_ref, block_ref, right_buffer, sems):
    half, zs, wide = half_ref[0], block_ref.shape[0], out_ref.shape[-1]
    right_copy = pltpu.make_async_copy(right_ref, right_buffer, sems.at[zs])
    right_copy.start()
    copies = [
        pltpu.make_async_copy(slab_ref.at[place, half], block_ref.at[place], sems.at[place])
        for place in range(zs)
    ]
    for copy in copies:
        copy.start()
    right_copy.wait()
    high, low = split(right_buffer[...], 2)
    pair_ref[:, :wide] = high
    pair_ref[:, wide:] = low
    for place in range(0, zs, STEP):
        for copy in copies[place : place + STEP]:
            copy.wait()
        high, low = split(rows_of(block_ref, place, STEP), 2)
        first = dot(high, pair_ref[...])
        value = first[:, :wide] + (first[:, wide:] + dot(low, pair_ref[:, :wide]))
        out_ref[place : place + STEP] = value.reshape(STEP, -1, wide)


def multiply(slab, right, half):
    zs, _, height, depth = slab.shape
    wide = right.shape[1]
    high_memory = pl.BlockSpec(memory_space=pltpu.HBM)
    return pl.pallas_call(
        multiply_kernel,
        in_specs=[pl.BlockSpec(memory_space=pltpu.SMEM), high_memory, high_memory],
        out_specs=pl.BlockSpec(memory_space=pltpu.VMEM),
        scratch_shapes=[
            pltpu.VMEM((depth, 2 * wide), jnp.bfloat16),
            pltpu.VMEM((zs, height, depth), jnp.float32),
            pltpu.VMEM((depth, wide), jnp.float32),
            pltpu.SemaphoreType.DMA((zs + 1,)),
        ],
        out_shape=jax.ShapeDtypeStruct((zs, height, wide), jnp.float32),
        compiler_params=params(),
        cost_estimate=cost(zs * height, depth, wide, 4),
        name="multiply",
    )(half, keep(slab, pltpu.HBM), keep(right, pltpu.HBM))


def parts_kernel(turn, core_ref, slab_ref, *refs):
    block_ref, sems = refs[-2:]
    part_refs = refs[-2 - 2 * COUNT : -2]
    zs, core = block_ref.shape[0], core_ref[0]

    @pl.when(core == turn)
    def _():
        copies = [
            [
                pltpu.make_async_copy(
                    slab_ref.at[place, half], block_ref.at[place, half], sems.at[place, half]
                )
                for half in range(2)
            ]
            for place in range(zs)
        ]
        for pair in copies:
            for copy in pair:
                copy.start()
        for place in range(zs):
            for half, refs in ((turn, part_refs[:COUNT]), (1 - turn, part_refs[COUNT:])):
                copies[place][half].wait()
                for part, ref in zip(split(block_ref[place, half], COUNT), refs):
                    ref[place] = part


def parts_of(slab, core, turn, before=(), passed=None):
    zs, _, height, depth = slab.shape
    high_memory = pl.BlockSpec(memory_space=pltpu.HBM)
    memory = pl.BlockSpec(memory_space=pltpu.VMEM)
    count = 2 * COUNT
    through = [] if passed is None else [passed]
    shapes = [pltpu.VMEM((zs, height, depth), jnp.bfloat16)] * count
    shapes += [jax.ShapeDtypeStruct(value.shape, value.dtype) for value in through]
    place = 2 + len(through)
    aliases = {2: count} if through else {}
    aliases |= {place + i: i for i in range(len(before))}

    def kernel(*refs):
        outs = refs[place + len(before) :]
        parts_kernel(turn, *refs[:2], *outs[:count], *outs[-2:])

    return pl.pallas_call(
        kernel,
        in_specs=[pl.BlockSpec(memory_space=pltpu.SMEM), high_memory]
        + [memory] * (len(through) + len(before)),
        out_specs=[memory] * (count + len(through)),
        scratch_shapes=[
            pltpu.VMEM((zs, 2, height, depth), jnp.float32),
            pltpu.SemaphoreType.DMA((zs, 2)),
        ],
        out_shape=shapes,
        input_output_aliases=aliases,
        compiler_params=params(),
        cost_estimate=cost(2 * zs * height, depth, 128, 4),
        name="parts",
    )(core, keep(slab, pltpu.HBM), *through, *[keep(part, pltpu.VMEM) for part in before])


def cost(height, depth, wide, times):
    return pl.CostEstimate(
        flops=2 * height * depth * wide * times,
        bytes_accessed=4 * height * depth,
        transcendentals=0,
    )


def project_kernel(right_ref, high_ref, middle_ref, low_ref, out_ref):
    wide = right_ref.shape[1]
    parts = split(right_ref[...], COUNT)
    pair = jnp.concatenate(parts[:2], axis=1)
    for place in range(0, out_ref.shape[0], STEP):
        high, middle = rows_of(high_ref, place, STEP), rows_of(middle_ref, place, STEP)
        first, second = dot(high, pair), dot(middle, pair)
        third = dot(high, parts[2]) + dot(rows_of(low_ref, place, STEP), parts[0])
        small = (first[:, wide:] + second[:, :wide]) + (second[:, wide:] + third)
        out_ref[place : place + STEP] = (first[:, :wide] + small).reshape(STEP, -1, wide)


def project(right, parts, after=()):
    zs, height, depth = parts[0].shape
    wide = right.shape[1]
    memory = pl.BlockSpec(memory_space=pltpu.VMEM)
    return pl.pallas_call(
        without(project_kernel, 1 + COUNT, len(after)),
        in_specs=[memory] * (1 + COUNT) + [pl.BlockSpec(memory_space=pl.ANY)] * len(after),
        out_specs=memory,
        out_shape=jax.ShapeDtypeStruct((zs, height, wide), jnp.float32),
        compiler_params=params(),
        cost_estimate=cost(zs * height, depth, wide, 8),
        name="project",
    )(right, *[keep(part, pltpu.VMEM) for part in parts], *after)


def pull_kernel(more, left_ref, high_ref, low_ref, *refs):
    out_ref = refs[-1]
    zs, wide = left_ref.shape[0], left_ref.shape[-1]
    total = None
    for place in range(0, zs, PULL):
        left = jnp.transpose(rows_of(left_ref, place, PULL))
        high, low = split(left, 2)
        block = rows_of(high_ref, place, PULL)
        both = dot(jnp.concatenate([high, low], axis=0), block)
        value = both[:wide] + (both[wide:] + dot(high, rows_of(low_ref, place, PULL)))
        total = value if total is None else total + value
    result = jnp.transpose(total)
    out_ref[...] = result + refs[0][...] if more else result


def pull(left, parts, before=None):
    zs, height, depth = parts[0].shape
    wide = left.shape[-1]
    memory = pl.BlockSpec(memory_space=pltpu.VMEM)
    more = before is not None
    return pl.pallas_call(
        functools.partial(pull_kernel, more),
        in_specs=[memory] * (3 + more),
        out_specs=memory,
        out_shape=jax.ShapeDtypeStruct((depth, wide), jnp.float32),
        compiler_params=params(),
        cost_estimate=cost(zs * height, depth, wide, 4),
        name="pull",
    )(left, *[keep(part, pltpu.VMEM) for part in parts[:2]], *([before] if more else []))


def spread(row):
    return jnp.broadcast_to(row, (TILE, row.shape[1]))


def eliminate(gram, floor):
    n = gram.shape[0]
    count, per = n // TILE, PANEL // TILE
    sub = lax.broadcasted_iota(jnp.int32, (TILE, n), 0)
    lane = lax.broadcasted_iota(jnp.int32, (TILE, n), 1)
    left = [gram[TILE * i : TILE * (i + 1)] for i in range(count)]
    right = [(lane == sub + TILE * i).astype(jnp.float32) for i in range(count)]
    scale = [None] * count
    for start in range(0, count, per):
        tiles = range(start, min(start + 2 * per, count))
        base = start * TILE
        column = {
            (t, q): jnp.broadcast_to(left[q][:, base + t : base + t + 1], (TILE, n))
            for t in range(PANEL)
            for q in tiles
            if start + t // TILE <= q
        }
        pivots = []
        for s in range(PANEL):
            here, at = start + s // TILE, s % TILE
            pivot = jnp.maximum(spread(column[s, here][at : at + 1]), floor)
            over = 1.0 / pivot
            pivots.append(pivot)
            entry = {
                t: spread(column[s, start + t // TILE][t % TILE : t % TILE + 1])
                if start + t // TILE > here
                else spread(column[t, here][at : at + 1])
                for t in range(s + 1, PANEL)
            }
            left_row, right_row = spread(left[here][at : at + 1]), spread(right[here][at : at + 1])
            for q in tiles:
                if q < here:
                    continue
                ratio = column[s, q] * over
                if q == here:
                    ratio = jnp.where(sub > at, ratio, 0.0)
                for t in range(s + 1, PANEL):
                    if (t, q) in column:
                        column[t, q] = column[t, q] - ratio * entry[t]
                left[q] = left[q] - ratio * left_row
                right[q] = right[q] - ratio * right_row
        for i in range(per):
            own = [pivots[i * TILE + s][s : s + 1] for s in range(TILE)]
            scale[start + i] = lax.rsqrt(jnp.concatenate(own, axis=0))
        rest = start + 2 * per
        if rest < count:
            panel = range(start, start + per)
            u = jnp.concatenate([left[i] * scale[i] for i in panel], axis=0)
            v = jnp.concatenate([right[i] * scale[i] for i in panel], axis=0)
            change = dot(u, jnp.concatenate([u, v], axis=1), CONTRACT, HIGHEST)
            for q in range(rest, count):
                rows = change[TILE * q : TILE * (q + 1)]
                left[q] = left[q] - rows[:, :n]
                right[q] = right[q] - rows[:, n:]
    upper = [jnp.where(lane >= sub + TILE * i, left[i] * scale[i], 0.0) for i in range(count)]
    lower = [right[i] * scale[i] for i in range(count)]
    return jnp.concatenate(upper, axis=0), jnp.concatenate(lower, axis=0)


def pack(gram):
    n = gram.shape[0]
    q = n // 4
    middle = jnp.concatenate([gram[q : 2 * q, q:], gram[3 * q :, 3 * q :]], axis=1)
    low = gram[2 * q : 3 * q, 2 * q :]
    tail = jnp.concatenate([low[: q // 2], low[q // 2 :]], axis=1)
    return jnp.concatenate([gram[:q], middle, tail], axis=0)


def unpack(packed):
    n = packed.shape[1]
    q = n // 4
    middle, tail = packed[q : 2 * q], packed[2 * q :]
    low = jnp.concatenate([tail[:, : 2 * q], tail[:, 2 * q :]], axis=0)
    second = jnp.concatenate([jnp.zeros((q, q), jnp.float32), middle[:, : 3 * q]], axis=1)
    third = jnp.concatenate([jnp.zeros((q, 2 * q), jnp.float32), low], axis=1)
    fourth = jnp.concatenate([jnp.zeros((q, 3 * q), jnp.float32), middle[:, 3 * q :]], axis=1)
    upper = jnp.concatenate([packed[:q], second, third, fourth], axis=0)
    row = lax.broadcasted_iota(jnp.int32, (n, n), 0)
    column = lax.broadcasted_iota(jnp.int32, (n, n), 1)
    return jnp.where(row <= column, upper, jnp.transpose(upper))


def store_halves(core, gram, own_ref, other_ref):
    packed = pack(gram)
    middle = packed.shape[0] // 2
    first, second = packed[:middle], packed[middle:]
    own_ref[...] = jnp.where(core == 0, first, second)
    other_ref[...] = jnp.where(core == 0, second, first)


def load_halves(core, own, other):
    first = jnp.where(core == 0, own, other)
    second = jnp.where(core == 0, other, own)
    return unpack(jnp.concatenate([first, second], axis=0))


def floor_of(gram):
    return 1e-9 * jnp.max(gram)


def without(kernel, place, count):
    def call(*refs):
        kernel(*refs[:place], *refs[place + count :])

    return call


def small_call(kernel, shapes, name, cycles, operands, scalars=(), after=()):
    memory = pl.BlockSpec(memory_space=pltpu.VMEM)
    return pl.pallas_call(
        without(kernel, len(scalars) + len(operands), len(after)),
        in_specs=[pl.BlockSpec(memory_space=pltpu.SMEM)] * len(scalars)
        + [memory] * len(operands)
        + [pl.BlockSpec(memory_space=pl.ANY)] * len(after),
        out_specs=[memory] * len(shapes),
        out_shape=[jax.ShapeDtypeStruct(shape, jnp.float32) for shape in shapes],
        compiler_params=params(),
        cost_estimate=pl.CostEstimate(
            flops=cycles * 10**6, bytes_accessed=4 * shapes[0][-1], transcendentals=0
        ),
        name=name,
    )(*scalars, *operands, *after)


def plain_call(kernel, shape, name, *operands, after=()):
    return small_call(kernel, [shape], name, 100, operands, after=after)[0]


def gram_kernel(core_ref, value_ref, own_ref, other_ref):
    value = value_ref[...]
    store_halves(core_ref[0], dot(value, value, CONTRACT, HIGHEST), own_ref, other_ref)


def add_kernel(first_ref, second_ref, out_ref):
    out_ref[...] = first_ref[...] + second_ref[...]


def total_kernel(scale, pieces_ref, out_ref):
    value = pieces_ref[0]
    for place in range(1, pieces_ref.shape[0]):
        value += pieces_ref[place]
    out_ref[...] = jnp.broadcast_to((value * scale)[None], out_ref.shape)


def add(first, second, after=()):
    return plain_call(add_kernel, first.shape, "add", first, second, after=after)


def pair_kernel(own_ref, other_ref, out_ref):
    out_ref[...] = jnp.broadcast_to((own_ref[...] + other_ref[...])[None], out_ref.shape)


def total(pieces, count, scale=1.0):
    shape = (count,) + pieces.shape[1:]
    return plain_call(functools.partial(total_kernel, scale), shape, "total", pieces)


def join_kernel(product_ref, sent_ref, own_ref, other_ref, out_ref):
    height = product_ref.shape[1]
    out_ref[:, :height] = product_ref[...] + sent_ref[...]
    gram = own_ref[...] + other_ref[...]
    out_ref[:, height:] = jnp.broadcast_to(gram[None], (out_ref.shape[0],) + gram.shape)


def tail_kernel(start, pieces_ref, out_ref):
    value = pieces_ref[0, start:]
    for place in range(1, pieces_ref.shape[0]):
        value += pieces_ref[place, start:]
    out_ref[...] = value


def middle_kernel(
    core_ref, pieces_ref, pulled_own_ref, pulled_other_ref, inner_ref, before_ref, own_ref, other_ref
):
    gram = load_halves(core_ref[0], pulled_own_ref[...], pulled_other_ref[...])
    before_ref[...], lower = eliminate(gram, floor_of(gram))
    height = inner_ref.shape[0]
    sketch = pieces_ref[0, :height]
    for place in range(1, pieces_ref.shape[0]):
        sketch += pieces_ref[place, :height]
    inner = dot(sketch, lower, TRANSPOSED, HIGHEST)
    inner_ref[...] = inner
    store_halves(core_ref[0], dot(inner, inner, CONTRACT, HIGHEST), own_ref, other_ref)


def last_kernel(
    root_rows, core_ref, own_ref, other_ref, inner_ref, before_ref, basis_ref, factor_ref
):
    gram = load_halves(core_ref[0], own_ref[...], other_ref[...])
    upper, lower = eliminate(gram, floor_of(gram))
    basis_ref[...] = dot(inner_ref[...], lower, TRANSPOSED, HIGHEST) * root_rows
    factor_ref[...] = dot(upper, before_ref[...], precision=HIGHEST) / root_rows


def local(slab, test_matrix):
    rows, columns = slab.shape
    wide = test_matrix.shape[1]
    zs = lax.axis_size("z")
    row_count = lax.axis_size(ROW)
    row_total = rows * row_count
    root_rows = math.sqrt(row_total)
    core = lax.axis_index("core").astype(jnp.int32).reshape(1)
    far = 1 - core
    slab = slab.reshape(zs, 2, -1, columns)
    square = (wide, wide)
    halves = [(5 * wide // 16, wide)] * 2

    sent = swap(multiply(slab, test_matrix, far))
    product = multiply(slab, test_matrix, core)
    made = parts_of(slab, core, 0)
    part = add(product, sent, made[:1])
    own = exchange(total(exchange(part, "z"), zs), "z")

    *made, own = parts_of(slab, core, 1, made, own)
    parts, far_parts = made[:COUNT], made[COUNT:]
    other = swap(own)
    part = pull(other, far_parts, pull(own, parts))
    pieces = total(exchange(part.reshape(row_count, -1, wide), ROW), row_count, 1.0 / row_total)
    pulled = exchange(pieces, ROW).reshape(-1, wide)

    own, other = small_call(gram_kernel, halves, "gram", 700, [pulled], [core])
    other = swap(other)
    sent = swap(project(pulled, far_parts))
    product = project(pulled, parts)
    height = product.shape[1]
    shape = (zs, height + own.shape[0], wide)
    joined = plain_call(join_kernel, shape, "join", product, sent, own, other)
    pieces = exchange(joined, "z")
    own = plain_call(functools.partial(tail_kernel, height), own.shape, "tail", pieces)

    inner, before, own, other = small_call(
        middle_kernel,
        [(height, wide), square] + halves,
        "middle",
        4300,
        [pieces, own, swap(own)],
        [core],
    )
    copies = plain_call(pair_kernel, (row_count,) + own.shape, "pair", own, swap(other))
    copies = total(exchange(copies, ROW), zs)
    own = total(exchange(copies, "z"), 1)[0]
    basis, factor = small_call(
        functools.partial(last_kernel, root_rows),
        [inner.shape, square],
        "last",
        4600,
        [own, swap(own), inner, before],
        [core],
    )
    return basis, factor


def solution(mesh):
    sizes = dict(mesh.shape)
    chips = mesh.devices.reshape(4, sizes["row"] // 4, sizes["col"] // 2, 2)
    fine = Mesh(chips, ("y", "x", "z", "core"))
    col = ("z", "core")
    in_specs = (P(ROW, col), P(col, None))
    out_specs = (P(ROW + col, None), P())
    return jax.shard_map(local, mesh=fine, in_specs=in_specs, out_specs=out_specs, check_vma=False)
```

```python
import functools
import math

import jax
import jax.numpy as jnp
from jax import lax
from jax.experimental import pallas as pl
from jax.experimental.pallas import tpu as pltpu
from jax.sharding import Mesh
from jax.sharding import PartitionSpec as P

HIGHEST = lax.Precision.HIGHEST
CONTRACT = (((0,), (0,)), ((), ()))
TRANSPOSED = (((1,), (1,)), ((), ()))
ROW = ("y", "x")
SWAP = [(0, 1), (1, 0)]
TILE = 8
PANEL = 16
STEP = 2
PULL = 8
PARTS = 5
VMEM = 12 * 1024 * 1024


def swap(value):
    return lax.ppermute(value, "core", SWAP)


def exchange(value, axes):
    return lax.all_to_all(value, axes, 0, 0, tiled=False)


def dot(a, b, dims=(((1,), (0,)), ((), ())), precision=None):
    return lax.dot_general(a, b, dims, precision=precision, preferred_element_type=jnp.float32)


def split(value, count):
    parts = []
    for _ in range(count):
        parts.append(value.astype(jnp.bfloat16))
        value = value - parts[-1].astype(jnp.float32)
    return parts


keep = pltpu.with_memory_space_constraint


def params():
    return pltpu.CompilerParams(vmem_limit_bytes=VMEM)


def rows_of(ref, place, height):
    return ref[place : place + height].reshape(-1, ref.shape[-1])


def multiply_kernel(half_ref, slab_ref, right_ref, out_ref, pair_ref, block_ref, right_buffer, sems):
    half, zs, wide = half_ref[0], block_ref.shape[0], out_ref.shape[-1]
    right_copy = pltpu.make_async_copy(right_ref, right_buffer, sems.at[zs])
    right_copy.start()
    copies = [
        pltpu.make_async_copy(slab_ref.at[place, half], block_ref.at[place], sems.at[place])
        for place in range(zs)
    ]
    for copy in copies:
        copy.start()
    right_copy.wait()
    high, low = split(right_buffer[...], 2)
    pair_ref[:, :wide] = high
    pair_ref[:, wide:] = low
    for place in range(0, zs, STEP):
        for copy in copies[place : place + STEP]:
            copy.wait()
        high, low = split(rows_of(block_ref, place, STEP), 2)
        first = dot(high, pair_ref[...])
        value = first[:, :wide] + (first[:, wide:] + dot(low, pair_ref[:, :wide]))
        out_ref[place : place + STEP] = value.reshape(STEP, -1, wide)


def multiply(slab, right, half):
    zs, _, height, depth = slab.shape
    wide = right.shape[1]
    high_memory = pl.BlockSpec(memory_space=pltpu.HBM)
    return pl.pallas_call(
        multiply_kernel,
        in_specs=[pl.BlockSpec(memory_space=pltpu.SMEM), high_memory, high_memory],
        out_specs=pl.BlockSpec(memory_space=pltpu.VMEM),
        scratch_shapes=[
            pltpu.VMEM((depth, 2 * wide), jnp.bfloat16),
            pltpu.VMEM((zs, height, depth), jnp.float32),
            pltpu.VMEM((depth, wide), jnp.float32),
            pltpu.SemaphoreType.DMA((zs + 1,)),
        ],
        out_shape=jax.ShapeDtypeStruct((zs, height, wide), jnp.float32),
        compiler_params=params(),
        cost_estimate=cost(zs * height, depth, wide, 4),
        name="multiply",
    )(half, keep(slab, pltpu.HBM), keep(right, pltpu.HBM))


def parts_kernel(turn, slab_ref, part_refs, block_ref, sems):
    zs, _, height, _ = block_ref.shape
    copies = [
        [
            pltpu.make_async_copy(
                slab_ref.at[place, half], block_ref.at[place, half], sems.at[place, half]
            )
            for half in range(2)
        ]
        for place in range(zs)
    ]
    for pair in copies:
        for copy in pair:
            copy.start()
    for place in range(zs):
        for half in range(2):
            refs = part_refs[PARTS * (half != turn) :][:PARTS]
            copies[place][half].wait()
            block = block_ref[place, half]
            for part, ref in zip(split(block, 2), refs[:2]):
                ref[place] = part
            for part, ref in zip(split(jnp.transpose(block), 3), refs[2:]):
                ref[:, place * height : (place + 1) * height] = part


def parts_of(slab, core, turn, before=(), passed=None):
    zs, _, height, depth = slab.shape
    high_memory = pl.BlockSpec(memory_space=pltpu.HBM)
    memory = pl.BlockSpec(memory_space=pltpu.VMEM)
    count = 2 * PARTS
    through = [] if passed is None else [passed]
    shapes = [pltpu.VMEM((zs, height, depth), jnp.bfloat16)] * 2
    shapes += [pltpu.VMEM((depth, zs * height), jnp.bfloat16)] * 3
    shapes = shapes * 2
    shapes += [jax.ShapeDtypeStruct(value.shape, value.dtype) for value in through]
    place = 2 + len(through)
    aliases = {2: count} if through else {}
    aliases |= {place + i: i for i in range(len(before))}

    def kernel(*refs):
        outs = refs[place + len(before) :]

        @pl.when(refs[0][0] == turn)
        def _():
            parts_kernel(turn, refs[1], outs[:count], *outs[-2:])

    return pl.pallas_call(
        kernel,
        in_specs=[pl.BlockSpec(memory_space=pltpu.SMEM), high_memory]
        + [memory] * (len(through) + len(before)),
        out_specs=[memory] * (count + len(through)),
        scratch_shapes=[
            pltpu.VMEM((zs, 2, height, depth), jnp.float32),
            pltpu.SemaphoreType.DMA((zs, 2)),
        ],
        out_shape=shapes,
        input_output_aliases=aliases,
        compiler_params=params(),
        cost_estimate=cost(2 * zs * height, depth, 128, 4),
        name="parts",
    )(core, keep(slab, pltpu.HBM), *through, *[keep(part, pltpu.VMEM) for part in before])


def cost(height, depth, wide, times):
    return pl.CostEstimate(
        flops=2 * height * depth * wide * times,
        bytes_accessed=4 * height * depth,
        transcendentals=0,
    )


def project_kernel(right_ref, high_ref, middle_ref, low_ref, out_ref):
    wide, height = right_ref.shape[1], out_ref.shape[1]
    parts = split(jnp.transpose(right_ref[...]), 3)
    stack = jnp.concatenate(parts, axis=0)
    for place in range(0, out_ref.shape[0], STEP):
        run = slice(place * height, (place + STEP) * height)
        first = dot(stack, high_ref[:, run])
        second = dot(stack[: 2 * wide], middle_ref[:, run])
        third = first[2 * wide :] + dot(parts[0], low_ref[:, run])
        small = (first[wide : 2 * wide] + second[:wide]) + (second[wide:] + third)
        value = jnp.transpose(first[:wide] + small)
        out_ref[place : place + STEP] = value.reshape(STEP, height, wide)


def project(right, parts, zs):
    depth, height = parts[0].shape
    wide = right.shape[1]
    memory = pl.BlockSpec(memory_space=pltpu.VMEM)
    return pl.pallas_call(
        project_kernel,
        in_specs=[memory] * 4,
        out_specs=memory,
        out_shape=jax.ShapeDtypeStruct((zs, height // zs, wide), jnp.float32),
        compiler_params=params(),
        cost_estimate=cost(height, depth, wide, 8),
        name="project",
    )(right, *[keep(part, pltpu.VMEM) for part in parts])


def pull_kernel(more, left_ref, high_ref, low_ref, *refs):
    out_ref = refs[-1]
    zs, wide = left_ref.shape[0], left_ref.shape[-1]
    total = None
    for place in range(0, zs, PULL):
        left = jnp.transpose(rows_of(left_ref, place, PULL))
        high, low = split(left, 2)
        block = rows_of(high_ref, place, PULL)
        both = dot(jnp.concatenate([high, low], axis=0), block)
        value = both[:wide] + (both[wide:] + dot(high, rows_of(low_ref, place, PULL)))
        total = value if total is None else total + value
    result = jnp.transpose(total)
    out_ref[...] = result + refs[0][...] if more else result


def pull(left, parts, before=None):
    zs, height, depth = parts[0].shape
    wide = left.shape[-1]
    memory = pl.BlockSpec(memory_space=pltpu.VMEM)
    more = before is not None
    return pl.pallas_call(
        functools.partial(pull_kernel, more),
        in_specs=[memory] * (3 + more),
        out_specs=memory,
        out_shape=jax.ShapeDtypeStruct((depth, wide), jnp.float32),
        compiler_params=params(),
        cost_estimate=cost(zs * height, depth, wide, 4),
        name="pull",
    )(left, *[keep(part, pltpu.VMEM) for part in parts], *([before] if more else []))


def spread(row):
    return jnp.broadcast_to(row, (TILE, row.shape[1]))


def eliminate(gram, floor):
    n = gram.shape[0]
    count, per = n // TILE, PANEL // TILE
    sub = lax.broadcasted_iota(jnp.int32, (TILE, n), 0)
    lane = lax.broadcasted_iota(jnp.int32, (TILE, n), 1)
    left = [gram[TILE * i : TILE * (i + 1)] for i in range(count)]
    right = [(lane == sub + TILE * i).astype(jnp.float32) for i in range(count)]
    scale = [None] * count
    for start in range(0, count, per):
        tiles = range(start, min(start + 2 * per, count))
        base = start * TILE
        column = {
            (t, q): jnp.broadcast_to(left[q][:, base + t : base + t + 1], (TILE, n))
            for t in range(PANEL)
            for q in tiles
            if start + t // TILE <= q
        }
        pivots = []
        for s in range(PANEL):
            here, at = start + s // TILE, s % TILE
            pivot = jnp.maximum(spread(column[s, here][at : at + 1]), floor)
            over = 1.0 / pivot
            pivots.append(pivot)
            entry = {
                t: spread(column[s, start + t // TILE][t % TILE : t % TILE + 1])
                if start + t // TILE > here
                else spread(column[t, here][at : at + 1])
                for t in range(s + 1, PANEL)
            }
            left_row, right_row = spread(left[here][at : at + 1]), spread(right[here][at : at + 1])
            for q in tiles:
                if q < here:
                    continue
                ratio = column[s, q] * over
                if q == here:
                    ratio = jnp.where(sub > at, ratio, 0.0)
                for t in range(s + 1, PANEL):
                    if (t, q) in column:
                        column[t, q] = column[t, q] - ratio * entry[t]
                left[q] = left[q] - ratio * left_row
                right[q] = right[q] - ratio * right_row
        for i in range(per):
            own = [pivots[i * TILE + s][s : s + 1] for s in range(TILE)]
            scale[start + i] = lax.rsqrt(jnp.concatenate(own, axis=0))
        rest = start + 2 * per
        if rest < count:
            panel = range(start, start + per)
            u = jnp.concatenate([left[i] * scale[i] for i in panel], axis=0)
            v = jnp.concatenate([right[i] * scale[i] for i in panel], axis=0)
            change = dot(u, jnp.concatenate([u, v], axis=1), CONTRACT, HIGHEST)
            for q in range(rest, count):
                rows = change[TILE * q : TILE * (q + 1)]
                left[q] = left[q] - rows[:, :n]
                right[q] = right[q] - rows[:, n:]
    upper = [jnp.where(lane >= sub + TILE * i, left[i] * scale[i], 0.0) for i in range(count)]
    lower = [right[i] * scale[i] for i in range(count)]
    return jnp.concatenate(upper, axis=0), jnp.concatenate(lower, axis=0)


def pack(gram):
    n = gram.shape[0]
    q = n // 4
    middle = jnp.concatenate([gram[q : 2 * q, q:], gram[3 * q :, 3 * q :]], axis=1)
    low = gram[2 * q : 3 * q, 2 * q :]
    tail = jnp.concatenate([low[: q // 2], low[q // 2 :]], axis=1)
    return jnp.concatenate([gram[:q], middle, tail], axis=0)


def unpack(packed):
    n = packed.shape[1]
    q = n // 4
    middle, tail = packed[q : 2 * q], packed[2 * q :]
    low = jnp.concatenate([tail[:, : 2 * q], tail[:, 2 * q :]], axis=0)
    second = jnp.concatenate([jnp.zeros((q, q), jnp.float32), middle[:, : 3 * q]], axis=1)
    third = jnp.concatenate([jnp.zeros((q, 2 * q), jnp.float32), low], axis=1)
    fourth = jnp.concatenate([jnp.zeros((q, 3 * q), jnp.float32), middle[:, 3 * q :]], axis=1)
    upper = jnp.concatenate([packed[:q], second, third, fourth], axis=0)
    row = lax.broadcasted_iota(jnp.int32, (n, n), 0)
    column = lax.broadcasted_iota(jnp.int32, (n, n), 1)
    return jnp.where(row <= column, upper, jnp.transpose(upper))


def store_halves(core, gram, own_ref, other_ref):
    packed = pack(gram)
    middle = packed.shape[0] // 2
    first, second = packed[:middle], packed[middle:]
    own_ref[...] = jnp.where(core == 0, first, second)
    other_ref[...] = jnp.where(core == 0, second, first)


def load_halves(core, own, other):
    first = jnp.where(core == 0, own, other)
    second = jnp.where(core == 0, other, own)
    return unpack(jnp.concatenate([first, second], axis=0))


def floor_of(gram):
    return 1e-9 * jnp.max(gram)


def without(kernel, place, count):
    def call(*refs):
        kernel(*refs[:place], *refs[place + count :])

    return call


def small_call(kernel, shapes, name, cycles, operands, scalars=(), after=()):
    memory = pl.BlockSpec(memory_space=pltpu.VMEM)
    return pl.pallas_call(
        without(kernel, len(scalars) + len(operands), len(after)),
        in_specs=[pl.BlockSpec(memory_space=pltpu.SMEM)] * len(scalars)
        + [memory] * len(operands)
        + [pl.BlockSpec(memory_space=pl.ANY)] * len(after),
        out_specs=[memory] * len(shapes),
        out_shape=[jax.ShapeDtypeStruct(shape, jnp.float32) for shape in shapes],
        compiler_params=params(),
        cost_estimate=pl.CostEstimate(
            flops=cycles * 10**6, bytes_accessed=4 * shapes[0][-1], transcendentals=0
        ),
        name=name,
    )(*scalars, *operands, *after)


def plain_call(kernel, shape, name, *operands, after=()):
    return small_call(kernel, [shape], name, 100, operands, after=after)[0]


def gram_kernel(core_ref, value_ref, own_ref, other_ref):
    value = value_ref[...]
    store_halves(core_ref[0], dot(value, value, CONTRACT, HIGHEST), own_ref, other_ref)


def add_kernel(first_ref, second_ref, out_ref):
    out_ref[...] = first_ref[...] + second_ref[...]


def total_kernel(scale, pieces_ref, out_ref):
    value = pieces_ref[0]
    for place in range(1, pieces_ref.shape[0]):
        value += pieces_ref[place]
    out_ref[...] = jnp.broadcast_to((value * scale)[None], out_ref.shape)


def add(first, second, after=()):
    return plain_call(add_kernel, first.shape, "add", first, second, after=after)


def pair_kernel(own_ref, other_ref, out_ref):
    out_ref[...] = jnp.broadcast_to((own_ref[...] + other_ref[...])[None], out_ref.shape)


def total(pieces, count, scale=1.0):
    shape = (count,) + pieces.shape[1:]
    return plain_call(functools.partial(total_kernel, scale), shape, "total", pieces)


def join_kernel(product_ref, sent_ref, own_ref, other_ref, out_ref):
    height = product_ref.shape[1]
    out_ref[:, :height] = product_ref[...] + sent_ref[...]
    gram = own_ref[...] + other_ref[...]
    out_ref[:, height:] = jnp.broadcast_to(gram[None], (out_ref.shape[0],) + gram.shape)


def tail_kernel(start, pieces_ref, out_ref):
    value = pieces_ref[0, start:]
    for place in range(1, pieces_ref.shape[0]):
        value += pieces_ref[place, start:]
    out_ref[...] = value


def middle_kernel(
    core_ref, pieces_ref, pulled_own_ref, pulled_other_ref, inner_ref, before_ref, own_ref, other_ref
):
    gram = load_halves(core_ref[0], pulled_own_ref[...], pulled_other_ref[...])
    before_ref[...], lower = eliminate(gram, floor_of(gram))
    height = inner_ref.shape[0]
    sketch = pieces_ref[0, :height]
    for place in range(1, pieces_ref.shape[0]):
        sketch += pieces_ref[place, :height]
    inner = dot(sketch, lower, TRANSPOSED, HIGHEST)
    inner_ref[...] = inner
    store_halves(core_ref[0], dot(inner, inner, CONTRACT, HIGHEST), own_ref, other_ref)


def last_kernel(
    root_rows, core_ref, own_ref, other_ref, inner_ref, before_ref, basis_ref, factor_ref
):
    gram = load_halves(core_ref[0], own_ref[...], other_ref[...])
    upper, lower = eliminate(gram, floor_of(gram))
    basis_ref[...] = dot(inner_ref[...], lower, TRANSPOSED, HIGHEST) * root_rows
    factor_ref[...] = dot(upper, before_ref[...], precision=HIGHEST) / root_rows


def local(slab, test_matrix):
    rows, columns = slab.shape
    wide = test_matrix.shape[1]
    zs = lax.axis_size("z")
    row_count = lax.axis_size(ROW)
    row_total = rows * row_count
    root_rows = math.sqrt(row_total)
    core = lax.axis_index("core").astype(jnp.int32).reshape(1)
    far = 1 - core
    slab = slab.reshape(zs, 2, -1, columns)
    square = (wide, wide)
    halves = [(5 * wide // 16, wide)] * 2

    sent = swap(multiply(slab, test_matrix, far))
    product = multiply(slab, test_matrix, core)
    made = parts_of(slab, core, 0)
    part = add(product, sent, made[:1])
    own = exchange(total(exchange(part, "z"), zs), "z")

    *made, own = parts_of(slab, core, 1, made, own)
    parts, far_parts = made[:PARTS], made[PARTS:]
    other = swap(own)
    part = pull(other, far_parts[:2], pull(own, parts[:2]))
    pieces = total(exchange(part.reshape(row_count, -1, wide), ROW), row_count, 1.0 / row_total)
    pulled = exchange(pieces, ROW).reshape(-1, wide)

    own, other = small_call(gram_kernel, halves, "gram", 700, [pulled], [core])
    other = swap(other)
    sent = swap(project(pulled, far_parts[2:], zs))
    product = project(pulled, parts[2:], zs)
    height = product.shape[1]
    shape = (zs, height + own.shape[0], wide)
    joined = plain_call(join_kernel, shape, "join", product, sent, own, other)
    pieces = exchange(joined, "z")
    own = plain_call(functools.partial(tail_kernel, height), own.shape, "tail", pieces)

    inner, before, own, other = small_call(
        middle_kernel,
        [(height, wide), square] + halves,
        "middle",
        4300,
        [pieces, own, swap(own)],
        [core],
    )
    copies = plain_call(pair_kernel, (row_count,) + own.shape, "pair", own, swap(other))
    copies = total(exchange(copies, ROW), zs)
    own = total(exchange(copies, "z"), 1)[0]
    basis, factor = small_call(
        functools.partial(last_kernel, root_rows),
        [inner.shape, square],
        "last",
        4600,
        [own, swap(own), inner, before],
        [core],
    )
    return basis, factor


def solution(mesh):
    sizes = dict(mesh.shape)
    chips = mesh.devices.reshape(4, sizes["row"] // 4, sizes["col"] // 2, 2)
    fine = Mesh(chips, ("y", "x", "z", "core"))
    col = ("z", "core")
    in_specs = (P(ROW, col), P(col, None))
    out_specs = (P(ROW + col, None), P())
    return jax.shard_map(local, mesh=fine, in_specs=in_specs, out_specs=out_specs, check_vma=False)
```

```python
import functools
import math

import jax
import jax.numpy as jnp
from jax import lax
from jax.experimental import pallas as pl
from jax.experimental.pallas import tpu as pltpu
from jax.sharding import Mesh
from jax.sharding import PartitionSpec as P

PLAIN = (((1,), (0,)), ((), ()))
CONTRACT = (((0,), (0,)), ((), ()))
TRANSPOSED = (((1,), (1,)), ((), ()))
ROW = ("y", "x")
SWAP = [(0, 1), (1, 0)]
TILE = 8
PANEL = 16
STEP = 2
PULL = 8
PARTS = 5
VMEM = 12 * 1024 * 1024


def swap(value):
    return lax.ppermute(value, "core", SWAP)


def exchange(value, axes):
    return lax.all_to_all(value, axes, 0, 0, tiled=False)


def dot(a, b, dims=PLAIN):
    return lax.dot_general(a, b, dims, preferred_element_type=jnp.float32)


def split(value, count):
    parts = []
    for _ in range(count):
        parts.append(value.astype(jnp.bfloat16))
        value = value - parts[-1].astype(jnp.float32)
    return parts


keep = pltpu.with_memory_space_constraint


def stacked(a, b, dims):
    (first,), (second,) = dims[0]
    a1, a2, a3 = split(a, 3)
    b1, b2, b3 = split(b, 3)
    left = jnp.concatenate([a1, a1, a2, a2, a1, a3], axis=first)
    return dot(left, jnp.concatenate([b1, b2, b1, b2, b3, b1], axis=second), dims)


def gram_of(value):
    wide = value.shape[1]
    high, middle, low = split(value, 3)
    pair = jnp.concatenate([high, middle], axis=1)
    four, cross = dot(pair, pair, CONTRACT), dot(high, low, CONTRACT)
    small = four[wide:, wide:] + (cross + jnp.transpose(cross))
    return four[:wide, :wide] + (four[:wide, wide:] + four[wide:, :wide] + small)


def params():
    return pltpu.CompilerParams(vmem_limit_bytes=VMEM)


def rows_of(ref, place, height):
    return ref[place : place + height].reshape(-1, ref.shape[-1])


def multiply_kernel(half_ref, slab_ref, right_ref, out_ref, pair_ref, block_ref, right_buffer, sems):
    half, zs, wide = half_ref[0], block_ref.shape[0], out_ref.shape[-1]
    right_copy = pltpu.make_async_copy(right_ref, right_buffer, sems.at[zs])
    right_copy.start()
    copies = [
        pltpu.make_async_copy(slab_ref.at[place, half], block_ref.at[place], sems.at[place])
        for place in range(zs)
    ]
    for copy in copies:
        copy.start()
    right_copy.wait()
    high, low = split(right_buffer[...], 2)
    pair_ref[:, :wide] = high
    pair_ref[:, wide:] = low
    for place in range(0, zs, STEP):
        for copy in copies[place : place + STEP]:
            copy.wait()
        high, low = split(rows_of(block_ref, place, STEP), 2)
        first = dot(high, pair_ref[...])
        value = first[:, :wide] + (first[:, wide:] + dot(low, pair_ref[:, :wide]))
        out_ref[place : place + STEP] = value.reshape(STEP, -1, wide)


def multiply(slab, right, half):
    zs, _, height, depth = slab.shape
    wide = right.shape[1]
    high_memory = pl.BlockSpec(memory_space=pltpu.HBM)
    return pl.pallas_call(
        multiply_kernel,
        in_specs=[pl.BlockSpec(memory_space=pltpu.SMEM), high_memory, high_memory],
        out_specs=pl.BlockSpec(memory_space=pltpu.VMEM),
        scratch_shapes=[
            pltpu.VMEM((depth, 2 * wide), jnp.bfloat16),
            pltpu.VMEM((zs, height, depth), jnp.float32),
            pltpu.VMEM((depth, wide), jnp.float32),
            pltpu.SemaphoreType.DMA((zs + 1,)),
        ],
        out_shape=jax.ShapeDtypeStruct((zs, height, wide), jnp.float32),
        compiler_params=params(),
        cost_estimate=cost(zs * height, depth, wide, 4),
        name="multiply",
    )(half, keep(slab, pltpu.HBM), keep(right, pltpu.HBM))


def parts_kernel(turn, slab_ref, part_refs, block_ref, sems):
    zs, _, height, _ = block_ref.shape
    copies = [
        [
            pltpu.make_async_copy(
                slab_ref.at[place, half], block_ref.at[place, half], sems.at[place, half]
            )
            for half in range(2)
        ]
        for place in range(zs)
    ]
    for pair in copies:
        for copy in pair:
            copy.start()
    for place in range(zs):
        for half in range(2):
            refs = part_refs[PARTS * (half != turn) :][:PARTS]
            copies[place][half].wait()
            block = block_ref[place, half]
            for part, ref in zip(split(block, 2), refs[:2]):
                ref[place] = part
            for part, ref in zip(split(jnp.transpose(block), 3), refs[2:]):
                ref[:, place * height : (place + 1) * height] = part


def parts_of(slab, core, turn, before=(), passed=None):
    zs, _, height, depth = slab.shape
    high_memory = pl.BlockSpec(memory_space=pltpu.HBM)
    memory = pl.BlockSpec(memory_space=pltpu.VMEM)
    count = 2 * PARTS
    through = [] if passed is None else [passed]
    shapes = [pltpu.VMEM((zs, height, depth), jnp.bfloat16)] * 2
    shapes += [pltpu.VMEM((depth, zs * height), jnp.bfloat16)] * 3
    shapes = shapes * 2
    shapes += [jax.ShapeDtypeStruct(value.shape, value.dtype) for value in through]
    place = 2 + len(through)
    aliases = {2: count} if through else {}
    aliases |= {place + i: i for i in range(len(before))}

    def kernel(*refs):
        outs = refs[place + len(before) :]

        @pl.when(refs[0][0] == turn)
        def _():
            parts_kernel(turn, refs[1], outs[:count], *outs[-2:])

    return pl.pallas_call(
        kernel,
        in_specs=[pl.BlockSpec(memory_space=pltpu.SMEM), high_memory]
        + [memory] * (len(through) + len(before)),
        out_specs=[memory] * (count + len(through)),
        scratch_shapes=[
            pltpu.VMEM((zs, 2, height, depth), jnp.float32),
            pltpu.SemaphoreType.DMA((zs, 2)),
        ],
        out_shape=shapes,
        input_output_aliases=aliases,
        compiler_params=params(),
        cost_estimate=cost(2 * zs * height, depth, 128, 4),
        name="parts",
    )(core, keep(slab, pltpu.HBM), *through, *[keep(part, pltpu.VMEM) for part in before])


def cost(height, depth, wide, times):
    return pl.CostEstimate(
        flops=2 * height * depth * wide * times,
        bytes_accessed=4 * height * depth,
        transcendentals=0,
    )


def project_kernel(right_ref, high_ref, middle_ref, low_ref, out_ref):
    wide, height = right_ref.shape[1], out_ref.shape[1]
    parts = split(jnp.transpose(right_ref[...]), 3)
    stack = jnp.concatenate(parts, axis=0)
    for place in range(0, out_ref.shape[0], STEP):
        run = slice(place * height, (place + STEP) * height)
        first = dot(stack, high_ref[:, run])
        second = dot(stack[: 2 * wide], middle_ref[:, run])
        third = first[2 * wide :] + dot(parts[0], low_ref[:, run])
        small = (first[wide : 2 * wide] + second[:wide]) + (second[wide:] + third)
        value = jnp.transpose(first[:wide] + small)
        out_ref[place : place + STEP] = value.reshape(STEP, height, wide)


def project(right, parts, zs):
    depth, height = parts[0].shape
    wide = right.shape[1]
    memory = pl.BlockSpec(memory_space=pltpu.VMEM)
    return pl.pallas_call(
        project_kernel,
        in_specs=[memory] * 4,
        out_specs=memory,
        out_shape=jax.ShapeDtypeStruct((zs, height // zs, wide), jnp.float32),
        compiler_params=params(),
        cost_estimate=cost(height, depth, wide, 8),
        name="project",
    )(right, *[keep(part, pltpu.VMEM) for part in parts])


def pull_kernel(more, left_ref, high_ref, low_ref, *refs):
    out_ref = refs[-1]
    zs, wide = left_ref.shape[0], left_ref.shape[-1]
    total = None
    for place in range(0, zs, PULL):
        left = jnp.transpose(rows_of(left_ref, place, PULL))
        high, low = split(left, 2)
        block = rows_of(high_ref, place, PULL)
        both = dot(jnp.concatenate([high, low], axis=0), block)
        value = both[:wide] + (both[wide:] + dot(high, rows_of(low_ref, place, PULL)))
        total = value if total is None else total + value
    result = jnp.transpose(total)
    out_ref[...] = result + refs[0][...] if more else result


def pull(left, parts, before=None):
    zs, height, depth = parts[0].shape
    wide = left.shape[-1]
    memory = pl.BlockSpec(memory_space=pltpu.VMEM)
    more = before is not None
    return pl.pallas_call(
        functools.partial(pull_kernel, more),
        in_specs=[memory] * (3 + more),
        out_specs=memory,
        out_shape=jax.ShapeDtypeStruct((depth, wide), jnp.float32),
        compiler_params=params(),
        cost_estimate=cost(zs * height, depth, wide, 4),
        name="pull",
    )(left, *[keep(part, pltpu.VMEM) for part in parts], *([before] if more else []))


def spread(row):
    return jnp.broadcast_to(row, (TILE, row.shape[1]))


def eliminate(gram, floor):
    n = gram.shape[0]
    count, per = n // TILE, PANEL // TILE
    sub = lax.broadcasted_iota(jnp.int32, (TILE, n), 0)
    lane = lax.broadcasted_iota(jnp.int32, (TILE, n), 1)
    left = [gram[TILE * i : TILE * (i + 1)] for i in range(count)]
    right = [(lane == sub + TILE * i).astype(jnp.float32) for i in range(count)]
    scale = [None] * count
    for start in range(0, count, per):
        tiles = range(start, min(start + 2 * per, count))
        base = start * TILE
        column = {
            (t, q): jnp.broadcast_to(left[q][:, base + t : base + t + 1], (TILE, n))
            for t in range(PANEL)
            for q in tiles
            if start + t // TILE <= q
        }
        pivots = []
        for s in range(PANEL):
            here, at = start + s // TILE, s % TILE
            pivot = jnp.maximum(spread(column[s, here][at : at + 1]), floor)
            over = 1.0 / pivot
            pivots.append(pivot)
            entry = {
                t: spread(column[s, start + t // TILE][t % TILE : t % TILE + 1])
                if start + t // TILE > here
                else spread(column[t, here][at : at + 1])
                for t in range(s + 1, PANEL)
            }
            left_row, right_row = spread(left[here][at : at + 1]), spread(right[here][at : at + 1])
            for q in tiles:
                if q < here:
                    continue
                ratio = column[s, q] * over
                if q == here:
                    ratio = jnp.where(sub > at, ratio, 0.0)
                for t in range(s + 1, PANEL):
                    if (t, q) in column:
                        column[t, q] = column[t, q] - ratio * entry[t]
                left[q] = left[q] - ratio * left_row
                right[q] = right[q] - ratio * right_row
        for i in range(per):
            own = [pivots[i * TILE + s][s : s + 1] for s in range(TILE)]
            scale[start + i] = lax.rsqrt(jnp.concatenate(own, axis=0))
        rest = start + 2 * per
        if rest < count:
            panel = range(start, start + per)
            u = jnp.concatenate([left[i] * scale[i] for i in panel], axis=0)
            v = jnp.concatenate([right[i] * scale[i] for i in panel], axis=0)
            change = stacked(u, jnp.concatenate([u, v], axis=1), CONTRACT)
            for q in range(rest, count):
                rows = change[TILE * q : TILE * (q + 1)]
                left[q] = left[q] - rows[:, :n]
                right[q] = right[q] - rows[:, n:]
    upper = [jnp.where(lane >= sub + TILE * i, left[i] * scale[i], 0.0) for i in range(count)]
    lower = [right[i] * scale[i] for i in range(count)]
    return jnp.concatenate(upper, axis=0), jnp.concatenate(lower, axis=0)


def pack(gram):
    n = gram.shape[0]
    q = n // 4
    middle = jnp.concatenate([gram[q : 2 * q, q:], gram[3 * q :, 3 * q :]], axis=1)
    low = gram[2 * q : 3 * q, 2 * q :]
    tail = jnp.concatenate([low[: q // 2], low[q // 2 :]], axis=1)
    return jnp.concatenate([gram[:q], middle, tail], axis=0)


def unpack(packed):
    n = packed.shape[1]
    q = n // 4
    middle, tail = packed[q : 2 * q], packed[2 * q :]
    low = jnp.concatenate([tail[:, : 2 * q], tail[:, 2 * q :]], axis=0)
    second = jnp.concatenate([jnp.zeros((q, q), jnp.float32), middle[:, : 3 * q]], axis=1)
    third = jnp.concatenate([jnp.zeros((q, 2 * q), jnp.float32), low], axis=1)
    fourth = jnp.concatenate([jnp.zeros((q, 3 * q), jnp.float32), middle[:, 3 * q :]], axis=1)
    upper = jnp.concatenate([packed[:q], second, third, fourth], axis=0)
    row = lax.broadcasted_iota(jnp.int32, (n, n), 0)
    column = lax.broadcasted_iota(jnp.int32, (n, n), 1)
    return jnp.where(row <= column, upper, jnp.transpose(upper))


def store_halves(core, gram, own_ref, other_ref):
    packed = pack(gram)
    middle = packed.shape[0] // 2
    first, second = packed[:middle], packed[middle:]
    own_ref[...] = jnp.where(core == 0, first, second)
    other_ref[...] = jnp.where(core == 0, second, first)


def load_halves(core, own, other):
    first = jnp.where(core == 0, own, other)
    second = jnp.where(core == 0, other, own)
    return unpack(jnp.concatenate([first, second], axis=0))


def floor_of(gram):
    return 1e-9 * jnp.max(gram)


def without(kernel, place, count):
    def call(*refs):
        kernel(*refs[:place], *refs[place + count :])

    return call


def small_call(kernel, shapes, name, cycles, operands, scalars=(), after=()):
    memory = pl.BlockSpec(memory_space=pltpu.VMEM)
    return pl.pallas_call(
        without(kernel, len(scalars) + len(operands), len(after)),
        in_specs=[pl.BlockSpec(memory_space=pltpu.SMEM)] * len(scalars)
        + [memory] * len(operands)
        + [pl.BlockSpec(memory_space=pl.ANY)] * len(after),
        out_specs=[memory] * len(shapes),
        out_shape=[jax.ShapeDtypeStruct(shape, jnp.float32) for shape in shapes],
        compiler_params=params(),
        cost_estimate=pl.CostEstimate(
            flops=cycles * 10**6, bytes_accessed=4 * shapes[0][-1], transcendentals=0
        ),
        name=name,
    )(*scalars, *operands, *after)


def plain_call(kernel, shape, name, *operands, after=()):
    return small_call(kernel, [shape], name, 100, operands, after=after)[0]


def gram_kernel(core_ref, value_ref, own_ref, other_ref):
    value = value_ref[...]
    store_halves(core_ref[0], gram_of(value), own_ref, other_ref)


def add_kernel(first_ref, second_ref, out_ref):
    out_ref[...] = first_ref[...] + second_ref[...]


def total_kernel(scale, pieces_ref, out_ref):
    value = pieces_ref[0]
    for place in range(1, pieces_ref.shape[0]):
        value += pieces_ref[place]
    out_ref[...] = jnp.broadcast_to((value * scale)[None], out_ref.shape)


def add(first, second, after=()):
    return plain_call(add_kernel, first.shape, "add", first, second, after=after)


def pair_kernel(own_ref, other_ref, out_ref):
    out_ref[...] = jnp.broadcast_to((own_ref[...] + other_ref[...])[None], out_ref.shape)


def total(pieces, count, scale=1.0):
    shape = (count,) + pieces.shape[1:]
    return plain_call(functools.partial(total_kernel, scale), shape, "total", pieces)


def join_kernel(product_ref, sent_ref, own_ref, other_ref, out_ref):
    height = product_ref.shape[1]
    out_ref[:, :height] = product_ref[...] + sent_ref[...]
    gram = own_ref[...] + other_ref[...]
    out_ref[:, height:] = jnp.broadcast_to(gram[None], (out_ref.shape[0],) + gram.shape)


def tail_kernel(start, pieces_ref, out_ref):
    value = pieces_ref[0, start:]
    for place in range(1, pieces_ref.shape[0]):
        value += pieces_ref[place, start:]
    out_ref[...] = value


def middle_kernel(
    core_ref, pieces_ref, pulled_own_ref, pulled_other_ref, inner_ref, before_ref, own_ref, other_ref
):
    gram = load_halves(core_ref[0], pulled_own_ref[...], pulled_other_ref[...])
    before_ref[...], lower = eliminate(gram, floor_of(gram))
    height = inner_ref.shape[0]
    sketch = pieces_ref[0, :height]
    for place in range(1, pieces_ref.shape[0]):
        sketch += pieces_ref[place, :height]
    inner = stacked(sketch, lower, TRANSPOSED)
    inner_ref[...] = inner
    store_halves(core_ref[0], stacked(inner, inner, CONTRACT), own_ref, other_ref)


def last_kernel(
    root_rows, core_ref, own_ref, other_ref, inner_ref, before_ref, basis_ref, factor_ref
):
    gram = load_halves(core_ref[0], own_ref[...], other_ref[...])
    upper, lower = eliminate(gram, floor_of(gram))
    basis_ref[...] = stacked(inner_ref[...], lower, TRANSPOSED) * root_rows
    factor_ref[...] = stacked(upper, before_ref[...], PLAIN) / root_rows


def local(slab, test_matrix):
    rows, columns = slab.shape
    wide = test_matrix.shape[1]
    zs = lax.axis_size("z")
    row_count = lax.axis_size(ROW)
    row_total = rows * row_count
    root_rows = math.sqrt(row_total)
    core = lax.axis_index("core").astype(jnp.int32).reshape(1)
    far = 1 - core
    slab = slab.reshape(zs, 2, -1, columns)
    square = (wide, wide)
    halves = [(5 * wide // 16, wide)] * 2

    sent = swap(multiply(slab, test_matrix, far))
    product = multiply(slab, test_matrix, core)
    made = parts_of(slab, core, 0)
    part = add(product, sent, made[:1])
    own = exchange(total(exchange(part, "z"), zs), "z")

    *made, own = parts_of(slab, core, 1, made, own)
    parts, far_parts = made[:PARTS], made[PARTS:]
    other = swap(own)
    part = pull(other, far_parts[:2], pull(own, parts[:2]))
    pieces = total(exchange(part.reshape(row_count, -1, wide), ROW), row_count, 1.0 / row_total)
    pulled = exchange(pieces, ROW).reshape(-1, wide)

    own, other = small_call(gram_kernel, halves, "gram", 700, [pulled], [core])
    other = swap(other)
    sent = swap(project(pulled, far_parts[2:], zs))
    product = project(pulled, parts[2:], zs)
    height = product.shape[1]
    shape = (zs, height + own.shape[0], wide)
    joined = plain_call(join_kernel, shape, "join", product, sent, own, other)
    pieces = exchange(joined, "z")
    own = plain_call(functools.partial(tail_kernel, height), own.shape, "tail", pieces)

    inner, before, own, other = small_call(
        middle_kernel,
        [(height, wide), square] + halves,
        "middle",
        4300,
        [pieces, own, swap(own)],
        [core],
    )
    copies = plain_call(pair_kernel, (row_count,) + own.shape, "pair", own, swap(other))
    copies = total(exchange(copies, ROW), zs)
    own = total(exchange(copies, "z"), 1)[0]
    basis, factor = small_call(
        functools.partial(last_kernel, root_rows),
        [inner.shape, square],
        "last",
        4600,
        [own, swap(own), inner, before],
        [core],
    )
    return basis, factor


def solution(mesh):
    sizes = dict(mesh.shape)
    chips = mesh.devices.reshape(4, sizes["row"] // 4, sizes["col"] // 2, 2)
    fine = Mesh(chips, ("y", "x", "z", "core"))
    col = ("z", "core")
    in_specs = (P(ROW, col), P(col, None))
    out_specs = (P(ROW + col, None), P())
    return jax.shard_map(local, mesh=fine, in_specs=in_specs, out_specs=out_specs, check_vma=False)
```

```python
import functools
import math

import jax
import jax.numpy as jnp
from jax import lax
from jax.experimental import pallas as pl
from jax.experimental.pallas import tpu as pltpu
from jax.sharding import Mesh
from jax.sharding import PartitionSpec as P

PLAIN = (((1,), (0,)), ((), ()))
CONTRACT = (((0,), (0,)), ((), ()))
TRANSPOSED = (((1,), (1,)), ((), ()))
ROW = ("y", "x")
SWAP = [(0, 1), (1, 0)]
TILE = 8
PANEL = 16
STEP = 2
PARTS = 5
VMEM = 12 * 1024 * 1024


def swap(value):
    return lax.ppermute(value, "core", SWAP)


def exchange(value, axes):
    return lax.all_to_all(value, axes, 0, 0, tiled=False)


def dot(a, b, dims=PLAIN):
    return lax.dot_general(a, b, dims, preferred_element_type=jnp.float32)


def split(value, count):
    parts = []
    for _ in range(count):
        parts.append(value.astype(jnp.bfloat16))
        value = value - parts[-1].astype(jnp.float32)
    return parts


keep = pltpu.with_memory_space_constraint


def stacked(a, b, dims):
    (first,), (second,) = dims[0]
    a1, a2, a3 = split(a, 3)
    b1, b2, b3 = split(b, 3)
    left = jnp.concatenate([a1, a1, a2, a2, a1, a3], axis=first)
    return dot(left, jnp.concatenate([b1, b2, b1, b2, b3, b1], axis=second), dims)


def gram_of(value):
    wide = value.shape[1]
    high, middle, low = split(value, 3)
    pair = jnp.concatenate([high, middle], axis=1)
    four, cross = dot(pair, pair, CONTRACT), dot(high, low, CONTRACT)
    small = four[wide:, wide:] + (cross + jnp.transpose(cross))
    return four[:wide, :wide] + (four[:wide, wide:] + four[wide:, :wide] + small)


def params():
    return pltpu.CompilerParams(vmem_limit_bytes=VMEM)


def rows_of(ref, place, height):
    return ref[place : place + height].reshape(-1, ref.shape[-1])


def multiply_kernel(half_ref, slab_ref, right_ref, out_ref, pair_ref, block_ref, right_buffer, sems):
    half, zs, wide = half_ref[0], block_ref.shape[0], out_ref.shape[-1]
    right_copy = pltpu.make_async_copy(right_ref, right_buffer, sems.at[zs])
    right_copy.start()
    copies = [
        pltpu.make_async_copy(slab_ref.at[place, half], block_ref.at[place], sems.at[place])
        for place in range(zs)
    ]
    for copy in copies:
        copy.start()
    right_copy.wait()
    high, low = split(right_buffer[...], 2)
    pair_ref[:, :wide] = high
    pair_ref[:, wide:] = low
    for place in range(0, zs, STEP):
        for copy in copies[place : place + STEP]:
            copy.wait()
        high, low = split(rows_of(block_ref, place, STEP), 2)
        first = dot(high, pair_ref[...])
        value = first[:, :wide] + (first[:, wide:] + dot(low, pair_ref[:, :wide]))
        out_ref[place : place + STEP] = value.reshape(STEP, -1, wide)


def multiply(slab, right, half):
    zs, _, height, depth = slab.shape
    wide = right.shape[1]
    high_memory = pl.BlockSpec(memory_space=pltpu.HBM)
    return pl.pallas_call(
        multiply_kernel,
        in_specs=[pl.BlockSpec(memory_space=pltpu.SMEM), high_memory, high_memory],
        out_specs=pl.BlockSpec(memory_space=pltpu.VMEM),
        scratch_shapes=[
            pltpu.VMEM((depth, 2 * wide), jnp.bfloat16),
            pltpu.VMEM((zs, height, depth), jnp.float32),
            pltpu.VMEM((depth, wide), jnp.float32),
            pltpu.SemaphoreType.DMA((zs + 1,)),
        ],
        out_shape=jax.ShapeDtypeStruct((zs, height, wide), jnp.float32),
        compiler_params=params(),
        cost_estimate=cost(zs * height, depth, wide, 4),
        name="multiply",
    )(half, keep(slab, pltpu.HBM), keep(right, pltpu.HBM))


def parts_kernel(turn, slab_ref, part_refs, block_ref, sems):
    zs, _, height, _ = block_ref.shape
    copies = [
        [
            pltpu.make_async_copy(
                slab_ref.at[place, half], block_ref.at[place, half], sems.at[place, half]
            )
            for half in range(2)
        ]
        for place in range(zs)
    ]
    for pair in copies:
        for copy in pair:
            copy.start()
    for place in range(zs):
        for half in range(2):
            refs = part_refs[PARTS * (half != turn) :][:PARTS]
            copies[place][half].wait()
            block = block_ref[place, half]
            for part, ref in zip(split(block, 2), refs[:2]):
                ref[place] = part
            for part, ref in zip(split(jnp.transpose(block), 3), refs[2:]):
                ref[:, place * height : (place + 1) * height] = part


def parts_of(slab, core, turn, before=(), passed=None):
    zs, _, height, depth = slab.shape
    high_memory = pl.BlockSpec(memory_space=pltpu.HBM)
    memory = pl.BlockSpec(memory_space=pltpu.VMEM)
    count = 2 * PARTS
    through = [] if passed is None else [passed]
    shapes = [pltpu.VMEM((zs, height, depth), jnp.bfloat16)] * 2
    shapes += [pltpu.VMEM((depth, zs * height), jnp.bfloat16)] * 3
    shapes = shapes * 2
    for value in through:
        shapes += [jax.ShapeDtypeStruct((zs // 2,) + value.shape[1:], value.dtype)] * 2
    place = 2 + len(through)
    aliases = {place + i: i for i in range(len(before))}

    def kernel(*refs):
        outs = refs[place + len(before) :]
        if through:
            outs[count][...] = refs[2][: zs // 2]
            outs[count + 1][...] = refs[2][zs // 2 :]

        @pl.when(refs[0][0] == turn)
        def _():
            parts_kernel(turn, refs[1], outs[:count], *outs[-2:])

    return pl.pallas_call(
        kernel,
        in_specs=[pl.BlockSpec(memory_space=pltpu.SMEM), high_memory]
        + [memory] * (len(through) + len(before)),
        out_specs=[memory] * len(shapes),
        scratch_shapes=[
            pltpu.VMEM((zs, 2, height, depth), jnp.float32),
            pltpu.SemaphoreType.DMA((zs, 2)),
        ],
        out_shape=shapes,
        input_output_aliases=aliases,
        compiler_params=params(),
        cost_estimate=cost(2 * zs * height, depth, 128, 4),
        name="parts",
    )(core, keep(slab, pltpu.HBM), *through, *[keep(part, pltpu.VMEM) for part in before])


def cost(height, depth, wide, times):
    return pl.CostEstimate(
        flops=2 * height * depth * wide * times,
        bytes_accessed=4 * height * depth,
        transcendentals=0,
    )


def project_kernel(right_ref, high_ref, middle_ref, low_ref, out_ref):
    wide, height = right_ref.shape[1], out_ref.shape[1]
    parts = split(jnp.transpose(right_ref[...]), 3)
    stack = jnp.concatenate(parts, axis=0)
    for place in range(0, out_ref.shape[0], STEP):
        run = slice(place * height, (place + STEP) * height)
        first = dot(stack, high_ref[:, run])
        second = dot(stack[: 2 * wide], middle_ref[:, run])
        third = first[2 * wide :] + dot(parts[0], low_ref[:, run])
        small = (first[wide : 2 * wide] + second[:wide]) + (second[wide:] + third)
        value = jnp.transpose(first[:wide] + small)
        out_ref[place : place + STEP] = value.reshape(STEP, height, wide)


def project(right, parts, zs):
    depth, height = parts[0].shape
    wide = right.shape[1]
    memory = pl.BlockSpec(memory_space=pltpu.VMEM)
    return pl.pallas_call(
        project_kernel,
        in_specs=[memory] * 4,
        out_specs=memory,
        out_shape=jax.ShapeDtypeStruct((zs, height // zs, wide), jnp.float32),
        compiler_params=params(),
        cost_estimate=cost(height, depth, wide, 8),
        name="project",
    )(right, *[keep(part, pltpu.VMEM) for part in parts])


def pull_kernel(count, start, more, *refs):
    left_refs, (high_ref, low_ref), out_ref = refs[:count], refs[count : count + 2], refs[-1]
    wide = out_ref.shape[-1]
    left = jnp.concatenate([rows_of(ref, 0, ref.shape[0]) for ref in left_refs], axis=0)
    run = sum(ref.shape[0] for ref in left_refs)
    high, low = split(jnp.transpose(left), 2)
    both = dot(jnp.concatenate([high, low], axis=0), rows_of(high_ref, start, run))
    value = both[:wide] + (both[wide:] + dot(high, rows_of(low_ref, start, run)))
    result = jnp.transpose(value)
    out_ref[...] = result + refs[count + 2][...] if more else result


def pull(lefts, parts, start=0, before=None):
    zs, height, depth = parts[0].shape
    wide = lefts[0].shape[-1]
    memory = pl.BlockSpec(memory_space=pltpu.VMEM)
    more = before is not None
    rows = height * sum(left.shape[0] for left in lefts)
    return pl.pallas_call(
        functools.partial(pull_kernel, len(lefts), start, more),
        in_specs=[memory] * (len(lefts) + 2 + more),
        out_specs=memory,
        out_shape=jax.ShapeDtypeStruct((depth, wide), jnp.float32),
        compiler_params=params(),
        cost_estimate=cost(rows, depth, wide, 4),
        name="pull",
    )(*lefts, *[keep(part, pltpu.VMEM) for part in parts], *([before] if more else []))


def spread(row):
    return jnp.broadcast_to(row, (TILE, row.shape[1]))


def eliminate(gram, floor=None):
    n = gram.shape[0]
    count, per = n // TILE, PANEL // TILE
    sub = lax.broadcasted_iota(jnp.int32, (TILE, n), 0)
    lane = lax.broadcasted_iota(jnp.int32, (TILE, n), 1)
    left = [gram[TILE * i : TILE * (i + 1)] for i in range(count)]
    right = [(lane == sub + TILE * i).astype(jnp.float32) for i in range(count)]
    scale = [None] * count
    for start in range(0, count, per):
        tiles = range(start, min(start + 2 * per, count))
        base = start * TILE
        column = {
            (t, q): jnp.broadcast_to(left[q][:, base + t : base + t + 1], (TILE, n))
            for t in range(PANEL)
            for q in tiles
            if start + t // TILE <= q
        }
        pivots = []
        for s in range(PANEL):
            here, at = start + s // TILE, s % TILE
            pivot = spread(column[s, here][at : at + 1])
            if floor is not None:
                pivot = jnp.maximum(pivot, floor)
            over = 1.0 / pivot
            pivots.append(pivot)
            entry = {
                t: spread(column[s, start + t // TILE][t % TILE : t % TILE + 1])
                if start + t // TILE > here
                else spread(column[t, here][at : at + 1])
                for t in range(s + 1, PANEL)
            }
            left_row, right_row = spread(left[here][at : at + 1]), spread(right[here][at : at + 1])
            for q in tiles:
                if q < here:
                    continue
                ratio = column[s, q] * over
                if q == here:
                    ratio = jnp.where(sub > at, ratio, 0.0)
                for t in range(s + 1, PANEL):
                    if (t, q) in column:
                        column[t, q] = column[t, q] - ratio * entry[t]
                left[q] = left[q] - ratio * left_row
                right[q] = right[q] - ratio * right_row
        for i in range(per):
            own = [pivots[i * TILE + s][s : s + 1] for s in range(TILE)]
            scale[start + i] = lax.rsqrt(jnp.concatenate(own, axis=0))
        rest = start + 2 * per
        if rest < count:
            panel = range(start, start + per)
            u = jnp.concatenate([left[i] * scale[i] for i in panel], axis=0)
            v = jnp.concatenate([right[i] * scale[i] for i in panel], axis=0)
            change = stacked(u, jnp.concatenate([u, v], axis=1), CONTRACT)
            for q in range(rest, count):
                rows = change[TILE * q : TILE * (q + 1)]
                left[q] = left[q] - rows[:, :n]
                right[q] = right[q] - rows[:, n:]
    upper = [jnp.where(lane >= sub + TILE * i, left[i] * scale[i], 0.0) for i in range(count)]
    lower = [right[i] * scale[i] for i in range(count)]
    return jnp.concatenate(upper, axis=0), jnp.concatenate(lower, axis=0)


def pack(gram):
    n = gram.shape[0]
    q = n // 4
    middle = jnp.concatenate([gram[q : 2 * q, q:], gram[3 * q :, 3 * q :]], axis=1)
    low = gram[2 * q : 3 * q, 2 * q :]
    tail = jnp.concatenate([low[: q // 2], low[q // 2 :]], axis=1)
    return jnp.concatenate([gram[:q], middle, tail], axis=0)


def unpack(packed):
    n = packed.shape[1]
    q = n // 4
    middle, tail = packed[q : 2 * q], packed[2 * q :]
    low = jnp.concatenate([tail[:, : 2 * q], tail[:, 2 * q :]], axis=0)
    second = jnp.concatenate([jnp.zeros((q, q), jnp.float32), middle[:, : 3 * q]], axis=1)
    third = jnp.concatenate([jnp.zeros((q, 2 * q), jnp.float32), low], axis=1)
    fourth = jnp.concatenate([jnp.zeros((q, 3 * q), jnp.float32), middle[:, 3 * q :]], axis=1)
    upper = jnp.concatenate([packed[:q], second, third, fourth], axis=0)
    row = lax.broadcasted_iota(jnp.int32, (n, n), 0)
    column = lax.broadcasted_iota(jnp.int32, (n, n), 1)
    return jnp.where(row <= column, upper, jnp.transpose(upper))


def store_halves(core, gram, own_ref, other_ref):
    packed = pack(gram)
    middle = packed.shape[0] // 2
    first, second = packed[:middle], packed[middle:]
    own_ref[...] = jnp.where(core == 0, first, second)
    other_ref[...] = jnp.where(core == 0, second, first)


def load_halves(core, own, other):
    first = jnp.where(core == 0, own, other)
    second = jnp.where(core == 0, other, own)
    return unpack(jnp.concatenate([first, second], axis=0))


def floor_of(gram):
    return 1e-9 * jnp.max(gram)


def without(kernel, place, count):
    def call(*refs):
        kernel(*refs[:place], *refs[place + count :])

    return call


def small_call(kernel, shapes, name, cycles, operands, scalars=(), after=()):
    memory = pl.BlockSpec(memory_space=pltpu.VMEM)
    return pl.pallas_call(
        without(kernel, len(scalars) + len(operands), len(after)),
        in_specs=[pl.BlockSpec(memory_space=pltpu.SMEM)] * len(scalars)
        + [memory] * len(operands)
        + [pl.BlockSpec(memory_space=pl.ANY)] * len(after),
        out_specs=[memory] * len(shapes),
        out_shape=[jax.ShapeDtypeStruct(shape, jnp.float32) for shape in shapes],
        compiler_params=params(),
        cost_estimate=pl.CostEstimate(
            flops=cycles * 10**6, bytes_accessed=4 * shapes[0][-1], transcendentals=0
        ),
        name=name,
    )(*scalars, *operands, *after)


def plain_call(kernel, shape, name, *operands, after=()):
    return small_call(kernel, [shape], name, 100, operands, after=after)[0]


def gram_kernel(core_ref, value_ref, own_ref, other_ref):
    value = value_ref[...]
    store_halves(core_ref[0], gram_of(value), own_ref, other_ref)


def add_kernel(first_ref, second_ref, out_ref):
    out_ref[...] = first_ref[...] + second_ref[...]


def total_kernel(scale, pieces_ref, out_ref):
    value = pieces_ref[0]
    for place in range(1, pieces_ref.shape[0]):
        value += pieces_ref[place]
    out_ref[...] = jnp.broadcast_to((value * scale)[None], out_ref.shape)


def add(first, second, after=()):
    return plain_call(add_kernel, first.shape, "add", first, second, after=after)


def pair_kernel(own_ref, other_ref, out_ref):
    out_ref[...] = jnp.broadcast_to((own_ref[...] + other_ref[...])[None], out_ref.shape)


def total(pieces, count, scale=1.0):
    shape = (count,) + pieces.shape[1:]
    return plain_call(functools.partial(total_kernel, scale), shape, "total", pieces)


def join_kernel(product_ref, sent_ref, own_ref, other_ref, out_ref):
    height = product_ref.shape[1]
    out_ref[:, :height] = product_ref[...] + sent_ref[...]
    gram = own_ref[...] + other_ref[...]
    out_ref[:, height:] = jnp.broadcast_to(gram[None], (out_ref.shape[0],) + gram.shape)


def tail_kernel(start, pieces_ref, out_ref):
    value = pieces_ref[0, start:]
    for place in range(1, pieces_ref.shape[0]):
        value += pieces_ref[place, start:]
    out_ref[...] = value


def middle_kernel(
    core_ref, pieces_ref, pulled_own_ref, pulled_other_ref, inner_ref, before_ref, own_ref, other_ref
):
    gram = load_halves(core_ref[0], pulled_own_ref[...], pulled_other_ref[...])
    before_ref[...], lower = eliminate(gram, floor_of(gram))
    height = inner_ref.shape[0]
    sketch = pieces_ref[0, :height]
    for place in range(1, pieces_ref.shape[0]):
        sketch += pieces_ref[place, :height]
    inner = stacked(sketch, lower, TRANSPOSED)
    inner_ref[...] = inner
    store_halves(core_ref[0], stacked(inner, inner, CONTRACT), own_ref, other_ref)


def last_kernel(
    root_rows, core_ref, own_ref, other_ref, inner_ref, before_ref, basis_ref, factor_ref
):
    gram = load_halves(core_ref[0], own_ref[...], other_ref[...])
    upper, lower = eliminate(gram)
    basis_ref[...] = stacked(inner_ref[...], lower, TRANSPOSED) * root_rows
    factor_ref[...] = stacked(upper, before_ref[...], PLAIN) / root_rows


def local(slab, test_matrix):
    rows, columns = slab.shape
    wide = test_matrix.shape[1]
    zs = lax.axis_size("z")
    row_count = lax.axis_size(ROW)
    row_total = rows * row_count
    root_rows = math.sqrt(row_total)
    core = lax.axis_index("core").astype(jnp.int32).reshape(1)
    far = 1 - core
    slab = slab.reshape(zs, 2, -1, columns)
    square = (wide, wide)
    halves = [(5 * wide // 16, wide)] * 2

    sent = swap(multiply(slab, test_matrix, far))
    product = multiply(slab, test_matrix, core)
    made = parts_of(slab, core, 0)
    part = add(product, sent, made[:1])
    own = exchange(total(exchange(part, "z"), zs), "z")

    *made, first, second = parts_of(slab, core, 1, made, own)
    parts, far_parts = made[:PARTS], made[PARTS:]
    others = [swap(first), swap(second)]
    part = pull([first, second], parts[:2])
    for place, other in enumerate(others):
        part = pull([other], far_parts[:2], place * zs // 2, part)
    pieces = total(exchange(part.reshape(row_count, -1, wide), ROW), row_count, 1.0 / row_total)
    pulled = exchange(pieces, ROW).reshape(-1, wide)

    own, other = small_call(gram_kernel, halves, "gram", 700, [pulled], [core])
    other = swap(other)
    sent = swap(project(pulled, far_parts[2:], zs))
    product = project(pulled, parts[2:], zs)
    height = product.shape[1]
    shape = (zs, height + own.shape[0], wide)
    joined = plain_call(join_kernel, shape, "join", product, sent, own, other)
    pieces = exchange(joined, "z")
    own = plain_call(functools.partial(tail_kernel, height), own.shape, "tail", pieces)

    inner, before, own, other = small_call(
        middle_kernel,
        [(height, wide), square] + halves,
        "middle",
        4300,
        [pieces, own, swap(own)],
        [core],
    )
    copies = plain_call(pair_kernel, (row_count,) + own.shape, "pair", own, swap(other))
    copies = total(exchange(copies, ROW), zs)
    own = total(exchange(copies, "z"), 1)[0]
    basis, factor = small_call(
        functools.partial(last_kernel, root_rows),
        [inner.shape, square],
        "last",
        4600,
        [own, swap(own), inner, before],
        [core],
    )
    return basis, factor


def solution(mesh):
    sizes = dict(mesh.shape)
    chips = mesh.devices.reshape(4, sizes["row"] // 4, sizes["col"] // 2, 2)
    fine = Mesh(chips, ("y", "x", "z", "core"))
    col = ("z", "core")
    in_specs = (P(ROW, col), P(col, None))
    out_specs = (P(ROW + col, None), P())
    return jax.shard_map(local, mesh=fine, in_specs=in_specs, out_specs=out_specs, check_vma=False)
```

```python
import functools
import math

import jax
import jax.numpy as jnp
from jax import lax
from jax.experimental import pallas as pl
from jax.experimental.pallas import tpu as pltpu
from jax.sharding import Mesh
from jax.sharding import PartitionSpec as P

PLAIN = (((1,), (0,)), ((), ()))
CONTRACT = (((0,), (0,)), ((), ()))
TRANSPOSED = (((1,), (1,)), ((), ()))
ROW = ("y", "x")
SWAP = [(0, 1), (1, 0)]
TILE = 8
PANEL = 16
STEP = 4
PARTS = 5
VMEM = 12 * 1024 * 1024


def swap(value):
    return lax.ppermute(value, "core", SWAP)


def exchange(value, axes):
    return lax.all_to_all(value, axes, 0, 0, tiled=False)


def dot(a, b, dims=PLAIN):
    return lax.dot_general(a, b, dims, preferred_element_type=jnp.float32)


def split(value, count):
    parts = []
    for _ in range(count):
        parts.append(value.astype(jnp.bfloat16))
        value = value - parts[-1].astype(jnp.float32)
    return parts


keep = pltpu.with_memory_space_constraint


def stacked(a, b, dims):
    (first,), (second,) = dims[0]
    a1, a2, a3 = split(a, 3)
    b1, b2, b3 = split(b, 3)
    left = jnp.concatenate([a1, a1, a2, a2, a1, a3], axis=first)
    return dot(left, jnp.concatenate([b1, b2, b1, b2, b3, b1], axis=second), dims)


def gram_of(value):
    wide = value.shape[1]
    high, middle, low = split(value, 3)
    pair = jnp.concatenate([high, middle], axis=1)
    four, cross = dot(pair, pair, CONTRACT), dot(high, low, CONTRACT)
    small = four[wide:, wide:] + (cross + jnp.transpose(cross))
    return four[:wide, :wide] + (four[:wide, wide:] + four[wide:, :wide] + small)


def params():
    return pltpu.CompilerParams(vmem_limit_bytes=VMEM)


def rows_of(ref, place, height):
    return ref[place : place + height].reshape(-1, ref.shape[-1])


def multiply_kernel(half_ref, slab_ref, right_ref, out_ref, pair_ref, block_ref, right_buffer, sems):
    half, zs, wide = half_ref[0], block_ref.shape[0], out_ref.shape[-1]
    right_copy = pltpu.make_async_copy(right_ref, right_buffer, sems.at[zs])
    right_copy.start()
    copies = [
        pltpu.make_async_copy(slab_ref.at[place, half], block_ref.at[place], sems.at[place])
        for place in range(zs)
    ]
    for copy in copies:
        copy.start()
    right_copy.wait()
    high, low = split(right_buffer[...], 2)
    pair_ref[:, :wide] = high
    pair_ref[:, wide:] = low
    for place in range(0, zs, STEP):
        for copy in copies[place : place + STEP]:
            copy.wait()
        high, low = split(rows_of(block_ref, place, STEP), 2)
        first = dot(high, pair_ref[...])
        value = first[:, :wide] + (first[:, wide:] + dot(low, pair_ref[:, :wide]))
        out_ref[place : place + STEP] = value.reshape(STEP, -1, wide)


def multiply(slab, right, half):
    zs, _, height, depth = slab.shape
    wide = right.shape[1]
    high_memory = pl.BlockSpec(memory_space=pltpu.HBM)
    return pl.pallas_call(
        multiply_kernel,
        in_specs=[pl.BlockSpec(memory_space=pltpu.SMEM), high_memory, high_memory],
        out_specs=pl.BlockSpec(memory_space=pltpu.VMEM),
        scratch_shapes=[
            pltpu.VMEM((depth, 2 * wide), jnp.bfloat16),
            pltpu.VMEM((zs, height, depth), jnp.float32),
            pltpu.VMEM((depth, wide), jnp.float32),
            pltpu.SemaphoreType.DMA((zs + 1,)),
        ],
        out_shape=jax.ShapeDtypeStruct((zs, height, wide), jnp.float32),
        compiler_params=params(),
        cost_estimate=cost(zs * height, depth, wide, 4),
        name="multiply",
    )(half, keep(slab, pltpu.HBM), keep(right, pltpu.HBM))


def parts_kernel(turn, slab_ref, part_refs, block_ref, sems):
    zs, _, height, _ = block_ref.shape
    copies = [
        [
            pltpu.make_async_copy(
                slab_ref.at[place, half], block_ref.at[place, half], sems.at[place, half]
            )
            for half in range(2)
        ]
        for place in range(zs)
    ]
    for pair in copies:
        for copy in pair:
            copy.start()
    for place in range(zs):
        for half in range(2):
            refs = part_refs[PARTS * (half != turn) :][:PARTS]
            copies[place][half].wait()
            block = block_ref[place, half]
            for part, ref in zip(split(block, 2), refs[:2]):
                ref[place] = part
            for part, ref in zip(split(jnp.transpose(block), 3), refs[2:]):
                ref[:, place * height : (place + 1) * height] = part


def parts_of(slab, core, turn, before=(), passed=None):
    zs, _, height, depth = slab.shape
    high_memory = pl.BlockSpec(memory_space=pltpu.HBM)
    memory = pl.BlockSpec(memory_space=pltpu.VMEM)
    count = 2 * PARTS
    through = [] if passed is None else [passed]
    shapes = [pltpu.VMEM((zs, height, depth), jnp.bfloat16)] * 2
    shapes += [pltpu.VMEM((depth, zs * height), jnp.bfloat16)] * 3
    shapes = shapes * 2
    for value in through:
        shapes += [jax.ShapeDtypeStruct((zs // 2,) + value.shape[1:], value.dtype)] * 2
    place = 2 + len(through)
    aliases = {place + i: i for i in range(len(before))}

    def kernel(*refs):
        outs = refs[place + len(before) :]
        if through:
            outs[count][...] = refs[2][: zs // 2]
            outs[count + 1][...] = refs[2][zs // 2 :]

        @pl.when(refs[0][0] == turn)
        def _():
            parts_kernel(turn, refs[1], outs[:count], *outs[-2:])

    return pl.pallas_call(
        kernel,
        in_specs=[pl.BlockSpec(memory_space=pltpu.SMEM), high_memory]
        + [memory] * (len(through) + len(before)),
        out_specs=[memory] * len(shapes),
        scratch_shapes=[
            pltpu.VMEM((zs, 2, height, depth), jnp.float32),
            pltpu.SemaphoreType.DMA((zs, 2)),
        ],
        out_shape=shapes,
        input_output_aliases=aliases,
        compiler_params=params(),
        cost_estimate=cost(2 * zs * height, depth, 128, 4),
        name="parts",
    )(core, keep(slab, pltpu.HBM), *through, *[keep(part, pltpu.VMEM) for part in before])


def cost(height, depth, wide, times):
    return pl.CostEstimate(
        flops=2 * height * depth * wide * times,
        bytes_accessed=4 * height * depth,
        transcendentals=0,
    )


def project_kernel(right_ref, high_ref, middle_ref, low_ref, out_ref):
    wide, height = right_ref.shape[1], out_ref.shape[1]
    parts = split(jnp.transpose(right_ref[...]), 3)
    stack = jnp.concatenate(parts, axis=0)
    for place in range(0, out_ref.shape[0], STEP):
        run = slice(place * height, (place + STEP) * height)
        first = dot(stack, high_ref[:, run])
        second = dot(stack[: 2 * wide], middle_ref[:, run])
        third = first[2 * wide :] + dot(parts[0], low_ref[:, run])
        small = (first[wide : 2 * wide] + second[:wide]) + (second[wide:] + third)
        value = jnp.transpose(first[:wide] + small)
        out_ref[place : place + STEP] = value.reshape(STEP, height, wide)


def project(right, parts, zs):
    depth, height = parts[0].shape
    wide = right.shape[1]
    memory = pl.BlockSpec(memory_space=pltpu.VMEM)
    return pl.pallas_call(
        project_kernel,
        in_specs=[memory] * 4,
        out_specs=memory,
        out_shape=jax.ShapeDtypeStruct((zs, height // zs, wide), jnp.float32),
        compiler_params=params(),
        cost_estimate=cost(height, depth, wide, 8),
        name="project",
    )(right, *[keep(part, pltpu.VMEM) for part in parts])


def pull_kernel(count, start, more, *refs):
    left_refs, (high_ref, low_ref), out_ref = refs[:count], refs[count : count + 2], refs[-1]
    wide = out_ref.shape[-1]
    left = jnp.concatenate([rows_of(ref, 0, ref.shape[0]) for ref in left_refs], axis=0)
    run = sum(ref.shape[0] for ref in left_refs)
    high, low = split(jnp.transpose(left), 2)
    both = dot(jnp.concatenate([high, low], axis=0), rows_of(high_ref, start, run))
    value = both[:wide] + (both[wide:] + dot(high, rows_of(low_ref, start, run)))
    result = jnp.transpose(value)
    out_ref[...] = result + refs[count + 2][...] if more else result


def pull(lefts, parts, start=0, before=None):
    zs, height, depth = parts[0].shape
    wide = lefts[0].shape[-1]
    memory = pl.BlockSpec(memory_space=pltpu.VMEM)
    more = before is not None
    rows = height * sum(left.shape[0] for left in lefts)
    return pl.pallas_call(
        functools.partial(pull_kernel, len(lefts), start, more),
        in_specs=[memory] * (len(lefts) + 2 + more),
        out_specs=memory,
        out_shape=jax.ShapeDtypeStruct((depth, wide), jnp.float32),
        compiler_params=params(),
        cost_estimate=cost(rows, depth, wide, 4),
        name="pull",
    )(*lefts, *[keep(part, pltpu.VMEM) for part in parts], *([before] if more else []))


def spread(row):
    return jnp.broadcast_to(row, (TILE, row.shape[1]))


def eliminate(gram, floor=None):
    n = gram.shape[0]
    count, per = n // TILE, PANEL // TILE
    sub = lax.broadcasted_iota(jnp.int32, (TILE, n), 0)
    lane = lax.broadcasted_iota(jnp.int32, (TILE, n), 1)
    left = [gram[TILE * i : TILE * (i + 1)] for i in range(count)]
    right = [(lane == sub + TILE * i).astype(jnp.float32) for i in range(count)]
    scale = [None] * count
    for start in range(0, count, per):
        tiles = range(start, min(start + 2 * per, count))
        base = start * TILE
        column = {
            (t, q): jnp.broadcast_to(left[q][:, base + t : base + t + 1], (TILE, n))
            for t in range(PANEL)
            for q in tiles
            if start + t // TILE <= q
        }
        pivots = []
        for s in range(PANEL):
            here, at = start + s // TILE, s % TILE
            pivot = spread(column[s, here][at : at + 1])
            if floor is not None:
                pivot = jnp.maximum(pivot, floor)
            over = 1.0 / pivot
            pivots.append(pivot)
            entry = {
                t: spread(column[s, start + t // TILE][t % TILE : t % TILE + 1])
                if start + t // TILE > here
                else spread(column[t, here][at : at + 1])
                for t in range(s + 1, PANEL)
            }
            left_row, right_row = spread(left[here][at : at + 1]), spread(right[here][at : at + 1])
            for q in tiles:
                if q < here:
                    continue
                ratio = column[s, q] * over
                if q == here:
                    ratio = jnp.where(sub > at, ratio, 0.0)
                for t in range(s + 1, PANEL):
                    if (t, q) in column:
                        column[t, q] = column[t, q] - ratio * entry[t]
                left[q] = left[q] - ratio * left_row
                right[q] = right[q] - ratio * right_row
        for i in range(per):
            own = [pivots[i * TILE + s][s : s + 1] for s in range(TILE)]
            scale[start + i] = lax.rsqrt(jnp.concatenate(own, axis=0))
        rest = start + 2 * per
        if rest < count:
            panel = range(start, start + per)
            u = jnp.concatenate([left[i] * scale[i] for i in panel], axis=0)
            v = jnp.concatenate([right[i] * scale[i] for i in panel], axis=0)
            change = stacked(u, jnp.concatenate([u, v], axis=1), CONTRACT)
            for q in range(rest, count):
                rows = change[TILE * q : TILE * (q + 1)]
                left[q] = left[q] - rows[:, :n]
                right[q] = right[q] - rows[:, n:]
    upper = [jnp.where(lane >= sub + TILE * i, left[i] * scale[i], 0.0) for i in range(count)]
    lower = [right[i] * scale[i] for i in range(count)]
    return jnp.concatenate(upper, axis=0), jnp.concatenate(lower, axis=0)


def pack(gram):
    n = gram.shape[0]
    q = n // 4
    middle = jnp.concatenate([gram[q : 2 * q, q:], gram[3 * q :, 3 * q :]], axis=1)
    low = gram[2 * q : 3 * q, 2 * q :]
    tail = jnp.concatenate([low[: q // 2], low[q // 2 :]], axis=1)
    return jnp.concatenate([gram[:q], middle, tail], axis=0)


def unpack(packed):
    n = packed.shape[1]
    q = n // 4
    middle, tail = packed[q : 2 * q], packed[2 * q :]
    low = jnp.concatenate([tail[:, : 2 * q], tail[:, 2 * q :]], axis=0)
    second = jnp.concatenate([jnp.zeros((q, q), jnp.float32), middle[:, : 3 * q]], axis=1)
    third = jnp.concatenate([jnp.zeros((q, 2 * q), jnp.float32), low], axis=1)
    fourth = jnp.concatenate([jnp.zeros((q, 3 * q), jnp.float32), middle[:, 3 * q :]], axis=1)
    upper = jnp.concatenate([packed[:q], second, third, fourth], axis=0)
    row = lax.broadcasted_iota(jnp.int32, (n, n), 0)
    column = lax.broadcasted_iota(jnp.int32, (n, n), 1)
    return jnp.where(row <= column, upper, jnp.transpose(upper))


def store_halves(core, gram, own_ref, other_ref):
    packed = pack(gram)
    middle = packed.shape[0] // 2
    first, second = packed[:middle], packed[middle:]
    own_ref[...] = jnp.where(core == 0, first, second)
    other_ref[...] = jnp.where(core == 0, second, first)


def load_halves(core, own, other):
    first = jnp.where(core == 0, own, other)
    second = jnp.where(core == 0, other, own)
    return unpack(jnp.concatenate([first, second], axis=0))


def floor_of(gram):
    return 1e-9 * jnp.max(gram)


def without(kernel, place, count):
    def call(*refs):
        kernel(*refs[:place], *refs[place + count :])

    return call


def small_call(kernel, shapes, name, cycles, operands, scalars=(), after=()):
    memory = pl.BlockSpec(memory_space=pltpu.VMEM)
    return pl.pallas_call(
        without(kernel, len(scalars) + len(operands), len(after)),
        in_specs=[pl.BlockSpec(memory_space=pltpu.SMEM)] * len(scalars)
        + [memory] * len(operands)
        + [pl.BlockSpec(memory_space=pl.ANY)] * len(after),
        out_specs=[memory] * len(shapes),
        out_shape=[jax.ShapeDtypeStruct(shape, jnp.float32) for shape in shapes],
        compiler_params=params(),
        cost_estimate=pl.CostEstimate(
            flops=cycles * 10**6, bytes_accessed=4 * shapes[0][-1], transcendentals=0
        ),
        name=name,
    )(*scalars, *operands, *after)


def plain_call(kernel, shape, name, *operands, after=()):
    return small_call(kernel, [shape], name, 100, operands, after=after)[0]


def gram_kernel(core_ref, value_ref, own_ref, other_ref):
    value = value_ref[...]
    store_halves(core_ref[0], gram_of(value), own_ref, other_ref)


def add_kernel(first_ref, second_ref, out_ref):
    out_ref[...] = first_ref[...] + second_ref[...]


def total_kernel(scale, pieces_ref, out_ref):
    value = pieces_ref[0]
    for place in range(1, pieces_ref.shape[0]):
        value += pieces_ref[place]
    out_ref[...] = jnp.broadcast_to((value * scale)[None], out_ref.shape)


def add(first, second, after=()):
    return plain_call(add_kernel, first.shape, "add", first, second, after=after)


def pair_kernel(own_ref, other_ref, out_ref):
    out_ref[...] = jnp.broadcast_to((own_ref[...] + other_ref[...])[None], out_ref.shape)


def total(pieces, count, scale=1.0):
    shape = (count,) + pieces.shape[1:]
    return plain_call(functools.partial(total_kernel, scale), shape, "total", pieces)


def join_kernel(product_ref, sent_ref, own_ref, other_ref, out_ref):
    height = product_ref.shape[1]
    out_ref[:, :height] = product_ref[...] + sent_ref[...]
    gram = own_ref[...] + other_ref[...]
    out_ref[:, height:] = jnp.broadcast_to(gram[None], (out_ref.shape[0],) + gram.shape)


def tail_kernel(start, pieces_ref, out_ref):
    value = pieces_ref[0, start:]
    for place in range(1, pieces_ref.shape[0]):
        value += pieces_ref[place, start:]
    out_ref[...] = value


def middle_kernel(
    core_ref, pieces_ref, pulled_own_ref, pulled_other_ref, inner_ref, before_ref, own_ref, other_ref
):
    gram = load_halves(core_ref[0], pulled_own_ref[...], pulled_other_ref[...])
    before_ref[...], lower = eliminate(gram, floor_of(gram))
    height = inner_ref.shape[0]
    sketch = pieces_ref[0, :height]
    for place in range(1, pieces_ref.shape[0]):
        sketch += pieces_ref[place, :height]
    inner = stacked(sketch, lower, TRANSPOSED)
    inner_ref[...] = inner
    store_halves(core_ref[0], stacked(inner, inner, CONTRACT), own_ref, other_ref)


def last_kernel(
    root_rows, core_ref, own_ref, other_ref, inner_ref, before_ref, basis_ref, factor_ref
):
    gram = load_halves(core_ref[0], own_ref[...], other_ref[...])
    upper, lower = eliminate(gram)
    basis_ref[...] = stacked(inner_ref[...], lower, TRANSPOSED) * root_rows
    factor_ref[...] = stacked(upper, before_ref[...], PLAIN) / root_rows


def local(slab, test_matrix):
    rows, columns = slab.shape
    wide = test_matrix.shape[1]
    zs = lax.axis_size("z")
    row_count = lax.axis_size(ROW)
    row_total = rows * row_count
    root_rows = math.sqrt(row_total)
    core = lax.axis_index("core").astype(jnp.int32).reshape(1)
    far = 1 - core
    slab = slab.reshape(zs, 2, -1, columns)
    square = (wide, wide)
    halves = [(5 * wide // 16, wide)] * 2

    sent = swap(multiply(slab, test_matrix, far))
    product = multiply(slab, test_matrix, core)
    made = parts_of(slab, core, 0)
    part = add(product, sent, made[:1])
    own = exchange(total(exchange(part, "z"), zs), "z")

    *made, first, second = parts_of(slab, core, 1, made, own)
    parts, far_parts = made[:PARTS], made[PARTS:]
    others = [swap(first), swap(second)]
    part = pull([first, second], parts[:2])
    for place, other in enumerate(others):
        part = pull([other], far_parts[:2], place * zs // 2, part)
    pieces = total(exchange(part.reshape(row_count, -1, wide), ROW), row_count, 1.0 / row_total)
    pulled = exchange(pieces, ROW).reshape(-1, wide)

    own, other = small_call(gram_kernel, halves, "gram", 700, [pulled], [core])
    other = swap(other)
    sent = swap(project(pulled, far_parts[2:], zs))
    product = project(pulled, parts[2:], zs)
    height = product.shape[1]
    shape = (zs, height + own.shape[0], wide)
    joined = plain_call(join_kernel, shape, "join", product, sent, own, other)
    pieces = exchange(joined, "z")
    own = plain_call(functools.partial(tail_kernel, height), own.shape, "tail", pieces)

    inner, before, own, other = small_call(
        middle_kernel,
        [(height, wide), square] + halves,
        "middle",
        4300,
        [pieces, own, swap(own)],
        [core],
    )
    copies = plain_call(pair_kernel, (row_count,) + own.shape, "pair", own, swap(other))
    copies = total(exchange(copies, ROW), zs)
    own = total(exchange(copies, "z"), 1)[0]
    basis, factor = small_call(
        functools.partial(last_kernel, root_rows),
        [inner.shape, square],
        "last",
        4600,
        [own, swap(own), inner, before],
        [core],
    )
    return basis, factor


def solution(mesh):
    sizes = dict(mesh.shape)
    chips = mesh.devices.reshape(4, sizes["row"] // 4, sizes["col"] // 2, 2)
    fine = Mesh(chips, ("y", "x", "z", "core"))
    col = ("z", "core")
    in_specs = (P(ROW, col), P(col, None))
    out_specs = (P(ROW + col, None), P())
    return jax.shard_map(local, mesh=fine, in_specs=in_specs, out_specs=out_specs, check_vma=False)
```

```python
import functools
import math

import jax
import jax.numpy as jnp
from jax import lax
from jax.experimental import pallas as pl
from jax.experimental.pallas import tpu as pltpu
from jax.sharding import Mesh
from jax.sharding import PartitionSpec as P

PLAIN = (((1,), (0,)), ((), ()))
CONTRACT = (((0,), (0,)), ((), ()))
TRANSPOSED = (((1,), (1,)), ((), ()))
ROW = ("y", "x")
SWAP = [(0, 1), (1, 0)]
TILE = 8
PANEL = 16
STEP = 2
PULL = 8
PARTS = 5
VMEM = 12 * 1024 * 1024


def swap(value):
    return lax.ppermute(value, "core", SWAP)


def exchange(value, axes):
    return lax.all_to_all(value, axes, 0, 0, tiled=False)


def dot(a, b, dims=PLAIN):
    return lax.dot_general(a, b, dims, preferred_element_type=jnp.float32)


def split(value, count):
    parts = []
    for _ in range(count):
        parts.append(value.astype(jnp.bfloat16))
        value = value - parts[-1].astype(jnp.float32)
    return parts


keep = pltpu.with_memory_space_constraint


def stacked(a, b, dims):
    (first,), (second,) = dims[0]
    a1, a2, a3 = split(a, 3)
    b1, b2, b3 = split(b, 3)
    left = jnp.concatenate([a1, a1, a2, a2, a1, a3], axis=first)
    return dot(left, jnp.concatenate([b1, b2, b1, b2, b3, b1], axis=second), dims)


def gram_of(value):
    wide = value.shape[1]
    high, middle, low = split(value, 3)
    pair = jnp.concatenate([high, middle], axis=1)
    four, cross = dot(pair, pair, CONTRACT), dot(high, low, CONTRACT)
    small = four[wide:, wide:] + (cross + jnp.transpose(cross))
    return four[:wide, :wide] + (four[:wide, wide:] + four[wide:, :wide] + small)


def params():
    return pltpu.CompilerParams(vmem_limit_bytes=VMEM)


def rows_of(ref, place, height):
    return ref[place : place + height].reshape(-1, ref.shape[-1])


def multiply_kernel(half_ref, slab_ref, right_ref, out_ref, pair_ref, block_ref, right_buffer, sems):
    half, zs, wide = half_ref[0], block_ref.shape[0], out_ref.shape[-1]
    right_copy = pltpu.make_async_copy(right_ref, right_buffer, sems.at[zs])
    right_copy.start()
    copies = [
        pltpu.make_async_copy(slab_ref.at[place, half], block_ref.at[place], sems.at[place])
        for place in range(zs)
    ]
    for copy in copies:
        copy.start()
    right_copy.wait()
    high, low = split(right_buffer[...], 2)
    pair_ref[:, :wide] = high
    pair_ref[:, wide:] = low
    for place in range(0, zs, STEP):
        for copy in copies[place : place + STEP]:
            copy.wait()
        high, low = split(rows_of(block_ref, place, STEP), 2)
        first = dot(high, pair_ref[...])
        value = first[:, :wide] + (first[:, wide:] + dot(low, pair_ref[:, :wide]))
        out_ref[place : place + STEP] = value.reshape(STEP, -1, wide)


def multiply(slab, right, half):
    zs, _, height, depth = slab.shape
    wide = right.shape[1]
    high_memory = pl.BlockSpec(memory_space=pltpu.HBM)
    return pl.pallas_call(
        multiply_kernel,
        in_specs=[pl.BlockSpec(memory_space=pltpu.SMEM), high_memory, high_memory],
        out_specs=pl.BlockSpec(memory_space=pltpu.VMEM),
        scratch_shapes=[
            pltpu.VMEM((depth, 2 * wide), jnp.bfloat16),
            pltpu.VMEM((zs, height, depth), jnp.float32),
            pltpu.VMEM((depth, wide), jnp.float32),
            pltpu.SemaphoreType.DMA((zs + 1,)),
        ],
        out_shape=jax.ShapeDtypeStruct((zs, height, wide), jnp.float32),
        compiler_params=params(),
        cost_estimate=cost(zs * height, depth, wide, 4),
        name="multiply",
    )(half, keep(slab, pltpu.HBM), keep(right, pltpu.HBM))


def parts_kernel(turn, slab_ref, part_refs, block_ref, sems):
    zs, _, height, _ = block_ref.shape
    copies = [
        [
            pltpu.make_async_copy(
                slab_ref.at[place, half], block_ref.at[place, half], sems.at[place, half]
            )
            for half in range(2)
        ]
        for place in range(zs)
    ]
    for pair in copies:
        for copy in pair:
            copy.start()
    for place in range(zs):
        for half in range(2):
            refs = part_refs[PARTS * (half != turn) :][:PARTS]
            copies[place][half].wait()
            block = block_ref[place, half]
            for part, ref in zip(split(block, 2), refs[:2]):
                ref[place] = part
            for part, ref in zip(split(jnp.transpose(block), 3), refs[2:]):
                ref[:, place * height : (place + 1) * height] = part


def parts_of(slab, core, turn, before=(), passed=None):
    zs, _, height, depth = slab.shape
    high_memory = pl.BlockSpec(memory_space=pltpu.HBM)
    memory = pl.BlockSpec(memory_space=pltpu.VMEM)
    count = 2 * PARTS
    through = [] if passed is None else [passed]
    shapes = [pltpu.VMEM((zs, height, depth), jnp.bfloat16)] * 2
    shapes += [pltpu.VMEM((depth, zs * height), jnp.bfloat16)] * 3
    shapes = shapes * 2
    shapes += [jax.ShapeDtypeStruct(value.shape, value.dtype) for value in through]
    place = 2 + len(through)
    aliases = {2: count} if through else {}
    aliases |= {place + i: i for i in range(len(before))}

    def kernel(*refs):
        outs = refs[place + len(before) :]

        @pl.when(refs[0][0] == turn)
        def _():
            parts_kernel(turn, refs[1], outs[:count], *outs[-2:])

    return pl.pallas_call(
        kernel,
        in_specs=[pl.BlockSpec(memory_space=pltpu.SMEM), high_memory]
        + [memory] * (len(through) + len(before)),
        out_specs=[memory] * (count + len(through)),
        scratch_shapes=[
            pltpu.VMEM((zs, 2, height, depth), jnp.float32),
            pltpu.SemaphoreType.DMA((zs, 2)),
        ],
        out_shape=shapes,
        input_output_aliases=aliases,
        compiler_params=params(),
        cost_estimate=cost(2 * zs * height, depth, 128, 4),
        name="parts",
    )(core, keep(slab, pltpu.HBM), *through, *[keep(part, pltpu.VMEM) for part in before])


def cost(height, depth, wide, times):
    return pl.CostEstimate(
        flops=2 * height * depth * wide * times,
        bytes_accessed=4 * height * depth,
        transcendentals=0,
    )


def project_kernel(right_ref, high_ref, middle_ref, low_ref, out_ref):
    wide, height = right_ref.shape[1], out_ref.shape[1]
    parts = split(jnp.transpose(right_ref[...]), 3)
    stack = jnp.concatenate(parts, axis=0)
    for place in range(0, out_ref.shape[0], STEP):
        run = slice(place * height, (place + STEP) * height)
        first = dot(stack, high_ref[:, run])
        second = dot(stack[: 2 * wide], middle_ref[:, run])
        third = first[2 * wide :] + dot(parts[0], low_ref[:, run])
        small = (first[wide : 2 * wide] + second[:wide]) + (second[wide:] + third)
        value = jnp.transpose(first[:wide] + small)
        out_ref[place : place + STEP] = value.reshape(STEP, height, wide)


def project(right, parts, zs):
    depth, height = parts[0].shape
    wide = right.shape[1]
    memory = pl.BlockSpec(memory_space=pltpu.VMEM)
    return pl.pallas_call(
        project_kernel,
        in_specs=[memory] * 4,
        out_specs=memory,
        out_shape=jax.ShapeDtypeStruct((zs, height // zs, wide), jnp.float32),
        compiler_params=params(),
        cost_estimate=cost(height, depth, wide, 8),
        name="project",
    )(right, *[keep(part, pltpu.VMEM) for part in parts])


def pull_kernel(more, left_ref, high_ref, low_ref, *refs):
    out_ref = refs[-1]
    zs, wide = left_ref.shape[0], left_ref.shape[-1]
    total = None
    for place in range(0, zs, PULL):
        left = jnp.transpose(rows_of(left_ref, place, PULL))
        high, low = split(left, 2)
        block = rows_of(high_ref, place, PULL)
        both = dot(jnp.concatenate([high, low], axis=0), block)
        value = both[:wide] + (both[wide:] + dot(high, rows_of(low_ref, place, PULL)))
        total = value if total is None else total + value
    result = jnp.transpose(total)
    out_ref[...] = result + refs[0][...] if more else result


def pull(left, parts, before=None):
    zs, height, depth = parts[0].shape
    wide = left.shape[-1]
    memory = pl.BlockSpec(memory_space=pltpu.VMEM)
    more = before is not None
    return pl.pallas_call(
        functools.partial(pull_kernel, more),
        in_specs=[memory] * (3 + more),
        out_specs=memory,
        out_shape=jax.ShapeDtypeStruct((depth, wide), jnp.float32),
        compiler_params=params(),
        cost_estimate=cost(zs * height, depth, wide, 4),
        name="pull",
    )(left, *[keep(part, pltpu.VMEM) for part in parts], *([before] if more else []))


def spread(row):
    return jnp.broadcast_to(row, (TILE, row.shape[1]))


def eliminate(gram, floor=None):
    n = gram.shape[0]
    count, per = n // TILE, PANEL // TILE
    sub = lax.broadcasted_iota(jnp.int32, (TILE, n), 0)
    lane = lax.broadcasted_iota(jnp.int32, (TILE, n), 1)
    left = [gram[TILE * i : TILE * (i + 1)] for i in range(count)]
    right = [(lane == sub + TILE * i).astype(jnp.float32) for i in range(count)]
    scale = [None] * count
    for start in range(0, count, per):
        tiles = range(start, min(start + 2 * per, count))
        base = start * TILE
        column = {
            (t, q): jnp.broadcast_to(left[q][:, base + t : base + t + 1], (TILE, n))
            for t in range(PANEL)
            for q in tiles
            if start + t // TILE <= q
        }
        pivots = []
        for s in range(PANEL):
            here, at = start + s // TILE, s % TILE
            pivot = spread(column[s, here][at : at + 1])
            if floor is not None:
                pivot = jnp.maximum(pivot, floor)
            over = 1.0 / pivot
            pivots.append(pivot)
            entry = {
                t: spread(column[s, start + t // TILE][t % TILE : t % TILE + 1])
                if start + t // TILE > here
                else spread(column[t, here][at : at + 1])
                for t in range(s + 1, PANEL)
            }
            left_row, right_row = spread(left[here][at : at + 1]), spread(right[here][at : at + 1])
            for q in tiles:
                if q < here:
                    continue
                ratio = column[s, q] * over
                if q == here:
                    ratio = jnp.where(sub > at, ratio, 0.0)
                for t in range(s + 1, PANEL):
                    if (t, q) in column:
                        column[t, q] = column[t, q] - ratio * entry[t]
                left[q] = left[q] - ratio * left_row
                right[q] = right[q] - ratio * right_row
        for i in range(per):
            own = [pivots[i * TILE + s][s : s + 1] for s in range(TILE)]
            scale[start + i] = lax.rsqrt(jnp.concatenate(own, axis=0))
        rest = start + 2 * per
        if rest < count:
            panel = range(start, start + per)
            u = jnp.concatenate([left[i] * scale[i] for i in panel], axis=0)
            v = jnp.concatenate([right[i] * scale[i] for i in panel], axis=0)
            change = stacked(u, jnp.concatenate([u, v], axis=1), CONTRACT)
            for q in range(rest, count):
                rows = change[TILE * q : TILE * (q + 1)]
                left[q] = left[q] - rows[:, :n]
                right[q] = right[q] - rows[:, n:]
    upper = [jnp.where(lane >= sub + TILE * i, left[i] * scale[i], 0.0) for i in range(count)]
    lower = [right[i] * scale[i] for i in range(count)]
    return jnp.concatenate(upper, axis=0), jnp.concatenate(lower, axis=0)


def pack(gram):
    n = gram.shape[0]
    q = n // 4
    middle = jnp.concatenate([gram[q : 2 * q, q:], gram[3 * q :, 3 * q :]], axis=1)
    low = gram[2 * q : 3 * q, 2 * q :]
    tail = jnp.concatenate([low[: q // 2], low[q // 2 :]], axis=1)
    return jnp.concatenate([gram[:q], middle, tail], axis=0)


def unpack(packed):
    n = packed.shape[1]
    q = n // 4
    middle, tail = packed[q : 2 * q], packed[2 * q :]
    low = jnp.concatenate([tail[:, : 2 * q], tail[:, 2 * q :]], axis=0)
    second = jnp.concatenate([jnp.zeros((q, q), jnp.float32), middle[:, : 3 * q]], axis=1)
    third = jnp.concatenate([jnp.zeros((q, 2 * q), jnp.float32), low], axis=1)
    fourth = jnp.concatenate([jnp.zeros((q, 3 * q), jnp.float32), middle[:, 3 * q :]], axis=1)
    upper = jnp.concatenate([packed[:q], second, third, fourth], axis=0)
    row = lax.broadcasted_iota(jnp.int32, (n, n), 0)
    column = lax.broadcasted_iota(jnp.int32, (n, n), 1)
    return jnp.where(row <= column, upper, jnp.transpose(upper))


def store_halves(core, gram, own_ref, other_ref):
    packed = pack(gram)
    middle = packed.shape[0] // 2
    first, second = packed[:middle], packed[middle:]
    own_ref[...] = jnp.where(core == 0, first, second)
    other_ref[...] = jnp.where(core == 0, second, first)


def load_halves(core, own, other):
    first = jnp.where(core == 0, own, other)
    second = jnp.where(core == 0, other, own)
    return unpack(jnp.concatenate([first, second], axis=0))


def floor_of(gram):
    return 1e-9 * jnp.max(gram)


def without(kernel, place, count):
    def call(*refs):
        kernel(*refs[:place], *refs[place + count :])

    return call


def small_call(kernel, shapes, name, cycles, operands, scalars=(), after=()):
    memory = pl.BlockSpec(memory_space=pltpu.VMEM)
    return pl.pallas_call(
        without(kernel, len(scalars) + len(operands), len(after)),
        in_specs=[pl.BlockSpec(memory_space=pltpu.SMEM)] * len(scalars)
        + [memory] * len(operands)
        + [pl.BlockSpec(memory_space=pl.ANY)] * len(after),
        out_specs=[memory] * len(shapes),
        out_shape=[jax.ShapeDtypeStruct(shape, jnp.float32) for shape in shapes],
        compiler_params=params(),
        cost_estimate=pl.CostEstimate(
            flops=cycles * 10**6, bytes_accessed=4 * shapes[0][-1], transcendentals=0
        ),
        name=name,
    )(*scalars, *operands, *after)


def plain_call(kernel, shape, name, *operands, after=()):
    return small_call(kernel, [shape], name, 100, operands, after=after)[0]


def gram_kernel(core_ref, value_ref, own_ref, other_ref):
    value = value_ref[...]
    store_halves(core_ref[0], gram_of(value), own_ref, other_ref)


def add_kernel(first_ref, second_ref, out_ref):
    out_ref[...] = first_ref[...] + second_ref[...]


def total_kernel(scale, pieces_ref, out_ref):
    value = pieces_ref[0]
    for place in range(1, pieces_ref.shape[0]):
        value += pieces_ref[place]
    out_ref[...] = jnp.broadcast_to((value * scale)[None], out_ref.shape)


def add(first, second, after=()):
    return plain_call(add_kernel, first.shape, "add", first, second, after=after)


def pair_kernel(own_ref, other_ref, out_ref):
    out_ref[...] = jnp.broadcast_to((own_ref[...] + other_ref[...])[None], out_ref.shape)


def total(pieces, count, scale=1.0):
    shape = (count,) + pieces.shape[1:]
    return plain_call(functools.partial(total_kernel, scale), shape, "total", pieces)


def join_kernel(product_ref, sent_ref, own_ref, other_ref, out_ref):
    height = product_ref.shape[1]
    out_ref[:, :height] = product_ref[...] + sent_ref[...]
    gram = own_ref[...] + other_ref[...]
    out_ref[:, height:] = jnp.broadcast_to(gram[None], (out_ref.shape[0],) + gram.shape)


def tail_kernel(start, pieces_ref, out_ref):
    value = pieces_ref[0, start:]
    for place in range(1, pieces_ref.shape[0]):
        value += pieces_ref[place, start:]
    out_ref[...] = value


def middle_kernel(
    core_ref, pieces_ref, pulled_own_ref, pulled_other_ref, inner_ref, before_ref, own_ref, other_ref
):
    gram = load_halves(core_ref[0], pulled_own_ref[...], pulled_other_ref[...])
    before_ref[...], lower = eliminate(gram, floor_of(gram))
    height = inner_ref.shape[0]
    sketch = pieces_ref[0, :height]
    for place in range(1, pieces_ref.shape[0]):
        sketch += pieces_ref[place, :height]
    inner = stacked(sketch, lower, TRANSPOSED)
    inner_ref[...] = inner
    store_halves(core_ref[0], stacked(inner, inner, CONTRACT), own_ref, other_ref)


def last_kernel(
    root_rows, core_ref, own_ref, other_ref, inner_ref, before_ref, basis_ref, factor_ref
):
    gram = load_halves(core_ref[0], own_ref[...], other_ref[...])
    upper, lower = eliminate(gram)
    basis_ref[...] = stacked(inner_ref[...], lower, TRANSPOSED) * root_rows
    factor_ref[...] = stacked(upper, before_ref[...], PLAIN) / root_rows


def local(slab, test_matrix):
    rows, columns = slab.shape
    wide = test_matrix.shape[1]
    zs = lax.axis_size("z")
    row_count = lax.axis_size(ROW)
    row_total = rows * row_count
    root_rows = math.sqrt(row_total)
    core = lax.axis_index("core").astype(jnp.int32).reshape(1)
    far = 1 - core
    slab = slab.reshape(zs, 2, -1, columns)
    square = (wide, wide)
    halves = [(5 * wide // 16, wide)] * 2

    sent = swap(multiply(slab, test_matrix, far))
    product = multiply(slab, test_matrix, core)
    made = parts_of(slab, core, 0)
    part = add(product, sent, made[:1])
    own = exchange(total(exchange(part, "z"), zs), "z")

    *made, own = parts_of(slab, core, 1, made, own)
    parts, far_parts = made[:PARTS], made[PARTS:]
    other = swap(own)
    part = pull(other, far_parts[:2], pull(own, parts[:2]))
    pieces = total(exchange(part.reshape(row_count, -1, wide), ROW), row_count, 1.0 / row_total)
    pulled = exchange(pieces, ROW).reshape(-1, wide)

    own, other = small_call(gram_kernel, halves, "gram", 700, [pulled], [core])
    other = swap(other)
    sent = swap(project(pulled, far_parts[2:], zs))
    product = project(pulled, parts[2:], zs)
    height = product.shape[1]
    shape = (zs, height + own.shape[0], wide)
    joined = plain_call(join_kernel, shape, "join", product, sent, own, other)
    pieces = exchange(joined, "z")
    own = plain_call(functools.partial(tail_kernel, height), own.shape, "tail", pieces)

    inner, before, own, other = small_call(
        middle_kernel,
        [(height, wide), square] + halves,
        "middle",
        4300,
        [pieces, own, swap(own)],
        [core],
    )
    copies = plain_call(pair_kernel, (row_count,) + own.shape, "pair", own, swap(other))
    copies = total(exchange(copies, ROW), zs)
    own = total(exchange(copies, "z"), 1)[0]
    basis, factor = small_call(
        functools.partial(last_kernel, root_rows),
        [inner.shape, square],
        "last",
        4600,
        [own, swap(own), inner, before],
        [core],
    )
    return basis, factor


def solution(mesh):
    sizes = dict(mesh.shape)
    chips = mesh.devices.reshape(4, sizes["row"] // 4, sizes["col"] // 2, 2)
    fine = Mesh(chips, ("y", "x", "z", "core"))
    col = ("z", "core")
    in_specs = (P(ROW, col), P(col, None))
    out_specs = (P(ROW + col, None), P())
    return jax.shard_map(local, mesh=fine, in_specs=in_specs, out_specs=out_specs, check_vma=False)
```
